32 devices in a mesh: groups: 2 (over x), curve: 16 (over z, y, core).
Axes of the slice: x: 2, y: 2, z: 4, core: 2. Of those that a mesh axis runs over, the one named last changes fastest.
Arguments:
- latlon_cotangent: bfloat16 [2, 69, 24576], P('groups', None, 'curve'), parts along dimension 0, may hold values from -6 to 6
- healpix_cotangent: bfloat16 [2, 69, 24576], P('groups', None, 'curve'), parts along dimension 0, may hold values from -6 to 6
- outward_weights: bfloat16 [2304, 128, 128], P('curve'), may hold values from -0.15625 to 0.15625
- outward_source: int32 [2304], P('curve'), may hold values from 0 to 11
- outward_target: int32 [2304], P('curve'), may hold values from 0 to 11
- outward_counts: int32 [16, 16], P('curve'), may hold values from 1 to 18, 144 in all within a row
- inward_weights: bfloat16 [2304, 128, 128], P('curve'), may hold values from -0.15625 to 0.15625
- inward_source: int32 [2304], P('curve'), may hold values from 0 to 11
- inward_target: int32 [2304], P('curve'), may hold values from 0 to 11
- inward_counts: int32 [16, 16], P('curve'), may hold values from 1 to 18, 144 in all within a row
Outputs:
- healpix_gradient: bfloat16 [2, 69, 24576], P('groups', None, 'curve'), parts along dimension 0
- latlon_gradient: bfloat16 [2, 69, 24576], P('groups', None, 'curve'), parts along dimension 0
The draws below stay inside these ranges and needn't reach their ends.
There are 2 independent parts, one for each index of `groups`. The reference program is written for one: setup_inputs(seed, part) draws one part's arguments, and reference() takes and returns one part's arrays. A program takes and returns all parts, laid end to end along the dimension named above; an argument that names none is the same for every part. Nothing has to cross between parts.
Inputs may be any that keep to these rules, and one draw needn't show every extreme that they name: `outward_counts`: each row sums to 144; its largest entry is exactly 18. `inward_counts`: each row sums to 144; its largest entry is exactly 18.
All inputs are finite; a program needn't handle non-finite values.
Results may differ from the reference program's by a relative error of at most 0.005.
Values may be sent and summed in bfloat16 or wider, within the bound.
No kernel may reach another device: no remote copies, remote signals or barrier semaphores. Data moves between devices by JAX's collectives and lax.ppermute only.
A program may use at most 128 MiB of HBM per device.

```python
import math
import jax
import jax.numpy as jnp
import numpy as np
from jax import lax

C = 69
T_SIZE = 128
TIMES = 1
TL_DEV = 12
TH_DEV = 12
B_DEV = 144
SLOT = 18
LL_CELLS = 24576
HP_CELLS = 24576
BLOCKS = 2304
N_CURVE = 16


def set_ends(values, rng, low, largest):
    dims = values.shape
    spot = [jax.random.randint(jax.random.fold_in(rng, axis), (), 0, dims[axis]) for axis in range(len(dims))]
    values = values.at[tuple(spot)].set(low)
    longest = dims.index(max(dims))
    spot[longest] = (spot[longest] + 1) % dims[longest]
    return values.at[tuple(spot)].set(largest)


def level_of(stream_key, extent, shards, least, top_value):
    def one(axis_at, blocks):
        steps = jax.random.uniform(jax.random.fold_in(jax.random.fold_in(stream_key, 6), axis_at), (blocks,), jnp.float32, least / len(shards), top_value / len(shards))
        return jnp.repeat(jnp.exp(steps), extent[axis_at] // blocks).reshape((-1,) + (1,) * (len(extent) - axis_at - 1))

    loudness = one(*shards[0])
    for cut in shards[1:]:
        loudness = loudness * one(*cut)
    return loudness


def profile(amount, total, limit, slope):
    portions = [(1 << 20) // math.isqrt(standing ** slope) + 1 for standing in range(2, amount + 1)]
    rest, given = total - limit - (amount - 1), [1] * (amount - 1)
    while rest > 0:
        candidates = [i for i in range(amount - 1) if given[i] < limit]
        mass, budget = sum([portions[i] for i in candidates]), rest
        for i in candidates:
            more = min(limit - given[i], max(1, budget * portions[i] // mass), rest)
            given[i] = given[i] + more
            rest = rest - more
    return np.array([limit] + given)


def uneven(stream_key, number_of, total, reach, lean):
    if number_of == 2:
        one = jax.random.randint(stream_key, (), max(1, total - reach), min(reach, total - 1) + 1)
        return jnp.stack([one, total - one])
    sizes = jnp.asarray(profile(number_of, total, reach, lean), jnp.int32)
    twos = (number_of - 1) // 2
    source_of, taker = sizes[1:1 + 2 * twos:2], sizes[2:2 + 2 * twos:2]
    margin = jnp.minimum(source_of - 1, reach - taker)
    passed = jax.random.randint(jax.random.fold_in(stream_key, 1), (twos,), 0, 1 << 20) % (margin + 1)
    sizes = sizes.at[1:1 + 2 * twos:2].set(source_of - passed).at[2:2 + 2 * twos:2].set(taker + passed)
    return sizes[jax.random.permutation(jax.random.fold_in(stream_key, 2), number_of)]


def normal_values(key, shape, spread, limit, split=(), kind=jnp.bfloat16):
    loudness = level_of(key, shape, split, -0.22, 0.18) if split else 1.0
    array = jax.random.normal(key, shape, jnp.float32) * spread * loudness
    return jnp.minimum(jnp.maximum(array, -limit), limit).astype(kind)


def setup_inputs(seed: int = 0, part: int = 0) -> dict:
    arg_keys = jax.random.split(jax.random.key(seed), 11)
    own_keys = jax.random.split(jax.random.fold_in(arg_keys[10], part), 11)
    return {
        "latlon_cotangent": normal_values(own_keys[0], (TIMES, C, LL_CELLS), 1.0, 6.0, ((2, 16),)),
        "healpix_cotangent": normal_values(own_keys[1], (TIMES, C, HP_CELLS), 1.0, 6.0, ((2, 16),)),
        "outward_weights": normal_values(arg_keys[2], (BLOCKS, T_SIZE, T_SIZE), (T_SIZE * B_DEV // TH_DEV) ** -0.5, 0.15625, ((0, 16),)),
        "outward_source": set_ends(jax.random.randint(arg_keys[3], (BLOCKS,), 0, TL_DEV), jax.random.fold_in(arg_keys[3], 1), 0, TL_DEV - 1).astype(jnp.int32),
        "outward_target": set_ends(jax.random.randint(arg_keys[4], (BLOCKS,), 0, TH_DEV), jax.random.fold_in(arg_keys[4], 1), 0, TH_DEV - 1).astype(jnp.int32),
        "outward_counts": jax.vmap(lambda own: uneven(own, N_CURVE, B_DEV, SLOT, 2))(jax.random.split(arg_keys[5], N_CURVE)).reshape((N_CURVE, N_CURVE)).astype(jnp.int32),
        "inward_weights": normal_values(arg_keys[6], (BLOCKS, T_SIZE, T_SIZE), (T_SIZE * B_DEV // TL_DEV) ** -0.5, 0.15625, ((0, 16),)),
        "inward_source": set_ends(jax.random.randint(arg_keys[7], (BLOCKS,), 0, TH_DEV), jax.random.fold_in(arg_keys[7], 1), 0, TH_DEV - 1).astype(jnp.int32),
        "inward_target": set_ends(jax.random.randint(arg_keys[8], (BLOCKS,), 0, TL_DEV), jax.random.fold_in(arg_keys[8], 1), 0, TL_DEV - 1).astype(jnp.int32),
        "inward_counts": jax.vmap(lambda own: uneven(own, N_CURVE, B_DEV, SLOT, 2))(jax.random.split(arg_keys[9], N_CURVE)).reshape((N_CURVE, N_CURVE)).astype(jnp.int32),
    }


def owners_of(count_row):
    inclusive = jnp.cumsum(count_row)
    positions = jnp.arange(B_DEV, dtype=jnp.int32)
    return jnp.sum((positions[:, None] >= inclusive[None, :]).astype(jnp.int32), axis=1)


def regrid(cotangent, weights, source, target, counts, tiles_in, tiles_out):
    width = weights.shape[1]
    lead = cotangent.shape[0] * cotangent.shape[1]
    tiled = cotangent.reshape(lead, N_CURVE * tiles_in, width)

    def visit(total, device):
        start = device * B_DEV
        block_weights = lax.dynamic_slice_in_dim(weights, start, B_DEV, 0)
        block_source = lax.dynamic_slice_in_dim(source, start, B_DEV, 0)
        block_target = lax.dynamic_slice_in_dim(target, start, B_DEV, 0)
        count_row = lax.dynamic_index_in_dim(counts, device, 0, keepdims=False)
        owner = owners_of(count_row)
        picked = jnp.take(tiled, (device * tiles_in + block_source).astype(jnp.int32), axis=1)
        products = jnp.einsum("kbi,bij->bkj", picked.astype(jnp.float32), block_weights.astype(jnp.float32))
        products = lax.optimization_barrier(products.astype(jnp.bfloat16)).astype(jnp.float32)
        total = total.at[(owner * tiles_out + block_target).astype(jnp.int32)].add(products)
        return total, None

    initial = jnp.zeros((N_CURVE * tiles_out, lead, width), jnp.float32)
    total, unused = lax.scan(visit, initial, jnp.arange(N_CURVE, dtype=jnp.int32))
    result = jnp.transpose(total, (1, 0, 2)).reshape(cotangent.shape[0], cotangent.shape[1], N_CURVE * tiles_out * width)
    return result.astype(jnp.bfloat16)


def reference(latlon_cotangent, healpix_cotangent, outward_weights, outward_source, outward_target, outward_counts, inward_weights, inward_source, inward_target, inward_counts):
    healpix_gradient = regrid(latlon_cotangent, outward_weights, outward_source, outward_target, outward_counts, TL_DEV, TH_DEV)
    latlon_gradient = regrid(healpix_cotangent, inward_weights, inward_source, inward_target, inward_counts, TH_DEV, TL_DEV)
    return healpix_gradient, latlon_gradient
```

```python
import functools

import jax
import jax.numpy as jnp
from jax import lax
from jax.experimental import pallas as pl
from jax.experimental.pallas import tpu as pltpu
from jax.sharding import PartitionSpec as P

LANES = 128
HALVES = 2
ACC_LIMIT = 16 * 1024 * 1024


def round_up(value, unit):
    return -(-value // unit) * unit


def block_products(cotangent, weights, source):
    width = weights.shape[1]
    lead = cotangent.shape[0] * cotangent.shape[1]
    tiled = cotangent.reshape(lead, cotangent.shape[2] // width, width)
    picked = jnp.take(tiled, source, axis=1)
    products = jnp.einsum("kbi,bij->bkj", picked, weights, preferred_element_type=jnp.float32)
    return products.astype(jnp.bfloat16)


def pack_slots(products, target, count_row):
    blocks = products.shape[0]
    devices = count_row.shape[0]
    per_device = 2 * blocks // devices
    inclusive = jnp.cumsum(count_row)
    exclusive = inclusive - count_row
    positions = jnp.arange(blocks, dtype=jnp.int32)
    owner = jnp.sum((positions[:, None] >= inclusive[None, :]).astype(jnp.int32), axis=1)
    chosen = owner[:, None] == jnp.arange(devices, dtype=jnp.int32)[None, :]
    first = jnp.sum(jnp.where(chosen, exclusive[None, :], 0), axis=1)
    slot_index = owner * per_device + positions - first
    buffer = (
        jnp.zeros((devices * per_device,) + products.shape[1:], jnp.bfloat16)
        .at[slot_index]
        .set(products)
    )
    labels = jnp.full((devices * per_device,), -1, jnp.int32).at[slot_index].set(target)
    return (buffer, labels)


def sum_slots(received, labels, tiles_out, like_shape):
    selector = (labels[None, :] == jnp.arange(tiles_out, dtype=jnp.int32)[:, None]).astype(
        jnp.bfloat16
    )
    summed = jnp.einsum("ts,skc->ktc", selector, received, preferred_element_type=jnp.float32)
    return summed.reshape(like_shape[0], like_shape[1], -1).astype(jnp.bfloat16)


def slot_remap(cotangent, weights, source, target, counts, like_shape):
    products = block_products(cotangent, weights, source)
    buffer, labels = pack_slots(products, target, counts[0])
    arrived = lax.all_to_all(buffer, "curve", split_axis=0, concat_axis=0, tiled=True)
    arrived_labels = lax.all_to_all(labels, "curve", split_axis=0, concat_axis=0, tiled=True)
    return sum_slots(arrived, arrived_labels, like_shape[2] // weights.shape[1], like_shape)


def place_of(owner, me, bits):
    differ = jnp.bitwise_xor(owner, me)
    place = jnp.bitwise_and(differ, 1)
    for bit in range(1, bits):
        place = place * 2 + jnp.bitwise_and(jnp.right_shift(differ, bit), 1)
    return place


def product_kernel(
    bits, channels, pitch, tiles, step_blocks,
    source, target, counts, x_ref, w_ref, *rest,
):
    sends, keeps = rest[:HALVES], rest[HALVES:2 * HALVES]
    acc, xs, stage, state, sems = rest[2 * HALVES:]
    devices = 1 << bits
    part = tiles // HALVES
    rows = devices * part * pitch
    half_rows = rows // 2
    step = pl.program_id(0)
    me = lax.axis_index("curve")

    @pl.when(step == 0)
    def start():
        @pl.loop(0, HALVES * devices)
        def clear(index):
            at = pl.multiple_of(index * (part * pitch), part * pitch)
            acc[pl.ds(at, part * pitch), :] = jnp.zeros((part * pitch, LANES), jnp.float32)

        for tile in range(xs.shape[0]):
            xs[tile] = jnp.zeros(xs.shape[1:], xs.dtype)
            xs[tile, :channels, :] = x_ref[0, :, tile * LANES:(tile + 1) * LANES]
        state[0] = 0
        state[1] = counts[0]

    owner, end = state[0], state[1]
    places = []
    for index in range(step_blocks):
        block = step * step_blocks + index
        passed = (block >= end).astype(jnp.int32)
        owner = jnp.minimum(owner + passed, devices - 1)
        end = end + passed * counts[owner]
        tile = target[block]
        half = (tile >= part).astype(jnp.int32)
        place = (half * devices + place_of(owner, me, bits)) * part + tile - half * part
        places.append(pl.multiple_of(place * pitch, 8))
    state[0] = owner
    state[1] = end
    for index in range(step_blocks):
        x = xs[source[step * step_blocks + index], :pitch, :]
        product = jnp.dot(x, w_ref[index], preferred_element_type=jnp.float32)
        acc[pl.ds(places[index], pitch), :] += product

    @pl.when(step == pl.num_programs(0) - 1)
    def finish():
        copies = []
        for half in range(HALVES):
            base = half * rows

            @pl.loop(0, devices // 2)
            def convert(index):
                unit = part * pitch
                at = pl.multiple_of(index * unit, unit)
                stage[half, pl.ds(at, unit), :] = acc[
                    pl.ds(base + half_rows + at, unit), :
                ].astype(jnp.bfloat16)

            copies.append(pltpu.make_async_copy(stage.at[half], sends[half], sems.at[2 * half]))
            copies[-1].start()
            copies.append(
                pltpu.make_async_copy(
                    acc.at[pl.ds(base, half_rows)], keeps[half], sems.at[2 * half + 1]
                )
            )
            copies[-1].start()
        for copy in copies:
            copy.wait()


def products(cotangent, weights, source, target, counts, tiles, bits):
    devices = 1 << bits
    channels = cotangent.shape[1]
    pitch = round_up(channels, 8)
    tiles_in = cotangent.shape[2] // LANES
    blocks = weights.shape[0]
    step_blocks = max(size for size in range(1, 17) if blocks % size == 0)
    part = tiles // HALVES
    half_rows = devices * part * pitch // 2
    send = jax.ShapeDtypeStruct((half_rows, LANES), jnp.bfloat16)
    keep = jax.ShapeDtypeStruct((half_rows, LANES), jnp.float32)
    return pl.pallas_call(
        functools.partial(product_kernel, bits, channels, pitch, tiles, step_blocks),
        out_shape=[send] * HALVES + [keep] * HALVES,
        grid_spec=pltpu.PrefetchScalarGridSpec(
            num_scalar_prefetch=3,
            grid=(blocks // step_blocks,),
            in_specs=[
                pl.BlockSpec(cotangent.shape, lambda step, *_: (0, 0, 0)),
                pl.BlockSpec((step_blocks, LANES, LANES), lambda step, *_: (step, 0, 0)),
            ],
            out_specs=[pl.BlockSpec(memory_space=pl.ANY)] * (2 * HALVES),
            scratch_shapes=[
                pltpu.VMEM((HALVES * 2 * half_rows, LANES), jnp.float32),
                pltpu.VMEM((tiles_in, round_up(pitch, 16), LANES), jnp.bfloat16),
                pltpu.VMEM((HALVES, half_rows, LANES), jnp.bfloat16),
                pltpu.SMEM((2,), jnp.int32),
                pltpu.SemaphoreType.DMA((2 * HALVES,)),
            ],
        ),
        compiler_params=pltpu.CompilerParams(vmem_limit_bytes=32 * 1024 * 1024),
        cost_estimate=pl.CostEstimate(
            flops=2 * blocks * channels * LANES * LANES,
            bytes_accessed=2 * weights.size + 6 * HALVES * half_rows * LANES,
            transcendentals=0,
        ),
    )(source, target, counts.reshape(-1), cotangent, weights)


def exchange(value, bit, devices):
    return lax.ppermute(value, "curve", [(at, at ^ (1 << bit)) for at in range(devices)])


def reduce_halves(send, keep, bits):
    devices = 1 << bits
    terms = [keep]
    length = keep.shape[0]
    for bit in range(bits):
        terms.append(exchange(send, bit, devices))
        length //= 2
        if bit + 1 < bits:
            total = sum(term[length:2 * length].astype(jnp.float32) for term in terms)
            send = total.astype(jnp.bfloat16)
    return terms


def final_kernel(channels, pitch, part, count, *refs):
    out = refs[-1]
    for half in range(HALVES):
        terms = refs[half * count:(half + 1) * count]
        for tile in range(part):
            total = sum(
                term[tile * pitch:(tile + 1) * pitch, :].astype(jnp.float32) for term in terms
            )
            at = (half * part + tile) * LANES
            out[0, :, at:at + LANES] = total[:channels].astype(jnp.bfloat16)


def final_sum(terms, like_shape, pitch, part):
    rows = part * pitch
    flat = [term for half in terms for term in half]
    return pl.pallas_call(
        functools.partial(final_kernel, like_shape[1], pitch, part, len(terms[0])),
        out_shape=jax.ShapeDtypeStruct(like_shape, jnp.bfloat16),
        grid=(1,),
        in_specs=[pl.BlockSpec((rows, LANES), lambda step: (0, 0)) for _ in flat],
        out_specs=pl.BlockSpec(like_shape, lambda step: (0, 0, 0)),
        compiler_params=pltpu.CompilerParams(vmem_limit_bytes=32 * 1024 * 1024),
    )(*flat)


def bit_remaps(remaps, bits):
    made = []
    for cotangent, weights, source, target, counts, like_shape in remaps:
        tiles = like_shape[2] // LANES
        made.append(products(cotangent, weights, source, target, counts, tiles, bits))
    results = []
    for arrays, remap in zip(made, remaps):
        like_shape = remap[-1]
        terms = [reduce_halves(arrays[half], arrays[HALVES + half], bits) for half in range(HALVES)]
        part = like_shape[2] // LANES // HALVES
        results.append(final_sum(terms, like_shape, round_up(like_shape[1], 8), part))
    return results


def on_device(devices, *args):
    latlon, healpix = args[:2]
    remaps = [
        (latlon, args[2], args[3], args[4], args[5], healpix.shape),
        (healpix, args[6], args[7], args[8], args[9], latlon.shape),
    ]
    bits = devices.bit_length() - 1
    tiles = max(latlon.shape[2], healpix.shape[2]) // LANES
    size = devices * tiles * round_up(latlon.shape[1], 8) * LANES * 4
    if devices == 1 << bits and bits > 0 and size <= ACC_LIMIT:
        return tuple(bit_remaps(remaps, bits))
    return tuple(slot_remap(*remap) for remap in remaps)


def solution(mesh):
    in_specs = (
        P("groups", None, "curve"),
        P("groups", None, "curve"),
        P("curve", None, None),
        P("curve"),
        P("curve"),
        P("curve", None),
        P("curve", None, None),
        P("curve"),
        P("curve"),
        P("curve", None),
    )
    out_specs = (P("groups", None, "curve"), P("groups", None, "curve"))
    return jax.shard_map(
        functools.partial(on_device, mesh.shape["curve"]),
        mesh=mesh, in_specs=in_specs, out_specs=out_specs, check_vma=False,
    )
```

```python
import functools

import jax
import jax.numpy as jnp
from jax import lax
from jax.experimental import pallas as pl
from jax.experimental.pallas import tpu as pltpu
from jax.sharding import PartitionSpec as P

LANES = 128
ACC_LIMIT = 16 * 1024 * 1024
UNROLL = 8
PARTS = 4


def round_up(value, unit):
    return -(-value // unit) * unit


def block_products(cotangent, weights, source):
    width = weights.shape[1]
    lead = cotangent.shape[0] * cotangent.shape[1]
    tiled = cotangent.reshape(lead, cotangent.shape[2] // width, width)
    picked = jnp.take(tiled, source, axis=1)
    products = jnp.einsum("kbi,bij->bkj", picked, weights, preferred_element_type=jnp.float32)
    return products.astype(jnp.bfloat16)


def pack_slots(products, target, count_row):
    blocks = products.shape[0]
    devices = count_row.shape[0]
    per_device = 2 * blocks // devices
    inclusive = jnp.cumsum(count_row)
    exclusive = inclusive - count_row
    positions = jnp.arange(blocks, dtype=jnp.int32)
    owner = jnp.sum((positions[:, None] >= inclusive[None, :]).astype(jnp.int32), axis=1)
    chosen = owner[:, None] == jnp.arange(devices, dtype=jnp.int32)[None, :]
    first = jnp.sum(jnp.where(chosen, exclusive[None, :], 0), axis=1)
    slot_index = owner * per_device + positions - first
    buffer = (
        jnp.zeros((devices * per_device,) + products.shape[1:], jnp.bfloat16)
        .at[slot_index]
        .set(products)
    )
    labels = jnp.full((devices * per_device,), -1, jnp.int32).at[slot_index].set(target)
    return (buffer, labels)


def sum_slots(received, labels, tiles_out, like_shape):
    selector = (labels[None, :] == jnp.arange(tiles_out, dtype=jnp.int32)[:, None]).astype(
        jnp.bfloat16
    )
    summed = jnp.einsum("ts,skc->ktc", selector, received, preferred_element_type=jnp.float32)
    return summed.reshape(like_shape[0], like_shape[1], -1).astype(jnp.bfloat16)


def slot_remap(cotangent, weights, source, target, counts, like_shape):
    products = block_products(cotangent, weights, source)
    buffer, labels = pack_slots(products, target, counts[0])
    arrived = lax.all_to_all(buffer, "curve", split_axis=0, concat_axis=0, tiled=True)
    arrived_labels = lax.all_to_all(labels, "curve", split_axis=0, concat_axis=0, tiled=True)
    return sum_slots(arrived, arrived_labels, like_shape[2] // weights.shape[1], like_shape)


def slots_of(stages):
    return [[sum(((m >> i) & 1) << bit for i, bit in enumerate(stage)) for m in range(1 << len(stage))]
            for stage in stages]


def owners_in_order(stages):
    masks = [0]
    for stage in slots_of(stages):
        masks = [left + right for left in masks for right in stage]
    return masks


def product_kernel(
    bits, channels, pitch, chunks, first,
    source_hbm, target_hbm, counts_hbm, x_hbm, w_hbm, *rest,
):
    number = len(chunks)
    sends, keeps = rest[:number], rest[number:2 * number]
    acc, xs, x_in, w, source, target, counts, list_block, list_row, sems = rest[2 * number:]
    devices = 1 << bits
    blocks = w.shape[0]
    per_part = blocks // PARTS
    me = lax.axis_index("curve")

    scalars = [
        pltpu.make_async_copy(source_hbm, source, sems.at[0]),
        pltpu.make_async_copy(target_hbm, target, sems.at[1]),
        pltpu.make_async_copy(counts_hbm, counts, sems.at[2]),
    ]
    x_copy = pltpu.make_async_copy(x_hbm, x_in, sems.at[3])
    w_copies = [
        pltpu.make_async_copy(
            w_hbm.at[pl.ds(part * per_part, per_part)], w.at[pl.ds(part * per_part, per_part)],
            sems.at[4 + part],
        )
        for part in range(PARTS)
    ]
    for copy in scalars + [x_copy] + w_copies:
        copy.start()

    trash = acc.shape[0] - pitch

    @pl.loop(0, acc.shape[0] // pitch)
    def clear(index):
        acc[pl.ds(pl.multiple_of(index * pitch, pitch), pitch), :] = jnp.zeros((pitch, LANES), jnp.float32)

    for tile in range(xs.shape[0]):
        xs[tile] = jnp.zeros(xs.shape[1:], xs.dtype)
    for copy in scalars:
        copy.wait()

    bases, base = [], 0
    for low, high, stages in chunks:
        bases.append(base)
        base += devices // 2 * (high - low)
    length = jnp.int32(0)
    begin = jnp.int32(0)
    marks = [jnp.int32(0)] * (PARTS - 1)
    for owner in range(devices):
        differ = jnp.bitwise_xor(me, owner)
        count = counts[0, owner]
        starts, takes = [], []
        for base, (low, high, stages) in zip(bases, chunks):
            picked = jnp.bitwise_and(jnp.right_shift(differ, stages[1][0]), 1)
            takes.append(picked if first else 1 - picked)
            place = jnp.bitwise_and(jnp.right_shift(differ, stages[0][0]), 1)
            for stage in stages[2:]:
                for bit in reversed(stage):
                    place = place * 2 + jnp.bitwise_and(jnp.right_shift(differ, bit), 1)
            starts.append(base + place * (high - low) - low)

        def note(index, length, begin=begin, starts=starts, takes=takes):
            block = begin + index
            tile = target[block]
            place, take = starts[0], takes[0]
            for (low, high, stages), other, other_take in zip(chunks[1:], starts[1:], takes[1:]):
                place = jnp.where(tile >= low, other, place)
                take = jnp.where(tile >= low, other_take, take)
            list_block[length] = block
            list_row[length] = (place + tile) * pitch
            return length + take

        any_take = functools.reduce(jnp.maximum, takes)
        length = lax.fori_loop(0, count * any_take, note, length)
        begin = begin + count
        marks = [jnp.where(begin <= per_part * (part + 1), length, mark) for part, mark in enumerate(marks)]
    for index in range(UNROLL):
        list_block[length + index] = 0
        list_row[length + index] = trash

    x_copy.wait()
    for tile in range(xs.shape[0]):
        xs[tile, :channels, :] = x_in[0, :, tile * LANES:(tile + 1) * LANES]

    def some(step, carry):
        rows, found = [], []
        for index in range(UNROLL):
            at = step * UNROLL + index
            rows.append(pl.multiple_of(list_row[at], 8))
            found.append(list_block[at])
        for row, block in zip(rows, found):
            product = jnp.dot(xs[source[block], :pitch, :], w[block], preferred_element_type=jnp.float32)
            acc[pl.ds(row, pitch), :] += product
        return carry

    done = jnp.int32(0)
    for part in range(PARTS):
        w_copies[part].wait()
        upto = marks[part] // UNROLL if part + 1 < PARTS else (length + UNROLL - 1) // UNROLL
        lax.fori_loop(done, upto, some, jnp.int32(0))
        done = upto

    for base, (low, high, stages), send, keep in zip(bases, chunks, sends, keeps):
        unit = (high - low) * pitch
        places = devices // 4

        @pl.loop(0, places)
        def finish(index):
            at = pl.multiple_of(index * unit, 8)
            own = pl.multiple_of(base * pitch + index * unit, 8)
            other = pl.multiple_of((base + places * (high - low)) * pitch + index * unit, 8)
            send[pl.ds(at, unit), :] = acc[pl.ds(other, unit), :].astype(jnp.bfloat16)
            keep[pl.ds(at, unit), :] = acc[pl.ds(own, unit), :]


def products(remap, chunks, bits, first):
    cotangent, weights, source, target, counts = remap[:5]
    devices = 1 << bits
    channels = cotangent.shape[1]
    pitch = round_up(channels, 8)
    tiles_in = cotangent.shape[2] // LANES
    blocks = weights.shape[0]
    rows = [devices // 4 * (high - low) * pitch for low, high, stages in chunks]
    whole = pl.BlockSpec(memory_space=pltpu.VMEM)
    sums = sum(rows) * 2 + pitch
    return pl.pallas_call(
        functools.partial(product_kernel, bits, channels, pitch, chunks, first),
        out_shape=[jax.ShapeDtypeStruct((size, LANES), jnp.bfloat16) for size in rows]
        + [jax.ShapeDtypeStruct((size, LANES), jnp.float32) for size in rows],
        in_specs=[pl.BlockSpec(memory_space=pltpu.HBM)] * 5,
        out_specs=[whole] * (2 * len(rows)),
        scratch_shapes=[
            pltpu.VMEM((sums, LANES), jnp.float32),
            pltpu.VMEM((tiles_in, round_up(pitch, 16), LANES), jnp.bfloat16),
            pltpu.VMEM(cotangent.shape, jnp.bfloat16),
            pltpu.VMEM(weights.shape, jnp.bfloat16),
            pltpu.SMEM(source.shape, jnp.int32),
            pltpu.SMEM(target.shape, jnp.int32),
            pltpu.SMEM(counts.shape, jnp.int32),
            pltpu.SMEM((blocks + UNROLL,), jnp.int32),
            pltpu.SMEM((blocks + UNROLL,), jnp.int32),
            pltpu.SemaphoreType.DMA((4 + PARTS,)),
        ],
        compiler_params=pltpu.CompilerParams(vmem_limit_bytes=28 * 1024 * 1024),
        cost_estimate=pl.CostEstimate(
            flops=blocks * channels * LANES * LANES,
            bytes_accessed=2 * weights.size + 6 * sum(rows) * LANES,
            transcendentals=0,
        ),
    )(*[pltpu.with_memory_space_constraint(value, pltpu.HBM) for value in (source, target, counts, cotangent, weights)])


def exchange(value, mask, devices):
    return lax.ppermute(value, "curve", [(at, at ^ mask) for at in range(devices)])


def added(terms, low, high):
    return sum(term[low:high].astype(jnp.float32) for term in terms)


class Chain:
    def __init__(self, remap, chunk, bits):
        self.remap, self.chunk, self.devices = remap, chunk, 1 << bits
        self.slots = slots_of(chunk[2])
        self.stage = 2

    def take_first(self, send, keep):
        self.first_keep = keep
        self.first_got = exchange(send, self.slots[0][1], self.devices)

    def sum_first(self):
        total = added([self.first_keep, self.first_got], 0, self.first_keep.shape[0])
        self.total = total.astype(jnp.bfloat16)

    def send_second(self):
        self.got = [exchange(self.total, self.slots[1][1], self.devices)]

    def take_rest(self, send, keep):
        self.terms = [keep, exchange(send, self.slots[0][1], self.devices)]
        self.length = keep.shape[0]

    def send_next(self):
        self.terms = self.terms + self.got
        masks = self.slots[self.stage]
        self.length //= len(masks)
        self.got = []
        for place, mask in enumerate(masks[1:], 1):
            total = added(self.terms, place * self.length, (place + 1) * self.length)
            self.got.append(exchange(total.astype(jnp.bfloat16), mask, self.devices))
        self.stage += 1

    def finish(self):
        self.terms = self.terms + self.got
        return self.terms


def final_kernel(channels, pitch, parts, *refs):
    out = refs[-1]
    at = 0
    for low, high, count in parts:
        terms = refs[at:at + count]
        at += count
        for tile in range(high - low):
            total = sum(
                term[tile * pitch:(tile + 1) * pitch, :].astype(jnp.float32) for term in terms
            )
            lane = (low + tile) * LANES
            out[0, :, lane:lane + LANES] = total[:channels].astype(jnp.bfloat16)


def final_sum(chains, like_shape, pitch):
    parts = [(chain.chunk[0], chain.chunk[1], len(chain.terms)) for chain in chains]
    flat, specs = [], []
    for chain in chains:
        rows = (chain.chunk[1] - chain.chunk[0]) * pitch
        for term in chain.terms:
            flat.append(term)
            specs.append(pl.BlockSpec((rows, LANES), lambda step: (0, 0)))
    return pl.pallas_call(
        functools.partial(final_kernel, like_shape[1], pitch, parts),
        out_shape=jax.ShapeDtypeStruct(like_shape, jnp.bfloat16),
        grid=(1,),
        in_specs=specs,
        out_specs=pl.BlockSpec(like_shape, lambda step: (0, 0, 0)),
        compiler_params=pltpu.CompilerParams(vmem_limit_bytes=28 * 1024 * 1024),
    )(*flat)


def plan(tiles, bits):
    stages = tuple((bit,) for bit in range(bits))
    half = tiles // 2
    return [
        [(0, half, stages), (half, tiles, stages)],
        [(0, half, stages), (half, tiles, stages)],
    ]


def bit_remaps(remaps, bits):
    chunks = [plan(remap[-1][2] // LANES, bits)[index] for index, remap in enumerate(remaps)]
    chains = [[Chain(remap, chunk, bits) for chunk in own] for remap, own in zip(remaps, chunks)]
    for index, remap in enumerate(remaps):
        made = products(remap, chunks[index], bits, True)
        number = len(chunks[index])
        for chain, send, keep in zip(chains[index], made[:number], made[number:]):
            chain.take_first(send, keep)
            chain.sum_first()
    for index, remap in enumerate(remaps):
        sent = [chain.total for chain in chains[index]]
        tied = lax.optimization_barrier((remap[0], *sent))
        for chain, total in zip(chains[index], tied[1:]):
            chain.total = total
            chain.send_second()
        made = products((tied[0],) + remap[1:], chunks[index], bits, False)
        number = len(chunks[index])
        for chain, send, keep in zip(chains[index], made[:number], made[number:]):
            chain.take_rest(send, keep)
    line = [chain for own in chains for chain in own]
    for step in range(len(line) + bits - 3):
        ready = [chain for place, chain in enumerate(line)
                 if chain.stage == 2 + step - place and chain.stage < len(chain.slots)]
        tied = lax.optimization_barrier([chain.got for chain in ready])
        for chain, got in zip(ready, tied):
            chain.got = got
        for chain in reversed(ready):
            chain.send_next()
    results = []
    for index, remap in enumerate(remaps):
        for chain in chains[index]:
            chain.finish()
        results.append(final_sum(chains[index], remap[-1], round_up(remap[-1][1], 8)))
    return results


def on_device(devices, *args):
    latlon, healpix = args[:2]
    remaps = [
        (latlon, args[2], args[3], args[4], args[5], healpix.shape),
        (healpix, args[6], args[7], args[8], args[9], latlon.shape),
    ]
    bits = devices.bit_length() - 1
    tiles = max(latlon.shape[2], healpix.shape[2]) // LANES
    size = devices * tiles * round_up(latlon.shape[1], 8) * LANES * 4
    if devices == 1 << bits and bits > 2 and size <= ACC_LIMIT:
        return tuple(bit_remaps(remaps, bits))
    return tuple(slot_remap(*remap) for remap in remaps)


def solution(mesh):
    in_specs = (
        P("groups", None, "curve"),
        P("groups", None, "curve"),
        P("curve", None, None),
        P("curve"),
        P("curve"),
        P("curve", None),
        P("curve", None, None),
        P("curve"),
        P("curve"),
        P("curve", None),
    )
    out_specs = (P("groups", None, "curve"), P("groups", None, "curve"))
    return jax.shard_map(
        functools.partial(on_device, mesh.shape["curve"]),
        mesh=mesh, in_specs=in_specs, out_specs=out_specs, check_vma=False,
    )
```

```python
import functools

import jax
import jax.numpy as jnp
from jax import lax
from jax.experimental import pallas as pl
from jax.experimental.pallas import tpu as pltpu
from jax.sharding import PartitionSpec as P

LANES = 128
ACC_LIMIT = 16 * 1024 * 1024


def round_up(value, unit):
    return -(-value // unit) * unit


def block_products(cotangent, weights, source):
    width = weights.shape[1]
    lead = cotangent.shape[0] * cotangent.shape[1]
    tiled = cotangent.reshape(lead, cotangent.shape[2] // width, width)
    picked = jnp.take(tiled, source, axis=1)
    products = jnp.einsum("kbi,bij->bkj", picked, weights, preferred_element_type=jnp.float32)
    return products.astype(jnp.bfloat16)


def pack_slots(products, target, count_row):
    blocks = products.shape[0]
    devices = count_row.shape[0]
    per_device = 2 * blocks // devices
    inclusive = jnp.cumsum(count_row)
    exclusive = inclusive - count_row
    positions = jnp.arange(blocks, dtype=jnp.int32)
    owner = jnp.sum((positions[:, None] >= inclusive[None, :]).astype(jnp.int32), axis=1)
    chosen = owner[:, None] == jnp.arange(devices, dtype=jnp.int32)[None, :]
    first = jnp.sum(jnp.where(chosen, exclusive[None, :], 0), axis=1)
    slot_index = owner * per_device + positions - first
    buffer = (
        jnp.zeros((devices * per_device,) + products.shape[1:], jnp.bfloat16)
        .at[slot_index]
        .set(products)
    )
    labels = jnp.full((devices * per_device,), -1, jnp.int32).at[slot_index].set(target)
    return (buffer, labels)


def sum_slots(received, labels, tiles_out, like_shape):
    selector = (labels[None, :] == jnp.arange(tiles_out, dtype=jnp.int32)[:, None]).astype(
        jnp.bfloat16
    )
    summed = jnp.einsum("ts,skc->ktc", selector, received, preferred_element_type=jnp.float32)
    return summed.reshape(like_shape[0], like_shape[1], -1).astype(jnp.bfloat16)


def slot_remap(cotangent, weights, source, target, counts, like_shape):
    products = block_products(cotangent, weights, source)
    buffer, labels = pack_slots(products, target, counts[0])
    arrived = lax.all_to_all(buffer, "curve", split_axis=0, concat_axis=0, tiled=True)
    arrived_labels = lax.all_to_all(labels, "curve", split_axis=0, concat_axis=0, tiled=True)
    return sum_slots(arrived, arrived_labels, like_shape[2] // weights.shape[1], like_shape)


def product_kernel(
    devices, channels, pitch, tiles, step_blocks,
    source_hbm, target_hbm, counts_hbm, x_hbm, w_hbm, out, acc, xs, x_in, w, source, target, counts, sems,
):
    steps = w.shape[0] // step_blocks
    scalars = [
        pltpu.make_async_copy(source_hbm, source, sems.at[0]),
        pltpu.make_async_copy(target_hbm, target, sems.at[1]),
        pltpu.make_async_copy(counts_hbm, counts, sems.at[2]),
    ]
    x_copy = pltpu.make_async_copy(x_hbm, x_in, sems.at[3])

    def w_copy(step):
        at = pl.ds(step * step_blocks, step_blocks)
        return pltpu.make_async_copy(w_hbm.at[at], w.at[at], sems.at[4 + step])

    for copy in scalars + [x_copy]:
        copy.start()
    for step in range(steps):
        w_copy(step).start()

    @pl.loop(0, acc.shape[0] // pitch)
    def clear(index):
        acc[pl.ds(pl.multiple_of(index * pitch, pitch), pitch), :] = jnp.zeros((pitch, LANES), jnp.float32)

    for tile in range(xs.shape[0]):
        xs[tile] = jnp.zeros(xs.shape[1:], xs.dtype)
    x_copy.wait()
    for tile in range(xs.shape[0]):
        xs[tile, :channels, :] = x_in[0, :, tile * LANES:(tile + 1) * LANES]
    for copy in scalars:
        copy.wait()

    def some(step, carry):
        owner, end = carry
        w_copy(step).wait()
        rows = []
        for index in range(step_blocks):
            block = step * step_blocks + index
            passed = (block >= end).astype(jnp.int32)
            owner = jnp.minimum(owner + passed, devices - 1)
            end = end + passed * counts[0, owner]
            rows.append(pl.multiple_of((owner * tiles + target[block]) * pitch, 8))
        for index, row in enumerate(rows):
            block = step * step_blocks + index
            product = jnp.dot(xs[source[block], :pitch, :], w[block], preferred_element_type=jnp.float32)
            acc[pl.ds(row, pitch), :] += product
        return owner, end

    lax.fori_loop(0, steps, some, (jnp.int32(0), counts[0, 0]))

    @pl.loop(0, devices)
    def finish(index):
        unit = tiles * pitch
        at = pl.multiple_of(index * unit, 8)
        out[pl.ds(at, unit), :] = acc[pl.ds(at, unit), :].astype(out.dtype)


def sums(cotangent, weights, source, target, counts, like_shape):
    devices = counts.shape[1]
    channels = cotangent.shape[1]
    pitch = round_up(channels, 8)
    tiles_in, tiles = cotangent.shape[2] // LANES, like_shape[2] // LANES
    blocks = weights.shape[0]
    step_blocks = max(size for size in range(1, 17) if blocks % size == 0)
    rows = devices * tiles * pitch
    return pl.pallas_call(
        functools.partial(product_kernel, devices, channels, pitch, tiles, step_blocks),
        out_shape=jax.ShapeDtypeStruct((rows, LANES), jnp.bfloat16),
        in_specs=[pl.BlockSpec(memory_space=pltpu.HBM)] * 5,
        out_specs=pl.BlockSpec(memory_space=pltpu.VMEM),
        scratch_shapes=[
            pltpu.VMEM((rows, LANES), jnp.float32),
            pltpu.VMEM((tiles_in, round_up(pitch, 16), LANES), jnp.bfloat16),
            pltpu.VMEM(cotangent.shape, jnp.bfloat16),
            pltpu.VMEM(weights.shape, jnp.bfloat16),
            pltpu.SMEM(source.shape, jnp.int32),
            pltpu.SMEM(target.shape, jnp.int32),
            pltpu.SMEM(counts.shape, jnp.int32),
            pltpu.SemaphoreType.DMA((4 + blocks // step_blocks,)),
        ],
        compiler_params=pltpu.CompilerParams(vmem_limit_bytes=28 * 1024 * 1024),
        cost_estimate=pl.CostEstimate(
            flops=2 * blocks * channels * LANES * LANES, bytes_accessed=2 * weights.size + 2 * rows * LANES,
            transcendentals=0,
        ),
    )(*[pltpu.with_memory_space_constraint(value, pltpu.HBM) for value in (source, target, counts, cotangent, weights)])


def final_kernel(channels, pitch, tiles, total, out):
    for tile in range(tiles):
        out[0, :, tile * LANES:(tile + 1) * LANES] = total[tile * pitch:tile * pitch + channels, :]


def sum_remap(cotangent, weights, source, target, counts, like_shape):
    made = sums(cotangent, weights, source, target, counts, like_shape)
    total = lax.psum_scatter(made, "curve", scatter_dimension=0, tiled=True)
    return pl.pallas_call(
        functools.partial(
            final_kernel, like_shape[1], round_up(like_shape[1], 8), like_shape[2] // LANES
        ),
        out_shape=jax.ShapeDtypeStruct(like_shape, jnp.bfloat16),
    )(total)


def on_device(devices, *args):
    latlon, healpix = args[:2]
    remaps = [
        (latlon, args[2], args[3], args[4], args[5], healpix.shape),
        (healpix, args[6], args[7], args[8], args[9], latlon.shape),
    ]
    bits = devices.bit_length() - 1
    tiles = max(latlon.shape[2], healpix.shape[2]) // LANES
    size = devices * tiles * round_up(latlon.shape[1], 8) * LANES * 4
    if devices == 1 << bits and bits > 2 and size <= ACC_LIMIT:
        return tuple(sum_remap(*remap) for remap in remaps)
    return tuple(slot_remap(*remap) for remap in remaps)


def solution(mesh):
    in_specs = (
        P("groups", None, "curve"),
        P("groups", None, "curve"),
        P("curve", None, None),
        P("curve"),
        P("curve"),
        P("curve", None),
        P("curve", None, None),
        P("curve"),
        P("curve"),
        P("curve", None),
    )
    out_specs = (P("groups", None, "curve"), P("groups", None, "curve"))
    return jax.shard_map(
        functools.partial(on_device, mesh.shape["curve"]),
        mesh=mesh, in_specs=in_specs, out_specs=out_specs, check_vma=False,
    )
```

```python
import functools

import jax
import jax.numpy as jnp
from jax import lax
from jax.experimental import pallas as pl
from jax.experimental.pallas import tpu as pltpu
from jax.sharding import PartitionSpec as P

LANES = 128
ACC_LIMIT = 16 * 1024 * 1024


def round_up(value, unit):
    return -(-value // unit) * unit


def block_products(cotangent, weights, source):
    width = weights.shape[1]
    lead = cotangent.shape[0] * cotangent.shape[1]
    tiled = cotangent.reshape(lead, cotangent.shape[2] // width, width)
    picked = jnp.take(tiled, source, axis=1)
    products = jnp.einsum("kbi,bij->bkj", picked, weights, preferred_element_type=jnp.float32)
    return products.astype(jnp.bfloat16)


def pack_slots(products, target, count_row):
    blocks = products.shape[0]
    devices = count_row.shape[0]
    per_device = 2 * blocks // devices
    inclusive = jnp.cumsum(count_row)
    exclusive = inclusive - count_row
    positions = jnp.arange(blocks, dtype=jnp.int32)
    owner = jnp.sum((positions[:, None] >= inclusive[None, :]).astype(jnp.int32), axis=1)
    chosen = owner[:, None] == jnp.arange(devices, dtype=jnp.int32)[None, :]
    first = jnp.sum(jnp.where(chosen, exclusive[None, :], 0), axis=1)
    slot_index = owner * per_device + positions - first
    buffer = (
        jnp.zeros((devices * per_device,) + products.shape[1:], jnp.bfloat16)
        .at[slot_index]
        .set(products)
    )
    labels = jnp.full((devices * per_device,), -1, jnp.int32).at[slot_index].set(target)
    return (buffer, labels)


def sum_slots(received, labels, tiles_out, like_shape):
    selector = (labels[None, :] == jnp.arange(tiles_out, dtype=jnp.int32)[:, None]).astype(
        jnp.bfloat16
    )
    summed = jnp.einsum("ts,skc->ktc", selector, received, preferred_element_type=jnp.float32)
    return summed.reshape(like_shape[0], like_shape[1], -1).astype(jnp.bfloat16)


def slot_remap(cotangent, weights, source, target, counts, like_shape):
    products = block_products(cotangent, weights, source)
    buffer, labels = pack_slots(products, target, counts[0])
    arrived = lax.all_to_all(buffer, "curve", split_axis=0, concat_axis=0, tiled=True)
    arrived_labels = lax.all_to_all(labels, "curve", split_axis=0, concat_axis=0, tiled=True)
    return sum_slots(arrived, arrived_labels, like_shape[2] // weights.shape[1], like_shape)


def slots_of(stages):
    return [[sum(((m >> i) & 1) << bit for i, bit in enumerate(stage)) for m in range(1 << len(stage))]
            for stage in stages]


def owners_in_order(stages):
    masks = [0]
    for stage in slots_of(stages):
        masks = [left + right for left in masks for right in stage]
    return masks


def product_kernel(
    bits, channels, pitch, chunks, step_blocks,
    source_hbm, target_hbm, counts_hbm, x_hbm, w_hbm, *rest,
):
    number = len(chunks)
    outs, (acc, xs, x_in, w, source, target, counts, places, sems) = rest[:4], rest[4:]
    devices = 1 << bits
    steps = w.shape[0] // step_blocks
    me = lax.axis_index("curve")

    scalars = [
        pltpu.make_async_copy(source_hbm, source, sems.at[0]),
        pltpu.make_async_copy(target_hbm, target, sems.at[1]),
        pltpu.make_async_copy(counts_hbm, counts, sems.at[2]),
    ]
    x_copy = pltpu.make_async_copy(x_hbm, x_in, sems.at[3])

    def w_copy(step):
        at = pl.ds(step * step_blocks, step_blocks)
        return pltpu.make_async_copy(w_hbm.at[at], w.at[at], sems.at[4 + step])

    for copy in scalars + [x_copy]:
        copy.start()
    for step in range(steps):
        w_copy(step).start()

    @pl.loop(0, acc.shape[0] // pitch)
    def clear(index):
        acc[pl.ds(pl.multiple_of(index * pitch, pitch), pitch), :] = jnp.zeros((pitch, LANES), jnp.float32)

    for tile in range(xs.shape[0]):
        xs[tile] = jnp.zeros(xs.shape[1:], xs.dtype)

    bases, base = [], 0
    for chunk, (low, high, stages) in enumerate(chunks):
        bases.append(base)
        order = [stages[1], stages[0]] + list(stages[2:])
        for owner in range(devices):
            differ = jnp.bitwise_xor(me, owner)
            place = jnp.int32(0)
            for stage in order:
                for bit in reversed(stage):
                    place = place * 2 + jnp.bitwise_and(jnp.right_shift(differ, bit), 1)
            places[chunk, owner] = base + place * (high - low) - low
        base += devices * (high - low)

    x_copy.wait()
    for tile in range(xs.shape[0]):
        xs[tile, :channels, :] = x_in[0, :, tile * LANES:(tile + 1) * LANES]
    for copy in scalars:
        copy.wait()

    def some(step, carry):
        owner, end = carry
        w_copy(step).wait()
        rows = []
        for index in range(step_blocks):
            block = step * step_blocks + index
            passed = (block >= end).astype(jnp.int32)
            owner = jnp.minimum(owner + passed, devices - 1)
            end = end + passed * counts[0, owner]
            tile = target[block]
            place = places[0, owner]
            for chunk in range(1, number):
                place = jnp.where(tile >= chunks[chunk][0], places[chunk, owner], place)
            rows.append(pl.multiple_of((place + tile) * pitch, 8))
        for index, row in enumerate(rows):
            block = step * step_blocks + index
            product = jnp.dot(xs[source[block], :pitch, :], w[block], preferred_element_type=jnp.float32)
            acc[pl.ds(row, pitch), :] += product
        return owner, end

    lax.fori_loop(0, steps, some, (jnp.int32(0), counts[0, 0]))

    for base, (low, high, stages) in zip(bases, chunks):
        unit = (high - low) * pitch
        quarter = devices // 4

        @pl.loop(0, quarter)
        def finish(index):
            at = pl.multiple_of(quarter * low * pitch + index * unit, 8)
            for part, ref in enumerate(outs):
                row = pl.multiple_of((base + part * quarter * (high - low)) * pitch + index * unit, 8)
                ref[pl.ds(at, unit), :] = acc[pl.ds(row, unit), :].astype(ref.dtype)


def products(remap, chunks, bits):
    cotangent, weights, source, target, counts = remap[:5]
    devices = 1 << bits
    channels = cotangent.shape[1]
    pitch = round_up(channels, 8)
    tiles_in = cotangent.shape[2] // LANES
    blocks = weights.shape[0]
    step_blocks = max(size for size in range(1, 17) if blocks % size == 0)
    rows = devices // 4 * chunks[-1][1] * pitch
    return pl.pallas_call(
        functools.partial(product_kernel, bits, channels, pitch, chunks, step_blocks),
        out_shape=[jax.ShapeDtypeStruct((rows, LANES), kind) for kind in (jnp.float32, jnp.bfloat16) * 2],
        in_specs=[pl.BlockSpec(memory_space=pltpu.HBM)] * 5,
        out_specs=[pl.BlockSpec(memory_space=pltpu.VMEM)] * 4,
        scratch_shapes=[
            pltpu.VMEM((rows * 4, LANES), jnp.float32),
            pltpu.VMEM((tiles_in, round_up(pitch, 16), LANES), jnp.bfloat16),
            pltpu.VMEM(cotangent.shape, jnp.bfloat16),
            pltpu.VMEM(weights.shape, jnp.bfloat16),
            pltpu.SMEM(source.shape, jnp.int32),
            pltpu.SMEM(target.shape, jnp.int32),
            pltpu.SMEM(counts.shape, jnp.int32),
            pltpu.SMEM((len(chunks), devices), jnp.int32),
            pltpu.SemaphoreType.DMA((4 + blocks // step_blocks,)),
        ],
        compiler_params=pltpu.CompilerParams(vmem_limit_bytes=28 * 1024 * 1024),
        cost_estimate=pl.CostEstimate(
            flops=2 * blocks * channels * LANES * LANES,
            bytes_accessed=2 * weights.size + 12 * rows * LANES,
            transcendentals=0,
        ),
    )(*[pltpu.with_memory_space_constraint(value, pltpu.HBM) for value in (source, target, counts, cotangent, weights)])


def exchange(value, mask, devices):
    return lax.ppermute(value, "curve", [(at, at ^ mask) for at in range(devices)])


def added(terms, low, high):
    return sum(term[low:high].astype(jnp.float32) for term in terms)


class Chain:
    def __init__(self, chunk, bits, pitch):
        self.chunk, self.devices = chunk, 1 << bits
        self.slots = slots_of(chunk[2])
        self.stage = 2
        self.base = self.devices // 4 * chunk[0] * pitch
        self.length = self.devices // 4 * (chunk[1] - chunk[0]) * pitch

    def first(self, terms, at):
        base = self.base - at
        self.total = added(terms, base, base + self.length).astype(jnp.bfloat16)

    def second(self):
        self.got = [exchange(self.total, self.slots[1][1], self.devices)]

    def rest(self, terms):
        self.terms = [(term, self.base) for term in terms]

    def part(self, place):
        at = place * self.length
        return sum(term[base + at:base + at + self.length].astype(jnp.float32) for term, base in self.terms)

    def send_next(self):
        self.terms = self.terms + [(got, 0) for got in self.got]
        masks = self.slots[self.stage]
        self.length //= len(masks)
        self.sent = [self.part(place).astype(jnp.bfloat16) for place in range(1, len(masks))]
        self.got = [exchange(sent, mask, self.devices) for sent, mask in zip(self.sent, masks[1:])]
        self.stage += 1

    def finish(self):
        self.terms = self.terms + [(got, 0) for got in self.got]
        self.sent = ()


def final_kernel(channels, pitch, parts, *refs):
    out = refs[-1]
    at = 0
    for low, high, count in parts:
        terms = refs[at:at + count]
        at += count
        for tile in range(high - low):
            total = sum(
                term[tile * pitch:(tile + 1) * pitch, :].astype(jnp.float32) for term in terms
            )
            lane = (low + tile) * LANES
            out[0, :, lane:lane + LANES] = total[:channels].astype(jnp.bfloat16)


def final_sum(chains, like_shape, pitch):
    parts = [(chain.chunk[0], chain.chunk[1], len(chain.terms)) for chain in chains]
    flat, specs = [], []
    for chain in chains:
        rows = (chain.chunk[1] - chain.chunk[0]) * pitch
        for term, base in chain.terms:
            flat.append(term if base % rows == 0 else term[base:base + rows])
            at = base // rows if base % rows == 0 else 0
            specs.append(pl.BlockSpec((rows, LANES), lambda step, at=at: (at, 0)))
    return pl.pallas_call(
        functools.partial(final_kernel, like_shape[1], pitch, parts),
        out_shape=jax.ShapeDtypeStruct(like_shape, jnp.bfloat16),
        grid=(1,),
        in_specs=specs,
        out_specs=pl.BlockSpec(like_shape, lambda step: (0, 0, 0)),
        compiler_params=pltpu.CompilerParams(vmem_limit_bytes=28 * 1024 * 1024),
    )(*flat)


def plan(tiles, bits):
    later = tuple((bit,) for bit in range(3, bits))
    straight = ((0,), (1,), (2,)) + later
    turned = ((0,), (2,), (1,)) + later
    half, more, most = tiles // 2, (tiles + 2) * 7 // 14, tiles * 5 // 6
    return (
        [(0, more, straight), (more, tiles, turned)],
        [(0, half, straight), (half, most, straight), (most, tiles, straight)],
    )


class Order:
    def __init__(self):
        self.last = ()

    def after(self, values):
        values, unused = lax.optimization_barrier((values, self.last))
        return values

    def before(self, values):
        self.last = values


def bit_remaps(remaps, bits):
    one, two = remaps
    devices = 1 << bits
    pitch = round_up(one[-1][1], 8)
    plans = plan(one[-1][2] // LANES, bits)
    ones, twos = [[Chain(chunk, bits, pitch) for chunk in chunks] for chunks in plans]
    order = Order()

    def step(*chains):
        gots = order.after([chain.got for chain in chains])
        for chain, got in zip(chains, gots):
            chain.got = got
            if chain.stage < len(chain.slots):
                chain.send_next()
            else:
                chain.finish()
        order.before([chain.sent for chain in chains])

    def summed(line, terms, at):
        terms = order.after(terms)
        for chain in line:
            chain.first(terms, at)
        order.before([chain.total for chain in line])

    def both_cores(keep, send):
        return [keep, exchange(send, 1, devices)]

    keep, send, keep_on, send_on = products(one, plans[0], bits)
    on = both_cores(keep_on, send_on)
    rest = both_cores(keep, send)
    summed(ones, on, 0)
    for chain in ones:
        chain.second()
    rest = order.after(rest)
    order.before(rest)
    for chain in ones:
        chain.rest(rest)
    keep, send, keep_on, send_on = products((order.after(two[0]),) + two[1:], plans[1], bits)
    cut = devices // 4 * plans[1][0][1] * pitch
    on = [both_cores(keep_on[:cut], send_on[:cut]), both_cores(keep_on[cut:], send_on[cut:])]
    late = both_cores(keep, send)
    step(ones[1])
    step(ones[0])
    summed(twos[:1], on[0], 0)
    twos[0].second()
    step(ones[1])
    step(ones[0])
    summed(twos[1:], on[1], cut)
    twos[1].second()
    late = order.after(late)
    order.before(late)
    for chain in twos:
        chain.rest(late)
    step(twos[0])
    twos[2].total = order.after(twos[2].total)
    twos[2].second()
    step(twos[1])
    step(twos[0])
    step(*ones)
    step(twos[2])
    step(twos[1])
    step(twos[2])
    step(*twos)
    return [final_sum(line, remap[-1], pitch) for line, remap in zip((ones, twos), remaps)]


def on_device(devices, *args):
    latlon, healpix = args[:2]
    remaps = [
        (latlon, args[2], args[3], args[4], args[5], healpix.shape),
        (healpix, args[6], args[7], args[8], args[9], latlon.shape),
    ]
    bits = devices.bit_length() - 1
    tiles = max(latlon.shape[2], healpix.shape[2]) // LANES
    size = devices * tiles * round_up(latlon.shape[1], 8) * LANES * 4
    if devices == 1 << bits and bits > 2 and size <= ACC_LIMIT:
        return tuple(bit_remaps(remaps, bits))
    return tuple(slot_remap(*remap) for remap in remaps)


def solution(mesh):
    in_specs = (
        P("groups", None, "curve"),
        P("groups", None, "curve"),
        P("curve", None, None),
        P("curve"),
        P("curve"),
        P("curve", None),
        P("curve", None, None),
        P("curve"),
        P("curve"),
        P("curve", None),
    )
    out_specs = (P("groups", None, "curve"), P("groups", None, "curve"))
    return jax.shard_map(
        functools.partial(on_device, mesh.shape["curve"]),
        mesh=mesh, in_specs=in_specs, out_specs=out_specs, check_vma=False,
    )
```

```python
import functools

import jax
import jax.numpy as jnp
from jax import lax
from jax.experimental import pallas as pl
from jax.experimental.pallas import tpu as pltpu
from jax.sharding import PartitionSpec as P

LANES = 128
ACC_LIMIT = 16 * 1024 * 1024


def round_up(value, unit):
    return -(-value // unit) * unit


def block_products(cotangent, weights, source):
    width = weights.shape[1]
    lead = cotangent.shape[0] * cotangent.shape[1]
    tiled = cotangent.reshape(lead, cotangent.shape[2] // width, width)
    picked = jnp.take(tiled, source, axis=1)
    products = jnp.einsum("kbi,bij->bkj", picked, weights, preferred_element_type=jnp.float32)
    return products.astype(jnp.bfloat16)


def pack_slots(products, target, count_row):
    blocks = products.shape[0]
    devices = count_row.shape[0]
    per_device = 2 * blocks // devices
    inclusive = jnp.cumsum(count_row)
    exclusive = inclusive - count_row
    positions = jnp.arange(blocks, dtype=jnp.int32)
    owner = jnp.sum((positions[:, None] >= inclusive[None, :]).astype(jnp.int32), axis=1)
    chosen = owner[:, None] == jnp.arange(devices, dtype=jnp.int32)[None, :]
    first = jnp.sum(jnp.where(chosen, exclusive[None, :], 0), axis=1)
    slot_index = owner * per_device + positions - first
    buffer = (
        jnp.zeros((devices * per_device,) + products.shape[1:], jnp.bfloat16)
        .at[slot_index]
        .set(products)
    )
    labels = jnp.full((devices * per_device,), -1, jnp.int32).at[slot_index].set(target)
    return (buffer, labels)


def sum_slots(received, labels, tiles_out, like_shape):
    selector = (labels[None, :] == jnp.arange(tiles_out, dtype=jnp.int32)[:, None]).astype(
        jnp.bfloat16
    )
    summed = jnp.einsum("ts,skc->ktc", selector, received, preferred_element_type=jnp.float32)
    return summed.reshape(like_shape[0], like_shape[1], -1).astype(jnp.bfloat16)


def slot_remap(cotangent, weights, source, target, counts, like_shape):
    products = block_products(cotangent, weights, source)
    buffer, labels = pack_slots(products, target, counts[0])
    arrived = lax.all_to_all(buffer, "curve", split_axis=0, concat_axis=0, tiled=True)
    arrived_labels = lax.all_to_all(labels, "curve", split_axis=0, concat_axis=0, tiled=True)
    return sum_slots(arrived, arrived_labels, like_shape[2] // weights.shape[1], like_shape)


def slots_of(stages):
    return [[sum(((m >> i) & 1) << bit for i, bit in enumerate(stage)) for m in range(1 << len(stage))]
            for stage in stages]


def owners_in_order(stages):
    masks = [0]
    for stage in slots_of(stages):
        masks = [left + right for left in masks for right in stage]
    return masks


def product_kernel(
    bits, channels, pitch, chunks, step_blocks,
    source_hbm, target_hbm, counts_hbm, x_hbm, w_hbm, *rest,
):
    number = len(chunks)
    outs, (acc, xs, x_in, w, source, target, counts, places, sems) = rest[:4], rest[4:]
    devices = 1 << bits
    steps = w.shape[0] // step_blocks
    me = lax.axis_index("curve")

    scalars = [
        pltpu.make_async_copy(source_hbm, source, sems.at[0]),
        pltpu.make_async_copy(target_hbm, target, sems.at[1]),
        pltpu.make_async_copy(counts_hbm, counts, sems.at[2]),
    ]
    x_copy = pltpu.make_async_copy(x_hbm, x_in, sems.at[3])

    def w_copy(step):
        at = pl.ds(step * step_blocks, step_blocks)
        return pltpu.make_async_copy(w_hbm.at[at], w.at[at], sems.at[4 + step])

    for copy in scalars + [x_copy]:
        copy.start()
    for step in range(steps):
        w_copy(step).start()

    @pl.loop(0, acc.shape[0] // pitch)
    def clear(index):
        acc[pl.ds(pl.multiple_of(index * pitch, pitch), pitch), :] = jnp.zeros((pitch, LANES), jnp.float32)

    for tile in range(xs.shape[0]):
        xs[tile] = jnp.zeros(xs.shape[1:], xs.dtype)

    bases, base = [], 0
    for chunk, (low, high, stages) in enumerate(chunks):
        bases.append(base)
        order = [stages[1], stages[0]] + list(stages[2:])
        for owner in range(devices):
            differ = jnp.bitwise_xor(me, owner)
            place = jnp.int32(0)
            for stage in order:
                for bit in reversed(stage):
                    place = place * 2 + jnp.bitwise_and(jnp.right_shift(differ, bit), 1)
            places[chunk, owner] = base + place * (high - low) - low
        base += devices * (high - low)

    x_copy.wait()
    for tile in range(xs.shape[0]):
        xs[tile, :channels, :] = x_in[0, :, tile * LANES:(tile + 1) * LANES]
    for copy in scalars:
        copy.wait()

    def some(step, carry):
        owner, end = carry
        w_copy(step).wait()
        rows = []
        for index in range(step_blocks):
            block = step * step_blocks + index
            passed = (block >= end).astype(jnp.int32)
            owner = jnp.minimum(owner + passed, devices - 1)
            end = end + passed * counts[0, owner]
            tile = target[block]
            place = places[0, owner]
            for chunk in range(1, number):
                place = jnp.where(tile >= chunks[chunk][0], places[chunk, owner], place)
            rows.append(pl.multiple_of((place + tile) * pitch, 8))
        for index, row in enumerate(rows):
            block = step * step_blocks + index
            product = jnp.dot(xs[source[block], :pitch, :], w[block], preferred_element_type=jnp.float32)
            acc[pl.ds(row, pitch), :] += product
        return owner, end

    lax.fori_loop(0, steps, some, (jnp.int32(0), counts[0, 0]))

    for base, (low, high, stages) in zip(bases, chunks):
        unit = (high - low) * pitch
        quarter = devices // 4

        @pl.loop(0, quarter)
        def finish(index):
            at = pl.multiple_of(quarter * low * pitch + index * unit, 8)
            for part, ref in enumerate(outs):
                row = pl.multiple_of((base + part * quarter * (high - low)) * pitch + index * unit, 8)
                ref[pl.ds(at, unit), :] = acc[pl.ds(row, unit), :].astype(ref.dtype)


def products(remap, chunks, bits):
    cotangent, weights, source, target, counts = remap[:5]
    devices = 1 << bits
    channels = cotangent.shape[1]
    pitch = round_up(channels, 8)
    tiles_in = cotangent.shape[2] // LANES
    blocks = weights.shape[0]
    step_blocks = max(size for size in range(1, 17) if blocks % size == 0)
    rows = devices // 4 * chunks[-1][1] * pitch
    return pl.pallas_call(
        functools.partial(product_kernel, bits, channels, pitch, chunks, step_blocks),
        out_shape=[jax.ShapeDtypeStruct((rows, LANES), kind) for kind in (jnp.float32, jnp.bfloat16) * 2],
        in_specs=[pl.BlockSpec(memory_space=pltpu.HBM)] * 5,
        out_specs=[pl.BlockSpec(memory_space=pltpu.VMEM)] * 4,
        scratch_shapes=[
            pltpu.VMEM((rows * 4, LANES), jnp.float32),
            pltpu.VMEM((tiles_in, round_up(pitch, 16), LANES), jnp.bfloat16),
            pltpu.VMEM(cotangent.shape, jnp.bfloat16),
            pltpu.VMEM(weights.shape, jnp.bfloat16),
            pltpu.SMEM(source.shape, jnp.int32),
            pltpu.SMEM(target.shape, jnp.int32),
            pltpu.SMEM(counts.shape, jnp.int32),
            pltpu.SMEM((len(chunks), devices), jnp.int32),
            pltpu.SemaphoreType.DMA((4 + blocks // step_blocks,)),
        ],
        compiler_params=pltpu.CompilerParams(vmem_limit_bytes=28 * 1024 * 1024),
        cost_estimate=pl.CostEstimate(
            flops=2 * blocks * channels * LANES * LANES,
            bytes_accessed=2 * weights.size + 12 * rows * LANES,
            transcendentals=0,
        ),
    )(*[pltpu.with_memory_space_constraint(value, pltpu.HBM) for value in (source, target, counts, cotangent, weights)])


def exchange(value, mask, devices):
    return lax.ppermute(value, "curve", [(at, at ^ mask) for at in range(devices)])


def added(terms, low, high):
    return sum(term[low:high].astype(jnp.float32) for term in terms)


class Chain:
    def __init__(self, chunk, bits, pitch):
        self.chunk, self.devices = chunk, 1 << bits
        self.slots = slots_of(chunk[2])
        self.stage = 2
        self.base = self.devices // 4 * chunk[0] * pitch
        self.length = self.devices // 4 * (chunk[1] - chunk[0]) * pitch

    def first(self, terms):
        self.total = added(terms, self.base, self.base + self.length).astype(jnp.bfloat16)

    def second(self):
        self.got = [exchange(self.total, self.slots[1][1], self.devices)]

    def rest(self, terms):
        self.terms = [(term, self.base) for term in terms]

    def part(self, place):
        at = place * self.length
        return sum(term[base + at:base + at + self.length].astype(jnp.float32) for term, base in self.terms)

    def send_next(self):
        self.terms = self.terms + [(got, 0) for got in self.got]
        masks = self.slots[self.stage]
        self.length //= len(masks)
        self.sent = [self.part(place).astype(jnp.bfloat16) for place in range(1, len(masks))]
        self.got = [exchange(sent, mask, self.devices) for sent, mask in zip(self.sent, masks[1:])]
        self.stage += 1

    def finish(self):
        self.terms = self.terms + [(got, 0) for got in self.got]
        self.sent = ()


def final_kernel(channels, pitch, parts, *refs):
    out = refs[-1]
    at = 0
    for low, high, count in parts:
        terms = refs[at:at + count]
        at += count
        for tile in range(high - low):
            total = sum(
                term[tile * pitch:(tile + 1) * pitch, :].astype(jnp.float32) for term in terms
            )
            lane = (low + tile) * LANES
            out[0, :, lane:lane + LANES] = total[:channels].astype(jnp.bfloat16)


def final_sum(chains, like_shape, pitch):
    parts = [(chain.chunk[0], chain.chunk[1], len(chain.terms)) for chain in chains]
    flat, specs = [], []
    for chain in chains:
        rows = (chain.chunk[1] - chain.chunk[0]) * pitch
        for term, base in chain.terms:
            flat.append(term if base % rows == 0 else term[base:base + rows])
            at = base // rows if base % rows == 0 else 0
            specs.append(pl.BlockSpec((rows, LANES), lambda step, at=at: (at, 0)))
    return pl.pallas_call(
        functools.partial(final_kernel, like_shape[1], pitch, parts),
        out_shape=jax.ShapeDtypeStruct(like_shape, jnp.bfloat16),
        grid=(1,),
        in_specs=specs,
        out_specs=pl.BlockSpec(like_shape, lambda step: (0, 0, 0)),
        compiler_params=pltpu.CompilerParams(vmem_limit_bytes=28 * 1024 * 1024),
    )(*flat)


def plan(tiles):
    straight = ((0,), (1,), (2,), (3,))
    turned = ((0,), (2,), (3,), (1,))
    half, some, most = tiles // 2, tiles * 5 // 12, tiles * 3 // 4
    return (
        [(0, half, straight), (half, tiles, turned)],
        [(0, some, straight), (some, most, straight), (most, tiles, straight)],
    )


class Order:
    def __init__(self):
        self.last = ()

    def after(self, values):
        values, unused = lax.optimization_barrier((values, self.last))
        return values

    def before(self, values):
        self.last = values


def bit_remaps(remaps, bits):
    one, two = remaps
    devices = 1 << bits
    pitch = round_up(one[-1][1], 8)
    plans = plan(one[-1][2] // LANES)
    ones, twos = [[Chain(chunk, bits, pitch) for chunk in chunks] for chunks in plans]
    order = Order()

    def step(*chains):
        gots = order.after([chain.got for chain in chains])
        for chain, got in zip(chains, gots):
            chain.got = got
            if chain.stage < len(chain.slots):
                chain.send_next()
            else:
                chain.finish()
        order.before([chain.sent for chain in chains])

    def summed(line, terms):
        terms = order.after(terms)
        for chain in line:
            chain.first(terms)
        order.before([chain.total for chain in line])

    def both_cores(keep, send):
        return [keep, exchange(send, 1, devices)]

    def tied(first, second):
        return lax.optimization_barrier((first, second))

    made = products(one, plans[0], bits)
    cotangent, made = tied(two[0], made)
    keep, send, keep_on, send_on = made
    on = both_cores(keep_on, send_on)
    rest = both_cores(keep, send)
    keep, send, keep_on, send_on = products((cotangent,) + two[1:], plans[1], bits)
    order.before(keep)
    late_on = both_cores(keep_on, send_on)
    late = both_cores(keep, send)
    across, turned = ones
    early, middle, last = twos

    summed(ones, on)
    for chain in ones:
        chain.second()
    rest = order.after(rest)
    order.before(rest)
    for chain in ones:
        chain.rest(rest)
    summed(twos, late_on)
    early.second()
    late = order.after(late)
    order.before(late)
    for chain in twos:
        chain.rest(late)
    step(across)
    step(turned)
    middle.total = order.after(middle.total)
    middle.second()
    step(across)
    step(early)
    last.total = order.after(last.total)
    last.second()
    step(middle)
    step(turned)
    step(early)
    step(across)
    step(last)
    step(middle)
    step(last)
    step(turned)
    step(*twos)
    return [final_sum(line, remap[-1], pitch) for line, remap in zip((ones, twos), remaps)]


def on_device(devices, *args):
    latlon, healpix = args[:2]
    remaps = [
        (latlon, args[2], args[3], args[4], args[5], healpix.shape),
        (healpix, args[6], args[7], args[8], args[9], latlon.shape),
    ]
    bits = devices.bit_length() - 1
    tiles = max(latlon.shape[2], healpix.shape[2]) // LANES
    size = devices * tiles * round_up(latlon.shape[1], 8) * LANES * 4
    if devices == 1 << bits and bits == 4 and size <= ACC_LIMIT:
        return tuple(bit_remaps(remaps, bits))
    return tuple(slot_remap(*remap) for remap in remaps)


def solution(mesh):
    in_specs = (
        P("groups", None, "curve"),
        P("groups", None, "curve"),
        P("curve", None, None),
        P("curve"),
        P("curve"),
        P("curve", None),
        P("curve", None, None),
        P("curve"),
        P("curve"),
        P("curve", None),
    )
    out_specs = (P("groups", None, "curve"), P("groups", None, "curve"))
    return jax.shard_map(
        functools.partial(on_device, mesh.shape["curve"]),
        mesh=mesh, in_specs=in_specs, out_specs=out_specs, check_vma=False,
    )
```

```python
import functools

import jax
import jax.numpy as jnp
from jax import lax
from jax.experimental import pallas as pl
from jax.experimental.pallas import tpu as pltpu
from jax.sharding import PartitionSpec as P

LANES = 128
ACC_LIMIT = 16 * 1024 * 1024


def round_up(value, unit):
    return -(-value // unit) * unit


def block_products(cotangent, weights, source):
    width = weights.shape[1]
    lead = cotangent.shape[0] * cotangent.shape[1]
    tiled = cotangent.reshape(lead, cotangent.shape[2] // width, width)
    picked = jnp.take(tiled, source, axis=1)
    products = jnp.einsum("kbi,bij->bkj", picked, weights, preferred_element_type=jnp.float32)
    return products.astype(jnp.bfloat16)


def pack_slots(products, target, count_row):
    blocks = products.shape[0]
    devices = count_row.shape[0]
    per_device = 2 * blocks // devices
    inclusive = jnp.cumsum(count_row)
    exclusive = inclusive - count_row
    positions = jnp.arange(blocks, dtype=jnp.int32)
    owner = jnp.sum((positions[:, None] >= inclusive[None, :]).astype(jnp.int32), axis=1)
    chosen = owner[:, None] == jnp.arange(devices, dtype=jnp.int32)[None, :]
    first = jnp.sum(jnp.where(chosen, exclusive[None, :], 0), axis=1)
    slot_index = owner * per_device + positions - first
    buffer = (
        jnp.zeros((devices * per_device,) + products.shape[1:], jnp.bfloat16)
        .at[slot_index]
        .set(products)
    )
    labels = jnp.full((devices * per_device,), -1, jnp.int32).at[slot_index].set(target)
    return (buffer, labels)


def sum_slots(received, labels, tiles_out, like_shape):
    selector = (labels[None, :] == jnp.arange(tiles_out, dtype=jnp.int32)[:, None]).astype(
        jnp.bfloat16
    )
    summed = jnp.einsum("ts,skc->ktc", selector, received, preferred_element_type=jnp.float32)
    return summed.reshape(like_shape[0], like_shape[1], -1).astype(jnp.bfloat16)


def slot_remap(cotangent, weights, source, target, counts, like_shape):
    products = block_products(cotangent, weights, source)
    buffer, labels = pack_slots(products, target, counts[0])
    arrived = lax.all_to_all(buffer, "curve", split_axis=0, concat_axis=0, tiled=True)
    arrived_labels = lax.all_to_all(labels, "curve", split_axis=0, concat_axis=0, tiled=True)
    return sum_slots(arrived, arrived_labels, like_shape[2] // weights.shape[1], like_shape)


EVEN = (0, 1, 2, 3)
ODD = (0, 2, 1, 3)


def product_kernel(
    channels, pitch, chunks, step_blocks,
    source_hbm, target_hbm, counts_hbm, x_hbm, w_hbm, *rest,
):
    number = len(chunks)
    outs, (acc, xs, x_in, w, source, target, counts, places, sems) = rest[:4], rest[4:]
    devices = counts.shape[1]
    steps = w.shape[0] // step_blocks
    me = lax.axis_index("curve")

    scalars = [
        pltpu.make_async_copy(source_hbm, source, sems.at[0]),
        pltpu.make_async_copy(target_hbm, target, sems.at[1]),
        pltpu.make_async_copy(counts_hbm, counts, sems.at[2]),
    ]
    x_copy = pltpu.make_async_copy(x_hbm, x_in, sems.at[3])

    def w_copy(step):
        at = pl.ds(step * step_blocks, step_blocks)
        return pltpu.make_async_copy(w_hbm.at[at], w.at[at], sems.at[4 + step])

    for copy in scalars + [x_copy]:
        copy.start()
    for step in range(steps):
        w_copy(step).start()

    @pl.loop(0, acc.shape[0] // pitch)
    def clear(index):
        acc[pl.ds(pl.multiple_of(index * pitch, pitch), pitch), :] = jnp.zeros((pitch, LANES), jnp.float32)

    for tile in range(xs.shape[0]):
        xs[tile] = jnp.zeros(xs.shape[1:], xs.dtype)

    for owner in range(devices):
        differ = jnp.bitwise_xor(me, owner)
        first, second, *others = ODD if owner % 2 else EVEN
        place = jnp.int32(0)
        for bit in [second, first] + others:
            place = place * 2 + jnp.bitwise_and(jnp.right_shift(differ, bit), 1)
        for chunk, (low, high) in enumerate(chunks):
            places[chunk, owner] = devices * low + place * (high - low) - low

    x_copy.wait()
    for tile in range(xs.shape[0]):
        xs[tile, :channels, :] = x_in[0, :, tile * LANES:(tile + 1) * LANES]
    for copy in scalars:
        copy.wait()

    def some(step, carry):
        owner, end = carry
        w_copy(step).wait()
        rows = []
        for index in range(step_blocks):
            block = step * step_blocks + index
            passed = (block >= end).astype(jnp.int32)
            owner = jnp.minimum(owner + passed, devices - 1)
            end = end + passed * counts[0, owner]
            tile = target[block]
            place = places[0, owner]
            for chunk in range(1, number):
                place = jnp.where(tile >= chunks[chunk][0], places[chunk, owner], place)
            rows.append(pl.multiple_of((place + tile) * pitch, 8))
        for index, row in enumerate(rows):
            block = step * step_blocks + index
            product = jnp.dot(xs[source[block], :pitch, :], w[block], preferred_element_type=jnp.float32)
            acc[pl.ds(row, pitch), :] += product
        return owner, end

    lax.fori_loop(0, steps, some, (jnp.int32(0), counts[0, 0]))

    quarter = devices // 4
    for low, high in chunks:
        unit = (high - low) * pitch

        @pl.loop(0, quarter)
        def finish(index):
            at = pl.multiple_of(quarter * low * pitch + index * unit, 8)
            for part, ref in enumerate(outs):
                row = pl.multiple_of((devices * low + part * quarter * (high - low)) * pitch + index * unit, 8)
                ref[pl.ds(at, unit), :] = acc[pl.ds(row, unit), :].astype(ref.dtype)


def products(remap, chunks, devices):
    cotangent, weights, source, target, counts = remap[:5]
    channels = cotangent.shape[1]
    pitch = round_up(channels, 8)
    tiles_in = cotangent.shape[2] // LANES
    blocks = weights.shape[0]
    step_blocks = max(size for size in range(1, 17) if blocks % size == 0)
    rows = devices // 4 * chunks[-1][1] * pitch
    return pl.pallas_call(
        functools.partial(product_kernel, channels, pitch, chunks, step_blocks),
        out_shape=[jax.ShapeDtypeStruct((rows, LANES), kind) for kind in (jnp.float32, jnp.bfloat16) * 2],
        in_specs=[pl.BlockSpec(memory_space=pltpu.HBM)] * 5,
        out_specs=[pl.BlockSpec(memory_space=pltpu.VMEM)] * 4,
        scratch_shapes=[
            pltpu.VMEM((rows * 4, LANES), jnp.float32),
            pltpu.VMEM((tiles_in, round_up(pitch, 16), LANES), jnp.bfloat16),
            pltpu.VMEM(cotangent.shape, jnp.bfloat16),
            pltpu.VMEM(weights.shape, jnp.bfloat16),
            pltpu.SMEM(source.shape, jnp.int32),
            pltpu.SMEM(target.shape, jnp.int32),
            pltpu.SMEM(counts.shape, jnp.int32),
            pltpu.SMEM((len(chunks), devices), jnp.int32),
            pltpu.SemaphoreType.DMA((4 + blocks // step_blocks,)),
        ],
        compiler_params=pltpu.CompilerParams(vmem_limit_bytes=28 * 1024 * 1024),
        cost_estimate=pl.CostEstimate(
            flops=2 * blocks * channels * LANES * LANES,
            bytes_accessed=2 * weights.size + 12 * rows * LANES,
            transcendentals=0,
        ),
    )(*[pltpu.with_memory_space_constraint(value, pltpu.HBM) for value in (source, target, counts, cotangent, weights)])


def exchange(value, stage, devices):
    pairs = [(at, at ^ (1 << (ODD if at % 2 else EVEN)[stage])) for at in range(devices)]
    return lax.ppermute(value, "curve", pairs)


def added(terms, low, high):
    return sum(term[low:high].astype(jnp.float32) for term in terms)


class Chain:
    def __init__(self, chunk, devices, pitch):
        self.chunk, self.devices = chunk, devices
        self.base = devices // 4 * chunk[0] * pitch
        self.length = devices // 4 * (chunk[1] - chunk[0]) * pitch

    def first(self, terms):
        self.total = added(terms, self.base, self.base + self.length).astype(jnp.bfloat16)

    def second(self):
        self.stage = 1
        self.got = exchange(self.total, self.stage, self.devices)

    def rest(self, terms):
        self.terms = [(term, self.base) for term in terms]

    def send_next(self):
        self.terms = self.terms + [(self.got, 0)]
        self.stage += 1
        self.total = self.got
        if self.stage < len(EVEN):
            half = self.length // 2
            self.total = sum(
                term[base + half:base + self.length].astype(jnp.float32) for term, base in self.terms
            ).astype(jnp.bfloat16)
            self.length = half
            self.got = exchange(self.total, self.stage, self.devices)


def final_kernel(channels, pitch, parts, *refs):
    out = refs[-1]
    at = 0
    for low, high, count in parts:
        terms = refs[at:at + count]
        at += count
        for tile in range(high - low):
            total = sum(
                term[tile * pitch:(tile + 1) * pitch, :].astype(jnp.float32) for term in terms
            )
            lane = (low + tile) * LANES
            out[0, :, lane:lane + LANES] = total[:channels].astype(jnp.bfloat16)


def final_sum(chains, like_shape, pitch):
    parts = [(chain.chunk[0], chain.chunk[1], len(chain.terms)) for chain in chains]
    flat, specs = [], []
    for chain in chains:
        rows = (chain.chunk[1] - chain.chunk[0]) * pitch
        for term, base in chain.terms:
            flat.append(term if base % rows == 0 else term[base:base + rows])
            at = base // rows if base % rows == 0 else 0
            specs.append(pl.BlockSpec((rows, LANES), lambda step, at=at: (at, 0)))
    return pl.pallas_call(
        functools.partial(final_kernel, like_shape[1], pitch, parts),
        out_shape=jax.ShapeDtypeStruct(like_shape, jnp.bfloat16),
        grid=(1,),
        in_specs=specs,
        out_specs=pl.BlockSpec(like_shape, lambda step: (0, 0, 0)),
        compiler_params=pltpu.CompilerParams(vmem_limit_bytes=28 * 1024 * 1024),
    )(*flat)


class Order:
    def __init__(self):
        self.last = ()

    def after(self, values):
        values, unused = lax.optimization_barrier((values, self.last))
        return values

    def before(self, values):
        self.last = values


def bit_remaps(remaps, devices):
    one, two = remaps
    pitch = round_up(one[-1][1], 8)
    tiles = one[-1][2] // LANES
    plans = (
        [(0, tiles // 2), (tiles // 2, tiles)],
        [(0, tiles // 2), (tiles // 2, tiles * 5 // 6), (tiles * 5 // 6, tiles)],
    )
    ones, twos = [[Chain(chunk, devices, pitch) for chunk in chunks] for chunks in plans]
    order = Order()

    def step(*chains):
        gots = order.after([chain.got for chain in chains])
        for chain, got in zip(chains, gots):
            chain.got = got
            chain.send_next()
        order.before([chain.total for chain in chains])

    def summed(line, terms):
        terms = order.after(terms)
        for chain in line:
            chain.first(terms)
        order.before([chain.total for chain in line])

    def rested(line, terms):
        terms = order.after(terms)
        order.before(terms)
        for chain in line:
            chain.rest(terms)

    def begun(chain):
        chain.total = order.after(chain.total)
        chain.second()

    def both_cores(keep, send):
        return [keep, exchange(send, 0, devices)]

    made = products(one, plans[0], devices)
    cotangent, made = lax.optimization_barrier((two[0], made))
    keep, send, keep_on, send_on = made
    on = both_cores(keep_on, send_on)
    rest = both_cores(keep, send)
    keep, send, keep_on, send_on = products((cotangent,) + two[1:], plans[1], devices)
    order.before(keep)
    late_on = both_cores(keep_on, send_on)
    late = both_cores(keep, send)
    a, b = ones
    c, d, e = twos

    summed(ones, on)
    a.second()
    b.second()
    rested(ones, rest)
    summed(twos, late_on)
    c.second()
    rested(twos, late)
    step(a)
    step(b)
    begun(d)
    step(c)
    step(a)
    begun(e)
    step(b)
    step(d)
    step(c)
    step(a)
    step(e)
    step(d)
    step(b)
    step(e)
    step(*twos)
    return [final_sum(line, remap[-1], pitch) for line, remap in zip((ones, twos), remaps)]


def on_device(devices, *args):
    latlon, healpix = args[:2]
    remaps = [
        (latlon, args[2], args[3], args[4], args[5], healpix.shape),
        (healpix, args[6], args[7], args[8], args[9], latlon.shape),
    ]
    tiles = max(latlon.shape[2], healpix.shape[2]) // LANES
    size = devices * tiles * round_up(latlon.shape[1], 8) * LANES * 4
    if devices == 1 << len(EVEN) and size <= ACC_LIMIT:
        return tuple(bit_remaps(remaps, devices))
    return tuple(slot_remap(*remap) for remap in remaps)


def solution(mesh):
    in_specs = (
        P("groups", None, "curve"),
        P("groups", None, "curve"),
        P("curve", None, None),
        P("curve"),
        P("curve"),
        P("curve", None),
        P("curve", None, None),
        P("curve"),
        P("curve"),
        P("curve", None),
    )
    out_specs = (P("groups", None, "curve"), P("groups", None, "curve"))
    return jax.shard_map(
        functools.partial(on_device, mesh.shape["curve"]),
        mesh=mesh, in_specs=in_specs, out_specs=out_specs, check_vma=False,
    )
```

```python
import functools

import jax
import jax.numpy as jnp
from jax import lax
from jax.experimental import pallas as pl
from jax.experimental.pallas import tpu as pltpu
from jax.sharding import PartitionSpec as P

LANES = 128
ACC_LIMIT = 16 * 1024 * 1024


def round_up(value, unit):
    return -(-value // unit) * unit


def block_products(cotangent, weights, source):
    width = weights.shape[1]
    lead = cotangent.shape[0] * cotangent.shape[1]
    tiled = cotangent.reshape(lead, cotangent.shape[2] // width, width)
    picked = jnp.take(tiled, source, axis=1)
    products = jnp.einsum("kbi,bij->bkj", picked, weights, preferred_element_type=jnp.float32)
    return products.astype(jnp.bfloat16)


def pack_slots(products, target, count_row):
    blocks = products.shape[0]
    devices = count_row.shape[0]
    per_device = 2 * blocks // devices
    inclusive = jnp.cumsum(count_row)
    exclusive = inclusive - count_row
    positions = jnp.arange(blocks, dtype=jnp.int32)
    owner = jnp.sum((positions[:, None] >= inclusive[None, :]).astype(jnp.int32), axis=1)
    chosen = owner[:, None] == jnp.arange(devices, dtype=jnp.int32)[None, :]
    first = jnp.sum(jnp.where(chosen, exclusive[None, :], 0), axis=1)
    slot_index = owner * per_device + positions - first
    buffer = (
        jnp.zeros((devices * per_device,) + products.shape[1:], jnp.bfloat16)
        .at[slot_index]
        .set(products)
    )
    labels = jnp.full((devices * per_device,), -1, jnp.int32).at[slot_index].set(target)
    return (buffer, labels)


def sum_slots(received, labels, tiles_out, like_shape):
    selector = (labels[None, :] == jnp.arange(tiles_out, dtype=jnp.int32)[:, None]).astype(
        jnp.bfloat16
    )
    summed = jnp.einsum("ts,skc->ktc", selector, received, preferred_element_type=jnp.float32)
    return summed.reshape(like_shape[0], like_shape[1], -1).astype(jnp.bfloat16)


def slot_remap(cotangent, weights, source, target, counts, like_shape):
    products = block_products(cotangent, weights, source)
    buffer, labels = pack_slots(products, target, counts[0])
    arrived = lax.all_to_all(buffer, "curve", split_axis=0, concat_axis=0, tiled=True)
    arrived_labels = lax.all_to_all(labels, "curve", split_axis=0, concat_axis=0, tiled=True)
    return sum_slots(arrived, arrived_labels, like_shape[2] // weights.shape[1], like_shape)


STRAIGHT = ((0, 1, 2, 3), (0, 1, 2, 3))
MIXED = ((0, 1, 2, 3), (0, 2, 1, 3))
BITS = 4


def product_kernel(
    channels, pitch, chunks, step_blocks,
    source_hbm, target_hbm, counts_hbm, x_hbm, w_hbm, *rest,
):
    number = len(chunks)
    outs, (acc, xs, x_in, w, source, target, counts, places, sems) = rest[:4], rest[4:]
    devices = counts.shape[1]
    steps = w.shape[0] // step_blocks
    me = lax.axis_index("curve")

    scalars = [
        pltpu.make_async_copy(source_hbm, source, sems.at[0]),
        pltpu.make_async_copy(target_hbm, target, sems.at[1]),
        pltpu.make_async_copy(counts_hbm, counts, sems.at[2]),
    ]
    x_copy = pltpu.make_async_copy(x_hbm, x_in, sems.at[3])

    def w_copy(step):
        at = pl.ds(step * step_blocks, step_blocks)
        return pltpu.make_async_copy(w_hbm.at[at], w.at[at], sems.at[4 + step])

    for copy in scalars + [x_copy]:
        copy.start()
    for step in range(steps):
        w_copy(step).start()

    @pl.loop(0, acc.shape[0] // pitch)
    def clear(index):
        acc[pl.ds(pl.multiple_of(index * pitch, pitch), pitch), :] = jnp.zeros((pitch, LANES), jnp.float32)

    for tile in range(xs.shape[0]):
        xs[tile] = jnp.zeros(xs.shape[1:], xs.dtype)

    for owner in range(devices):
        differ = jnp.bitwise_xor(me, owner)
        found = {}
        for chunk, (low, high, way) in enumerate(chunks):
            first, second, *others = way[owner % 2]
            key = (second, first, *others)
            if key not in found:
                place = jnp.int32(0)
                for bit in key:
                    place = place * 2 + jnp.bitwise_and(jnp.right_shift(differ, bit), 1)
                found[key] = place
            places[chunk, owner] = devices * low + found[key] * (high - low) - low

    x_copy.wait()
    for tile in range(xs.shape[0]):
        xs[tile, :channels, :] = x_in[0, :, tile * LANES:(tile + 1) * LANES]
    for copy in scalars:
        copy.wait()

    def some(step, carry):
        owner, end = carry
        w_copy(step).wait()
        rows = []
        for index in range(step_blocks):
            block = step * step_blocks + index
            passed = (block >= end).astype(jnp.int32)
            owner = jnp.minimum(owner + passed, devices - 1)
            end = end + passed * counts[0, owner]
            tile = target[block]
            place = places[0, owner]
            for chunk in range(1, number):
                place = jnp.where(tile >= chunks[chunk][0], places[chunk, owner], place)
            rows.append(pl.multiple_of((place + tile) * pitch, 8))
        for index, row in enumerate(rows):
            block = step * step_blocks + index
            product = jnp.dot(xs[source[block], :pitch, :], w[block], preferred_element_type=jnp.float32)
            acc[pl.ds(row, pitch), :] += product
        return owner, end

    lax.fori_loop(0, steps, some, (jnp.int32(0), counts[0, 0]))

    quarter = devices // 4
    for low, high, way in chunks:
        unit = (high - low) * pitch

        @pl.loop(0, quarter)
        def finish(index):
            at = pl.multiple_of(quarter * low * pitch + index * unit, 8)
            for part, ref in enumerate(outs):
                row = pl.multiple_of((devices * low + part * quarter * (high - low)) * pitch + index * unit, 8)
                ref[pl.ds(at, unit), :] = acc[pl.ds(row, unit), :].astype(ref.dtype)


def products(remap, chunks, devices):
    cotangent, weights, source, target, counts = remap[:5]
    channels = cotangent.shape[1]
    pitch = round_up(channels, 8)
    tiles_in = cotangent.shape[2] // LANES
    blocks = weights.shape[0]
    step_blocks = max(size for size in range(1, 17) if blocks % size == 0)
    rows = devices // 4 * chunks[-1][1] * pitch
    return pl.pallas_call(
        functools.partial(product_kernel, channels, pitch, chunks, step_blocks),
        out_shape=[jax.ShapeDtypeStruct((rows, LANES), kind) for kind in (jnp.float32, jnp.bfloat16) * 2],
        in_specs=[pl.BlockSpec(memory_space=pltpu.HBM)] * 5,
        out_specs=[pl.BlockSpec(memory_space=pltpu.VMEM)] * 4,
        scratch_shapes=[
            pltpu.VMEM((rows * 4, LANES), jnp.float32),
            pltpu.VMEM((tiles_in, round_up(pitch, 16), LANES), jnp.bfloat16),
            pltpu.VMEM(cotangent.shape, jnp.bfloat16),
            pltpu.VMEM(weights.shape, jnp.bfloat16),
            pltpu.SMEM(source.shape, jnp.int32),
            pltpu.SMEM(target.shape, jnp.int32),
            pltpu.SMEM(counts.shape, jnp.int32),
            pltpu.SMEM((len(chunks), devices), jnp.int32),
            pltpu.SemaphoreType.DMA((4 + blocks // step_blocks,)),
        ],
        compiler_params=pltpu.CompilerParams(vmem_limit_bytes=28 * 1024 * 1024),
        cost_estimate=pl.CostEstimate(
            flops=2 * blocks * channels * LANES * LANES,
            bytes_accessed=2 * weights.size + 12 * rows * LANES,
            transcendentals=0,
        ),
    )(*[pltpu.with_memory_space_constraint(value, pltpu.HBM) for value in (source, target, counts, cotangent, weights)])


def exchange(value, way, stage, devices):
    pairs = [(at, at ^ (1 << way[at % 2][stage])) for at in range(devices)]
    return lax.ppermute(value, "curve", pairs)


def added(terms, low, high):
    return sum(term[low:high].astype(jnp.float32) for term in terms)


class Chain:
    def __init__(self, chunk, devices, pitch):
        self.chunk, self.devices = chunk, devices
        self.way = chunk[2]
        self.base = devices // 4 * chunk[0] * pitch
        self.length = devices // 4 * (chunk[1] - chunk[0]) * pitch

    def first(self, terms):
        self.total = added(terms, self.base, self.base + self.length).astype(jnp.bfloat16)

    def second(self):
        self.stage = 1
        self.got = exchange(self.total, self.way, self.stage, self.devices)

    def rest(self, terms):
        self.terms = [(term, self.base) for term in terms]

    def send_next(self):
        self.terms = self.terms + [(self.got, 0)]
        self.stage += 1
        self.total = self.got
        if self.stage < BITS:
            half = self.length // 2
            self.total = sum(
                term[base + half:base + self.length].astype(jnp.float32) for term, base in self.terms
            ).astype(jnp.bfloat16)
            self.length = half
            self.got = exchange(self.total, self.way, self.stage, self.devices)


def final_kernel(channels, pitch, parts, *refs):
    out = refs[-1]
    at = 0
    for low, high, count in parts:
        terms = refs[at:at + count]
        at += count
        for tile in range(high - low):
            total = sum(
                term[tile * pitch:(tile + 1) * pitch, :].astype(jnp.float32) for term in terms
            )
            lane = (low + tile) * LANES
            out[0, :, lane:lane + LANES] = total[:channels].astype(jnp.bfloat16)


def final_sum(chains, like_shape, pitch):
    parts = [(chain.chunk[0], chain.chunk[1], len(chain.terms)) for chain in chains]
    flat, specs = [], []
    for chain in chains:
        rows = (chain.chunk[1] - chain.chunk[0]) * pitch
        for term, base in chain.terms:
            flat.append(term if base % rows == 0 else term[base:base + rows])
            at = base // rows if base % rows == 0 else 0
            specs.append(pl.BlockSpec((rows, LANES), lambda step, at=at: (at, 0)))
    return pl.pallas_call(
        functools.partial(final_kernel, like_shape[1], pitch, parts),
        out_shape=jax.ShapeDtypeStruct(like_shape, jnp.bfloat16),
        grid=(1,),
        in_specs=specs,
        out_specs=pl.BlockSpec(like_shape, lambda step: (0, 0, 0)),
        compiler_params=pltpu.CompilerParams(vmem_limit_bytes=28 * 1024 * 1024),
    )(*flat)


class Order:
    def __init__(self):
        self.last = ()

    def after(self, values):
        values, unused = lax.optimization_barrier((values, self.last))
        return values

    def before(self, values):
        self.last = values


def bit_remaps(remaps, devices):
    one, two = remaps
    pitch = round_up(one[-1][1], 8)
    tiles = one[-1][2] // LANES
    some, most = tiles * 5 // 12, tiles * 3 // 4
    plans = (
        [(0, most, MIXED), (most, tiles, MIXED)],
        [(0, some, MIXED), (some, most, STRAIGHT), (most, tiles, STRAIGHT)],
    )
    ones, twos = [[Chain(chunk, devices, pitch) for chunk in chunks] for chunks in plans]
    order = Order()

    def step(*chains):
        gots = order.after([chain.got for chain in chains])
        for chain, got in zip(chains, gots):
            chain.got = got
            chain.send_next()
        order.before([chain.total for chain in chains])

    def summed(line, terms):
        terms = order.after(terms)
        for chain in line:
            chain.first(terms)
        order.before([chain.total for chain in line])

    def rested(line, terms):
        terms = order.after(terms)
        order.before(terms)
        for chain in line:
            chain.rest(terms)

    def begun(chain):
        chain.total = order.after(chain.total)
        chain.second()

    def both_cores(keep, send):
        return [keep, exchange(send, STRAIGHT, 0, devices)]

    a, b = ones
    c, d, e = twos

    keep, send, keep_on, send_on = products(one, plans[0], devices)
    on = both_cores(keep_on, send_on)
    rest = both_cores(keep, send)
    summed(ones, on)
    a.second()
    b.second()
    rested(ones, rest)
    made = products((order.after(two[0]),) + two[1:], plans[1], devices)
    order.before(made)
    keep, send, keep_on, send_on = made
    on = both_cores(keep_on, send_on)
    rest = both_cores(keep, send)

    step(a)
    step(b)
    summed(twos, on)
    c.second()
    begun(d)
    step(a)
    step(b)
    rested(twos, rest)
    step(c)
    begun(e)
    step(d)
    step(c)
    step(e)
    step(b)
    step(d)
    step(a)
    step(e)
    step(*twos)
    return [final_sum(line, remap[-1], pitch) for line, remap in zip((ones, twos), remaps)]


def on_device(devices, *args):
    latlon, healpix = args[:2]
    remaps = [
        (latlon, args[2], args[3], args[4], args[5], healpix.shape),
        (healpix, args[6], args[7], args[8], args[9], latlon.shape),
    ]
    tiles = max(latlon.shape[2], healpix.shape[2]) // LANES
    size = devices * tiles * round_up(latlon.shape[1], 8) * LANES * 4
    if devices == 1 << BITS and size <= ACC_LIMIT:
        return tuple(bit_remaps(remaps, devices))
    return tuple(slot_remap(*remap) for remap in remaps)


def solution(mesh):
    in_specs = (
        P("groups", None, "curve"),
        P("groups", None, "curve"),
        P("curve", None, None),
        P("curve"),
        P("curve"),
        P("curve", None),
        P("curve", None, None),
        P("curve"),
        P("curve"),
        P("curve", None),
    )
    out_specs = (P("groups", None, "curve"), P("groups", None, "curve"))
    return jax.shard_map(
        functools.partial(on_device, mesh.shape["curve"]),
        mesh=mesh, in_specs=in_specs, out_specs=out_specs, check_vma=False,
    )
```

```python
import functools

import jax
import jax.numpy as jnp
from jax import lax
from jax.experimental import pallas as pl
from jax.experimental.pallas import tpu as pltpu
from jax.sharding import PartitionSpec as P

LANES = 128
ACC_LIMIT = 16 * 1024 * 1024


def round_up(value, unit):
    return -(-value // unit) * unit


def block_products(cotangent, weights, source):
    width = weights.shape[1]
    lead = cotangent.shape[0] * cotangent.shape[1]
    tiled = cotangent.reshape(lead, cotangent.shape[2] // width, width)
    picked = jnp.take(tiled, source, axis=1)
    products = jnp.einsum("kbi,bij->bkj", picked, weights, preferred_element_type=jnp.float32)
    return products.astype(jnp.bfloat16)


def pack_slots(products, target, count_row):
    blocks = products.shape[0]
    devices = count_row.shape[0]
    per_device = 2 * blocks // devices
    inclusive = jnp.cumsum(count_row)
    exclusive = inclusive - count_row
    positions = jnp.arange(blocks, dtype=jnp.int32)
    owner = jnp.sum((positions[:, None] >= inclusive[None, :]).astype(jnp.int32), axis=1)
    chosen = owner[:, None] == jnp.arange(devices, dtype=jnp.int32)[None, :]
    first = jnp.sum(jnp.where(chosen, exclusive[None, :], 0), axis=1)
    slot_index = owner * per_device + positions - first
    buffer = (
        jnp.zeros((devices * per_device,) + products.shape[1:], jnp.bfloat16)
        .at[slot_index]
        .set(products)
    )
    labels = jnp.full((devices * per_device,), -1, jnp.int32).at[slot_index].set(target)
    return (buffer, labels)


def sum_slots(received, labels, tiles_out, like_shape):
    selector = (labels[None, :] == jnp.arange(tiles_out, dtype=jnp.int32)[:, None]).astype(
        jnp.bfloat16
    )
    summed = jnp.einsum("ts,skc->ktc", selector, received, preferred_element_type=jnp.float32)
    return summed.reshape(like_shape[0], like_shape[1], -1).astype(jnp.bfloat16)


def slot_remap(cotangent, weights, source, target, counts, like_shape):
    products = block_products(cotangent, weights, source)
    buffer, labels = pack_slots(products, target, counts[0])
    arrived = lax.all_to_all(buffer, "curve", split_axis=0, concat_axis=0, tiled=True)
    arrived_labels = lax.all_to_all(labels, "curve", split_axis=0, concat_axis=0, tiled=True)
    return sum_slots(arrived, arrived_labels, like_shape[2] // weights.shape[1], like_shape)


STRAIGHT = ((0, 1, 2, 3), (0, 1, 2, 3))
MIXED = ((0, 1, 2, 3), (0, 2, 1, 3))
BITS = 4


def product_kernel(
    channels, pitch, chunks, step_blocks,
    source_hbm, target_hbm, counts_hbm, x_hbm, w_hbm, *rest,
):
    number = len(chunks)
    outs, (acc, xs, x_in, w, source, target, counts, places, sems) = rest[:4], rest[4:]
    devices = counts.shape[1]
    steps = w.shape[0] // step_blocks
    me = lax.axis_index("curve")

    scalars = [
        pltpu.make_async_copy(source_hbm, source, sems.at[0]),
        pltpu.make_async_copy(target_hbm, target, sems.at[1]),
        pltpu.make_async_copy(counts_hbm, counts, sems.at[2]),
    ]
    x_copy = pltpu.make_async_copy(x_hbm, x_in, sems.at[3])

    def w_copy(step):
        at = pl.ds(step * step_blocks, step_blocks)
        return pltpu.make_async_copy(w_hbm.at[at], w.at[at], sems.at[4 + step])

    for copy in scalars + [x_copy]:
        copy.start()
    for step in range(steps):
        w_copy(step).start()

    @pl.loop(0, acc.shape[0] // pitch)
    def clear(index):
        acc[pl.ds(pl.multiple_of(index * pitch, pitch), pitch), :] = jnp.zeros((pitch, LANES), jnp.float32)

    for tile in range(xs.shape[0]):
        xs[tile] = jnp.zeros(xs.shape[1:], xs.dtype)

    for owner in range(devices):
        differ = jnp.bitwise_xor(me, owner)
        found = {}
        for chunk, (low, high, way) in enumerate(chunks):
            first, second, *others = way[owner % 2]
            key = (second, first, *others)
            if key not in found:
                place = jnp.int32(0)
                for bit in key:
                    place = place * 2 + jnp.bitwise_and(jnp.right_shift(differ, bit), 1)
                found[key] = place
            places[chunk, owner] = devices * low + found[key] * (high - low) - low

    x_copy.wait()
    for tile in range(xs.shape[0]):
        xs[tile, :channels, :] = x_in[0, :, tile * LANES:(tile + 1) * LANES]
    for copy in scalars:
        copy.wait()

    def some(step, carry):
        owner, end = carry
        w_copy(step).wait()
        rows = []
        for index in range(step_blocks):
            block = step * step_blocks + index
            passed = (block >= end).astype(jnp.int32)
            owner = jnp.minimum(owner + passed, devices - 1)
            end = end + passed * counts[0, owner]
            tile = target[block]
            place = places[0, owner]
            for chunk in range(1, number):
                place = jnp.where(tile >= chunks[chunk][0], places[chunk, owner], place)
            rows.append(pl.multiple_of((place + tile) * pitch, 8))
        for index, row in enumerate(rows):
            block = step * step_blocks + index
            product = jnp.dot(xs[source[block], :pitch, :], w[block], preferred_element_type=jnp.float32)
            acc[pl.ds(row, pitch), :] += product
        return owner, end

    lax.fori_loop(0, steps, some, (jnp.int32(0), counts[0, 0]))

    quarter = devices // 4
    for low, high, way in chunks:
        unit = (high - low) * pitch

        @pl.loop(0, quarter)
        def finish(index):
            at = pl.multiple_of(quarter * low * pitch + index * unit, 8)
            for part, ref in enumerate(outs):
                row = pl.multiple_of((devices * low + part * quarter * (high - low)) * pitch + index * unit, 8)
                ref[pl.ds(at, unit), :] = acc[pl.ds(row, unit), :].astype(ref.dtype)


def products(remap, chunks, devices):
    cotangent, weights, source, target, counts = remap[:5]
    channels = cotangent.shape[1]
    pitch = round_up(channels, 8)
    tiles_in = cotangent.shape[2] // LANES
    blocks = weights.shape[0]
    step_blocks = max(size for size in range(1, 17) if blocks % size == 0)
    rows = devices // 4 * chunks[-1][1] * pitch
    return pl.pallas_call(
        functools.partial(product_kernel, channels, pitch, chunks, step_blocks),
        out_shape=[jax.ShapeDtypeStruct((rows, LANES), kind) for kind in (jnp.float32, jnp.bfloat16) * 2],
        in_specs=[pl.BlockSpec(memory_space=pltpu.HBM)] * 5,
        out_specs=[pl.BlockSpec(memory_space=pltpu.VMEM)] * 4,
        scratch_shapes=[
            pltpu.VMEM((rows * 4, LANES), jnp.float32),
            pltpu.VMEM((tiles_in, round_up(pitch, 16), LANES), jnp.bfloat16),
            pltpu.VMEM(cotangent.shape, jnp.bfloat16),
            pltpu.VMEM(weights.shape, jnp.bfloat16),
            pltpu.SMEM(source.shape, jnp.int32),
            pltpu.SMEM(target.shape, jnp.int32),
            pltpu.SMEM(counts.shape, jnp.int32),
            pltpu.SMEM((len(chunks), devices), jnp.int32),
            pltpu.SemaphoreType.DMA((4 + blocks // step_blocks,)),
        ],
        compiler_params=pltpu.CompilerParams(vmem_limit_bytes=28 * 1024 * 1024),
        cost_estimate=pl.CostEstimate(
            flops=2 * blocks * channels * LANES * LANES,
            bytes_accessed=2 * weights.size + 12 * rows * LANES,
            transcendentals=0,
        ),
    )(*[pltpu.with_memory_space_constraint(value, pltpu.HBM) for value in (source, target, counts, cotangent, weights)])


def exchange(value, way, stage, devices):
    pairs = [(at, at ^ (1 << way[at % 2][stage])) for at in range(devices)]
    return lax.ppermute(value, "curve", pairs)


def added(terms, low, high):
    return sum(term[low:high].astype(jnp.float32) for term in terms)


class Chain:
    def __init__(self, chunk, devices, pitch):
        self.chunk, self.devices = chunk, devices
        self.way = chunk[2]
        self.base = devices // 4 * chunk[0] * pitch
        self.length = devices // 4 * (chunk[1] - chunk[0]) * pitch

    def first(self, terms):
        self.total = added(terms, self.base, self.base + self.length).astype(jnp.bfloat16)

    def second(self):
        self.stage = 1
        self.got = exchange(self.total, self.way, self.stage, self.devices)

    def rest(self, terms):
        self.terms = [(term, self.base) for term in terms]

    def send_next(self):
        self.terms = self.terms + [(self.got, 0)]
        self.stage += 1
        self.total = self.got
        if self.stage < BITS:
            half = self.length // 2
            self.total = sum(
                term[base + half:base + self.length].astype(jnp.float32) for term, base in self.terms
            ).astype(jnp.bfloat16)
            self.length = half
            self.got = exchange(self.total, self.way, self.stage, self.devices)


def final_kernel(channels, pitch, parts, *refs):
    out = refs[-1]
    at = 0
    for low, high, count in parts:
        terms = refs[at:at + count]
        at += count
        for tile in range(high - low):
            total = sum(
                term[tile * pitch:(tile + 1) * pitch, :].astype(jnp.float32) for term in terms
            )
            lane = (low + tile) * LANES
            out[0, :, lane:lane + LANES] = total[:channels].astype(jnp.bfloat16)


def final_sum(chains, like_shape, pitch):
    parts = [(chain.chunk[0], chain.chunk[1], len(chain.terms)) for chain in chains]
    flat, specs = [], []
    for chain in chains:
        rows = (chain.chunk[1] - chain.chunk[0]) * pitch
        for term, base in chain.terms:
            flat.append(term if base % rows == 0 else term[base:base + rows])
            at = base // rows if base % rows == 0 else 0
            specs.append(pl.BlockSpec((rows, LANES), lambda step, at=at: (at, 0)))
    return pl.pallas_call(
        functools.partial(final_kernel, like_shape[1], pitch, parts),
        out_shape=jax.ShapeDtypeStruct(like_shape, jnp.bfloat16),
        grid=(1,),
        in_specs=specs,
        out_specs=pl.BlockSpec(like_shape, lambda step: (0, 0, 0)),
        compiler_params=pltpu.CompilerParams(vmem_limit_bytes=28 * 1024 * 1024),
    )(*flat)


class Order:
    def __init__(self):
        self.last = ()

    def after(self, values):
        values, unused = lax.optimization_barrier((values, self.last))
        return values

    def before(self, values):
        self.last = values


def bit_remaps(remaps, devices):
    one, two = remaps
    pitch = round_up(one[-1][1], 8)
    tiles = one[-1][2] // LANES
    some, most = tiles * 5 // 12, tiles * 3 // 4
    plans = (
        [(0, tiles, MIXED)],
        [(0, some, MIXED), (some, most, MIXED), (most, tiles, STRAIGHT)],
    )
    ones, twos = [[Chain(chunk, devices, pitch) for chunk in chunks] for chunks in plans]
    order = Order()

    def step(*chains):
        gots = order.after([chain.got for chain in chains])
        for chain, got in zip(chains, gots):
            chain.got = got
            chain.send_next()
        order.before([chain.total for chain in chains])

    def summed(line, terms):
        terms = order.after(terms)
        for chain in line:
            chain.first(terms)
        order.before([chain.total for chain in line])

    def rested(line, terms):
        terms = order.after(terms)
        order.before(terms)
        for chain in line:
            chain.rest(terms)

    def both_cores(keep, send):
        return [keep, exchange(send, STRAIGHT, 0, devices)]

    (a,) = ones
    b, c, d = twos

    keep, send, keep_on, send_on = products(one, plans[0], devices)
    on = both_cores(keep_on, send_on)
    rest = both_cores(keep, send)
    summed(ones, on)
    a.second()
    rested(ones, rest)
    made = products((order.after(two[0]),) + two[1:], plans[1], devices)
    order.before(made)
    keep, send, keep_on, send_on = made
    on = both_cores(keep_on, send_on)
    rest = both_cores(keep, send)

    step(a)
    summed(twos, on)
    for chain in twos:
        chain.second()
    step(a)
    rested(twos, rest)
    step(b)
    step(c)
    step(b)
    step(d)
    step(a)
    step(c)
    step(d)
    step(c)
    step(b, d)
    return [final_sum(line, remap[-1], pitch) for line, remap in zip((ones, twos), remaps)]


def on_device(devices, *args):
    latlon, healpix = args[:2]
    remaps = [
        (latlon, args[2], args[3], args[4], args[5], healpix.shape),
        (healpix, args[6], args[7], args[8], args[9], latlon.shape),
    ]
    tiles = max(latlon.shape[2], healpix.shape[2]) // LANES
    size = devices * tiles * round_up(latlon.shape[1], 8) * LANES * 4
    if devices == 1 << BITS and size <= ACC_LIMIT:
        return tuple(bit_remaps(remaps, devices))
    return tuple(slot_remap(*remap) for remap in remaps)


def solution(mesh):
    in_specs = (
        P("groups", None, "curve"),
        P("groups", None, "curve"),
        P("curve", None, None),
        P("curve"),
        P("curve"),
        P("curve", None),
        P("curve", None, None),
        P("curve"),
        P("curve"),
        P("curve", None),
    )
    out_specs = (P("groups", None, "curve"), P("groups", None, "curve"))
    return jax.shard_map(
        functools.partial(on_device, mesh.shape["curve"]),
        mesh=mesh, in_specs=in_specs, out_specs=out_specs, check_vma=False,
    )
```

```python
import functools

import jax
import jax.numpy as jnp
from jax import lax
from jax.experimental import pallas as pl
from jax.experimental.pallas import tpu as pltpu
from jax.sharding import PartitionSpec as P

LANES = 128
ACC_LIMIT = 16 * 1024 * 1024


def round_up(value, unit):
    return -(-value // unit) * unit


def block_products(cotangent, weights, source):
    width = weights.shape[1]
    lead = cotangent.shape[0] * cotangent.shape[1]
    tiled = cotangent.reshape(lead, cotangent.shape[2] // width, width)
    picked = jnp.take(tiled, source, axis=1)
    products = jnp.einsum("kbi,bij->bkj", picked, weights, preferred_element_type=jnp.float32)
    return products.astype(jnp.bfloat16)


def pack_slots(products, target, count_row):
    blocks = products.shape[0]
    devices = count_row.shape[0]
    per_device = 2 * blocks // devices
    inclusive = jnp.cumsum(count_row)
    exclusive = inclusive - count_row
    positions = jnp.arange(blocks, dtype=jnp.int32)
    owner = jnp.sum((positions[:, None] >= inclusive[None, :]).astype(jnp.int32), axis=1)
    chosen = owner[:, None] == jnp.arange(devices, dtype=jnp.int32)[None, :]
    first = jnp.sum(jnp.where(chosen, exclusive[None, :], 0), axis=1)
    slot_index = owner * per_device + positions - first
    buffer = (
        jnp.zeros((devices * per_device,) + products.shape[1:], jnp.bfloat16)
        .at[slot_index]
        .set(products)
    )
    labels = jnp.full((devices * per_device,), -1, jnp.int32).at[slot_index].set(target)
    return (buffer, labels)


def sum_slots(received, labels, tiles_out, like_shape):
    selector = (labels[None, :] == jnp.arange(tiles_out, dtype=jnp.int32)[:, None]).astype(
        jnp.bfloat16
    )
    summed = jnp.einsum("ts,skc->ktc", selector, received, preferred_element_type=jnp.float32)
    return summed.reshape(like_shape[0], like_shape[1], -1).astype(jnp.bfloat16)


def slot_remap(cotangent, weights, source, target, counts, like_shape):
    products = block_products(cotangent, weights, source)
    buffer, labels = pack_slots(products, target, counts[0])
    arrived = lax.all_to_all(buffer, "curve", split_axis=0, concat_axis=0, tiled=True)
    arrived_labels = lax.all_to_all(labels, "curve", split_axis=0, concat_axis=0, tiled=True)
    return sum_slots(arrived, arrived_labels, like_shape[2] // weights.shape[1], like_shape)


STRAIGHT = ((0, 1, 2, 3), (0, 1, 2, 3))
MIXED = ((0, 1, 2, 3), (0, 2, 1, 3))
BITS = 4


def product_kernel(
    channels, pitch, chunks, step_blocks,
    source_hbm, target_hbm, counts_hbm, x_hbm, w_hbm, *rest,
):
    number = len(chunks)
    acc, send, send_on, xs, x_in, w, source, target, counts, places, sems = rest
    devices = counts.shape[1]
    steps = w.shape[0] // step_blocks
    me = lax.axis_index("curve")

    scalars = [
        pltpu.make_async_copy(source_hbm, source, sems.at[0]),
        pltpu.make_async_copy(target_hbm, target, sems.at[1]),
        pltpu.make_async_copy(counts_hbm, counts, sems.at[2]),
    ]
    x_copy = pltpu.make_async_copy(x_hbm, x_in, sems.at[3])

    def w_copy(step):
        at = pl.ds(step * step_blocks, step_blocks)
        return pltpu.make_async_copy(w_hbm.at[at], w.at[at], sems.at[4 + step])

    for copy in scalars + [x_copy]:
        copy.start()
    for step in range(steps):
        w_copy(step).start()

    @pl.loop(0, acc.shape[0] // pitch)
    def clear(index):
        acc[pl.ds(pl.multiple_of(index * pitch, pitch), pitch), :] = jnp.zeros((pitch, LANES), jnp.float32)

    for tile in range(xs.shape[0]):
        xs[tile] = jnp.zeros(xs.shape[1:], xs.dtype)

    for owner in range(devices):
        differ = jnp.bitwise_xor(me, owner)
        found = {}
        for chunk, (low, high, way) in enumerate(chunks):
            first, second, *others = way[owner % 2]
            key = (second, first, *others)
            if key not in found:
                place = jnp.int32(0)
                for bit in key:
                    place = place * 2 + jnp.bitwise_and(jnp.right_shift(differ, bit), 1)
                found[key] = place
            places[chunk, owner] = devices * low + found[key] * (high - low) - low

    x_copy.wait()
    for tile in range(xs.shape[0]):
        xs[tile, :channels, :] = x_in[0, :, tile * LANES:(tile + 1) * LANES]
    for copy in scalars:
        copy.wait()

    def some(step, carry):
        owner, end = carry
        w_copy(step).wait()
        rows = []
        for index in range(step_blocks):
            block = step * step_blocks + index
            passed = (block >= end).astype(jnp.int32)
            owner = jnp.minimum(owner + passed, devices - 1)
            end = end + passed * counts[0, owner]
            tile = target[block]
            place = places[0, owner]
            for chunk in range(1, number):
                place = jnp.where(tile >= chunks[chunk][0], places[chunk, owner], place)
            rows.append(pl.multiple_of((place + tile) * pitch, 8))
        for index, row in enumerate(rows):
            block = step * step_blocks + index
            product = jnp.dot(xs[source[block], :pitch, :], w[block], preferred_element_type=jnp.float32)
            acc[pl.ds(row, pitch), :] += product
        return owner, end

    lax.fori_loop(0, steps, some, (jnp.int32(0), counts[0, 0]))

    quarter = devices // 4
    for low, high, way in chunks:
        unit = (high - low) * pitch

        @pl.loop(0, quarter)
        def finish(index):
            at = pl.multiple_of(quarter * low * pitch + index * unit, 8)
            row = pl.multiple_of((devices * low + quarter * (high - low)) * pitch + index * unit, 8)
            send[pl.ds(at, unit), :] = acc[pl.ds(row, unit), :].astype(send.dtype)
            row = pl.multiple_of(row + 2 * quarter * unit, 8)
            send_on[pl.ds(at, unit), :] = acc[pl.ds(row, unit), :].astype(send.dtype)


def products(remap, chunks, devices):
    cotangent, weights, source, target, counts = remap[:5]
    channels = cotangent.shape[1]
    pitch = round_up(channels, 8)
    tiles_in = cotangent.shape[2] // LANES
    blocks = weights.shape[0]
    step_blocks = max(size for size in range(1, 17) if blocks % size == 0)
    rows = devices // 4 * chunks[-1][1] * pitch
    return pl.pallas_call(
        functools.partial(product_kernel, channels, pitch, chunks, step_blocks),
        out_shape=[
            jax.ShapeDtypeStruct((4 * rows, LANES), jnp.float32),
            jax.ShapeDtypeStruct((rows, LANES), jnp.bfloat16),
            jax.ShapeDtypeStruct((rows, LANES), jnp.bfloat16),
        ],
        in_specs=[pl.BlockSpec(memory_space=pltpu.HBM)] * 5,
        out_specs=[pl.BlockSpec(memory_space=pltpu.VMEM)] * 3,
        scratch_shapes=[
            pltpu.VMEM((tiles_in, round_up(pitch, 16), LANES), jnp.bfloat16),
            pltpu.VMEM(cotangent.shape, jnp.bfloat16),
            pltpu.VMEM(weights.shape, jnp.bfloat16),
            pltpu.SMEM(source.shape, jnp.int32),
            pltpu.SMEM(target.shape, jnp.int32),
            pltpu.SMEM(counts.shape, jnp.int32),
            pltpu.SMEM((len(chunks), devices), jnp.int32),
            pltpu.SemaphoreType.DMA((4 + blocks // step_blocks,)),
        ],
        compiler_params=pltpu.CompilerParams(vmem_limit_bytes=24 * 1024 * 1024),
        cost_estimate=pl.CostEstimate(
            flops=2 * blocks * channels * LANES * LANES,
            bytes_accessed=2 * weights.size + 20 * rows * LANES,
            transcendentals=0,
        ),
    )(*[pltpu.with_memory_space_constraint(value, pltpu.HBM) for value in (source, target, counts, cotangent, weights)])


def exchange(value, way, stage, devices):
    pairs = [(at, at ^ (1 << way[at % 2][stage])) for at in range(devices)]
    return lax.ppermute(value, "curve", pairs)


class Chain:
    def __init__(self, chunk, devices, pitch):
        self.chunk, self.devices = chunk, devices
        self.way = chunk[2]
        self.base = devices // 4 * chunk[0] * pitch
        self.length = devices // 4 * (chunk[1] - chunk[0]) * pitch

    def first(self, sums, got):
        self.terms = [(sums, 4 * self.base + 2 * self.length), (got, self.base)]
        self.total = self.part(0, self.length).astype(jnp.bfloat16)

    def part(self, low, high):
        return sum(term[base + low:base + high].astype(jnp.float32) for term, base in self.terms)

    def second(self):
        self.stage = 1
        self.got = exchange(self.total, self.way, self.stage, self.devices)

    def rest(self, sums, got):
        self.terms = [(sums, 4 * self.base), (got, self.base)]

    def send_next(self):
        self.terms = self.terms + [(self.got, 0)]
        self.stage += 1
        self.total = self.got
        if self.stage < BITS:
            half = self.length // 2
            self.total = self.part(half, self.length).astype(jnp.bfloat16)
            self.length = half
            self.got = exchange(self.total, self.way, self.stage, self.devices)
            if self.stage == BITS - 1:
                self.terms = [(self.part(0, half), 0)]


def final_kernel(channels, pitch, parts, *refs):
    out = refs[-1]
    at = 0
    for low, high, count in parts:
        terms = refs[at:at + count]
        at += count
        for tile in range(high - low):
            total = sum(
                term[tile * pitch:(tile + 1) * pitch, :].astype(jnp.float32) for term in terms
            )
            lane = (low + tile) * LANES
            out[0, :, lane:lane + LANES] = total[:channels].astype(jnp.bfloat16)


def final_sum(chains, like_shape, pitch):
    parts = [(chain.chunk[0], chain.chunk[1], len(chain.terms)) for chain in chains]
    flat, specs = [], []
    for chain in chains:
        rows = (chain.chunk[1] - chain.chunk[0]) * pitch
        for term, base in chain.terms:
            flat.append(term if base % rows == 0 else term[base:base + rows])
            at = base // rows if base % rows == 0 else 0
            specs.append(pl.BlockSpec((rows, LANES), lambda step, at=at: (at, 0)))
    return pl.pallas_call(
        functools.partial(final_kernel, like_shape[1], pitch, parts),
        out_shape=jax.ShapeDtypeStruct(like_shape, jnp.bfloat16),
        grid=(1,),
        in_specs=specs,
        out_specs=pl.BlockSpec(like_shape, lambda step: (0, 0, 0)),
        compiler_params=pltpu.CompilerParams(vmem_limit_bytes=24 * 1024 * 1024),
    )(*flat)


class Order:
    def __init__(self):
        self.last = ()

    def after(self, values):
        values, unused = lax.optimization_barrier((values, self.last))
        return values

    def before(self, values):
        self.last = values


def bit_remaps(remaps, devices):
    one, two = remaps
    pitch = round_up(one[-1][1], 8)
    tiles = one[-1][2] // LANES
    some, most = tiles * 5 // 12, tiles * 3 // 4
    plans = (
        [(0, most, MIXED), (most, tiles, MIXED)],
        [(0, some, MIXED), (some, most, STRAIGHT), (most, tiles, STRAIGHT)],
    )
    ones, twos = [[Chain(chunk, devices, pitch) for chunk in chunks] for chunks in plans]
    order = Order()

    def step(*chains):
        gots = order.after([chain.got for chain in chains])
        for chain, got in zip(chains, gots):
            chain.got = got
            chain.send_next()
        order.before([chain.total for chain in chains])

    def summed(line, sums, got):
        got = order.after(got)
        for chain in line:
            chain.first(sums, got)
        order.before([chain.total for chain in line])

    def rested(line, sums, got):
        got = order.after(got)
        order.before(got)
        for chain in line:
            chain.rest(sums, got)

    def begun(chain):
        chain.total = order.after(chain.total)
        chain.second()

    def cores(send):
        return exchange(send, STRAIGHT, 0, devices)

    a, b = ones
    c, d, e = twos

    sums, send, send_on = products(one, plans[0], devices)
    on, rest = cores(send_on), cores(send)
    summed(ones, sums, on)
    a.second()
    b.second()
    rested(ones, sums, rest)
    made = products((order.after(two[0]),) + two[1:], plans[1], devices)
    order.before(made)
    sums, send, send_on = made
    on, rest = cores(send_on), cores(send)

    step(a)
    step(b)
    summed(twos, sums, on)
    c.second()
    begun(d)
    step(a)
    step(b)
    rested(twos, sums, rest)
    step(c)
    begun(e)
    step(d)
    step(c)
    step(e)
    step(b)
    step(d)
    step(a)
    step(e)
    step(*twos)
    return [final_sum(line, remap[-1], pitch) for line, remap in zip((ones, twos), remaps)]


def on_device(devices, *args):
    latlon, healpix = args[:2]
    remaps = [
        (latlon, args[2], args[3], args[4], args[5], healpix.shape),
        (healpix, args[6], args[7], args[8], args[9], latlon.shape),
    ]
    tiles = max(latlon.shape[2], healpix.shape[2]) // LANES
    size = devices * tiles * round_up(latlon.shape[1], 8) * LANES * 4
    if devices == 1 << BITS and size <= ACC_LIMIT:
        return tuple(bit_remaps(remaps, devices))
    return tuple(slot_remap(*remap) for remap in remaps)


def solution(mesh):
    in_specs = (
        P("groups", None, "curve"),
        P("groups", None, "curve"),
        P("curve", None, None),
        P("curve"),
        P("curve"),
        P("curve", None),
        P("curve", None, None),
        P("curve"),
        P("curve"),
        P("curve", None),
    )
    out_specs = (P("groups", None, "curve"), P("groups", None, "curve"))
    return jax.shard_map(
        functools.partial(on_device, mesh.shape["curve"]),
        mesh=mesh, in_specs=in_specs, out_specs=out_specs, check_vma=False,
    )
```

```python
import functools

import jax
import jax.numpy as jnp
from jax import lax
from jax.experimental import pallas as pl
from jax.experimental.pallas import tpu as pltpu
from jax.sharding import PartitionSpec as P

LANES = 128
ACC_LIMIT = 16 * 1024 * 1024


def round_up(value, unit):
    return -(-value // unit) * unit


def block_products(cotangent, weights, source):
    width = weights.shape[1]
    lead = cotangent.shape[0] * cotangent.shape[1]
    tiled = cotangent.reshape(lead, cotangent.shape[2] // width, width)
    picked = jnp.take(tiled, source, axis=1)
    products = jnp.einsum("kbi,bij->bkj", picked, weights, preferred_element_type=jnp.float32)
    return products.astype(jnp.bfloat16)


def pack_slots(products, target, count_row):
    blocks = products.shape[0]
    devices = count_row.shape[0]
    per_device = 2 * blocks // devices
    inclusive = jnp.cumsum(count_row)
    exclusive = inclusive - count_row
    positions = jnp.arange(blocks, dtype=jnp.int32)
    owner = jnp.sum((positions[:, None] >= inclusive[None, :]).astype(jnp.int32), axis=1)
    chosen = owner[:, None] == jnp.arange(devices, dtype=jnp.int32)[None, :]
    first = jnp.sum(jnp.where(chosen, exclusive[None, :], 0), axis=1)
    slot_index = owner * per_device + positions - first
    buffer = (
        jnp.zeros((devices * per_device,) + products.shape[1:], jnp.bfloat16)
        .at[slot_index]
        .set(products)
    )
    labels = jnp.full((devices * per_device,), -1, jnp.int32).at[slot_index].set(target)
    return (buffer, labels)


def sum_slots(received, labels, tiles_out, like_shape):
    selector = (labels[None, :] == jnp.arange(tiles_out, dtype=jnp.int32)[:, None]).astype(
        jnp.bfloat16
    )
    summed = jnp.einsum("ts,skc->ktc", selector, received, preferred_element_type=jnp.float32)
    return summed.reshape(like_shape[0], like_shape[1], -1).astype(jnp.bfloat16)


def slot_remap(cotangent, weights, source, target, counts, like_shape):
    products = block_products(cotangent, weights, source)
    buffer, labels = pack_slots(products, target, counts[0])
    arrived = lax.all_to_all(buffer, "curve", split_axis=0, concat_axis=0, tiled=True)
    arrived_labels = lax.all_to_all(labels, "curve", split_axis=0, concat_axis=0, tiled=True)
    return sum_slots(arrived, arrived_labels, like_shape[2] // weights.shape[1], like_shape)


STRAIGHT = ((0, 1, 2, 3), (0, 1, 2, 3))
MIXED = ((0, 1, 2, 3), (0, 2, 1, 3))
BITS = 4


def product_kernel(
    channels, pitch, chunks, step_blocks,
    source_hbm, target_hbm, counts_hbm, x_hbm, w_hbm, *rest,
):
    number = len(chunks)
    acc, send, send_on, xs, x_in, w, source, target, counts, places, sems = rest
    devices = counts.shape[1]
    steps = w.shape[0] // step_blocks
    me = lax.axis_index("curve")

    scalars = [
        pltpu.make_async_copy(source_hbm, source, sems.at[0]),
        pltpu.make_async_copy(target_hbm, target, sems.at[1]),
        pltpu.make_async_copy(counts_hbm, counts, sems.at[2]),
    ]
    x_copy = pltpu.make_async_copy(x_hbm, x_in, sems.at[3])

    def w_copy(step):
        at = pl.ds(step * step_blocks, step_blocks)
        return pltpu.make_async_copy(w_hbm.at[at], w.at[at], sems.at[4 + step])

    for copy in scalars + [x_copy]:
        copy.start()
    for step in range(steps):
        w_copy(step).start()

    @pl.loop(0, acc.shape[0] // pitch)
    def clear(index):
        acc[pl.ds(pl.multiple_of(index * pitch, pitch), pitch), :] = jnp.zeros((pitch, LANES), jnp.float32)

    for tile in range(xs.shape[0]):
        xs[tile] = jnp.zeros(xs.shape[1:], xs.dtype)

    for owner in range(devices):
        differ = jnp.bitwise_xor(me, owner)
        found = {}
        for chunk, (low, high, way) in enumerate(chunks):
            first, second, *others = way[owner % 2]
            key = (second, first, *others)
            if key not in found:
                place = jnp.int32(0)
                for bit in key:
                    place = place * 2 + jnp.bitwise_and(jnp.right_shift(differ, bit), 1)
                found[key] = place
            places[chunk, owner] = devices * low + found[key] * (high - low) - low

    x_copy.wait()
    for tile in range(xs.shape[0]):
        xs[tile, :channels, :] = x_in[0, :, tile * LANES:(tile + 1) * LANES]
    for copy in scalars:
        copy.wait()

    def some(step, carry):
        owner, end = carry
        w_copy(step).wait()
        rows = []
        for index in range(step_blocks):
            block = step * step_blocks + index
            passed = (block >= end).astype(jnp.int32)
            owner = jnp.minimum(owner + passed, devices - 1)
            end = end + passed * counts[0, owner]
            tile = target[block]
            place = places[0, owner]
            for chunk in range(1, number):
                place = jnp.where(tile >= chunks[chunk][0], places[chunk, owner], place)
            rows.append(pl.multiple_of((place + tile) * pitch, 8))
        for index, row in enumerate(rows):
            block = step * step_blocks + index
            product = jnp.dot(xs[source[block], :pitch, :], w[block], preferred_element_type=jnp.float32)
            acc[pl.ds(row, pitch), :] += product
        return owner, end

    lax.fori_loop(0, steps, some, (jnp.int32(0), counts[0, 0]))

    quarter = devices // 4
    for low, high, way in chunks:
        unit = (high - low) * pitch

        @pl.loop(0, quarter)
        def finish(index):
            at = pl.multiple_of(quarter * low * pitch + index * unit, 8)
            row = pl.multiple_of((devices * low + quarter * (high - low)) * pitch + index * unit, 8)
            send[pl.ds(at, unit), :] = acc[pl.ds(row, unit), :].astype(send.dtype)
            row = pl.multiple_of(row + 2 * quarter * unit, 8)
            send_on[pl.ds(at, unit), :] = acc[pl.ds(row, unit), :].astype(send.dtype)


def products(remap, chunks, devices):
    cotangent, weights, source, target, counts = remap[:5]
    channels = cotangent.shape[1]
    pitch = round_up(channels, 8)
    tiles_in = cotangent.shape[2] // LANES
    blocks = weights.shape[0]
    step_blocks = max(size for size in range(1, 17) if blocks % size == 0)
    rows = devices // 4 * chunks[-1][1] * pitch
    return pl.pallas_call(
        functools.partial(product_kernel, channels, pitch, chunks, step_blocks),
        out_shape=[
            jax.ShapeDtypeStruct((4 * rows, LANES), jnp.float32),
            jax.ShapeDtypeStruct((rows, LANES), jnp.bfloat16),
            jax.ShapeDtypeStruct((rows, LANES), jnp.bfloat16),
        ],
        in_specs=[pl.BlockSpec(memory_space=pltpu.HBM)] * 5,
        out_specs=[pl.BlockSpec(memory_space=pltpu.VMEM)] * 3,
        scratch_shapes=[
            pltpu.VMEM((tiles_in, round_up(pitch, 16), LANES), jnp.bfloat16),
            pltpu.VMEM(cotangent.shape, jnp.bfloat16),
            pltpu.VMEM(weights.shape, jnp.bfloat16),
            pltpu.SMEM(source.shape, jnp.int32),
            pltpu.SMEM(target.shape, jnp.int32),
            pltpu.SMEM(counts.shape, jnp.int32),
            pltpu.SMEM((len(chunks), devices), jnp.int32),
            pltpu.SemaphoreType.DMA((4 + blocks // step_blocks,)),
        ],
        compiler_params=pltpu.CompilerParams(vmem_limit_bytes=24 * 1024 * 1024),
        cost_estimate=pl.CostEstimate(
            flops=2 * blocks * channels * LANES * LANES,
            bytes_accessed=2 * weights.size + 20 * rows * LANES,
            transcendentals=0,
        ),
    )(*[pltpu.with_memory_space_constraint(value, pltpu.HBM) for value in (source, target, counts, cotangent, weights)])


def exchange(value, way, stage, devices):
    pairs = [(at, at ^ (1 << way[at % 2][stage])) for at in range(devices)]
    return lax.ppermute(value, "curve", pairs)


class Chain:
    def __init__(self, chunk, devices, pitch):
        self.chunk, self.devices = chunk, devices
        self.way = chunk[2]
        self.base = devices // 4 * chunk[0] * pitch
        self.length = devices // 4 * (chunk[1] - chunk[0]) * pitch

    def first(self, sums, got):
        self.terms = [(sums, 4 * self.base + 2 * self.length), (got, self.base)]
        self.total = self.part(0, self.length).astype(jnp.bfloat16)

    def part(self, low, high):
        return sum(term[base + low:base + high].astype(jnp.float32) for term, base in self.terms)

    def second(self):
        self.stage = 1
        self.got = exchange(self.total, self.way, self.stage, self.devices)

    def rest(self, sums, got):
        self.terms = [(sums, 4 * self.base), (got, self.base)]

    def send_next(self):
        self.terms = self.terms + [(self.got, 0)]
        self.stage += 1
        self.total = self.got
        if self.stage < BITS:
            half = self.length // 2
            self.total = self.part(half, self.length).astype(jnp.bfloat16)
            self.length = half
            self.got = exchange(self.total, self.way, self.stage, self.devices)
            if self.stage == BITS - 1:
                self.terms = [(self.part(0, half), 0)]


def final_kernel(channels, pitch, parts, *refs):
    out = refs[-1]
    at = 0
    for low, high, count in parts:
        terms = refs[at:at + count]
        at += count
        for tile in range(high - low):
            total = sum(
                term[tile * pitch:(tile + 1) * pitch, :].astype(jnp.float32) for term in terms
            )
            lane = (low + tile) * LANES
            out[0, :, lane:lane + LANES] = total[:channels].astype(jnp.bfloat16)


def final_sum(chains, like_shape, pitch):
    parts = [(chain.chunk[0], chain.chunk[1], len(chain.terms)) for chain in chains]
    flat, specs = [], []
    for chain in chains:
        rows = (chain.chunk[1] - chain.chunk[0]) * pitch
        for term, base in chain.terms:
            flat.append(term if base % rows == 0 else term[base:base + rows])
            at = base // rows if base % rows == 0 else 0
            specs.append(pl.BlockSpec((rows, LANES), lambda step, at=at: (at, 0)))
    return pl.pallas_call(
        functools.partial(final_kernel, like_shape[1], pitch, parts),
        out_shape=jax.ShapeDtypeStruct(like_shape, jnp.bfloat16),
        grid=(1,),
        in_specs=specs,
        out_specs=pl.BlockSpec(like_shape, lambda step: (0, 0, 0)),
        compiler_params=pltpu.CompilerParams(vmem_limit_bytes=24 * 1024 * 1024),
    )(*flat)


class Order:
    def __init__(self):
        self.last = ()

    def after(self, values):
        values, unused = lax.optimization_barrier((values, self.last))
        return values

    def before(self, values):
        self.last = values


def bit_remaps(remaps, devices):
    one, two = remaps
    pitch = round_up(one[-1][1], 8)
    tiles = one[-1][2] // LANES
    half, most, more = tiles // 2, tiles * 3 // 4, tiles * 5 // 6
    plans = (
        [(0, most, MIXED), (most, tiles, MIXED)],
        [(0, half, MIXED), (half, more, MIXED), (more, tiles, MIXED)],
    )
    ones, twos = [[Chain(chunk, devices, pitch) for chunk in chunks] for chunks in plans]
    order = Order()

    def step(*chains):
        gots = order.after([chain.got for chain in chains])
        for chain, got in zip(chains, gots):
            chain.got = got
            chain.send_next()
        order.before([chain.total for chain in chains])

    def summed(line, sums, got):
        got = order.after(got)
        for chain in line:
            chain.first(sums, got)
        order.before([chain.total for chain in line])

    def rested(line, sums, got):
        got = order.after(got)
        order.before(got)
        for chain in line:
            chain.rest(sums, got)

    def begun(chain):
        chain.total = order.after(chain.total)
        chain.second()

    def cores(send):
        return exchange(send, STRAIGHT, 0, devices)

    a, b = ones
    c, d, e = twos

    sums, send, send_on = products(one, plans[0], devices)
    on, rest = cores(send_on), cores(send)
    summed(ones, sums, on)
    a.second()
    b.second()
    rested(ones, sums, rest)
    made = products((order.after(two[0]),) + two[1:], plans[1], devices)
    order.before(made)
    sums, send, send_on = made
    on, rest = cores(send_on), cores(send)

    step(a)
    step(b)
    summed(twos, sums, on)
    c.second()
    begun(d)
    step(b)
    rested(twos, sums, rest)
    step(c)
    step(a)
    begun(e)
    step(d)
    step(c)
    step(e)
    step(b)
    step(d)
    step(c)
    step(a)
    step(e)
    step(d)
    step(e)
    return [final_sum(line, remap[-1], pitch) for line, remap in zip((ones, twos), remaps)]


def on_device(devices, *args):
    latlon, healpix = args[:2]
    remaps = [
        (latlon, args[2], args[3], args[4], args[5], healpix.shape),
        (healpix, args[6], args[7], args[8], args[9], latlon.shape),
    ]
    tiles = max(latlon.shape[2], healpix.shape[2]) // LANES
    size = devices * tiles * round_up(latlon.shape[1], 8) * LANES * 4
    if devices == 1 << BITS and size <= ACC_LIMIT:
        return tuple(bit_remaps(remaps, devices))
    return tuple(slot_remap(*remap) for remap in remaps)


def solution(mesh):
    in_specs = (
        P("groups", None, "curve"),
        P("groups", None, "curve"),
        P("curve", None, None),
        P("curve"),
        P("curve"),
        P("curve", None),
        P("curve", None, None),
        P("curve"),
        P("curve"),
        P("curve", None),
    )
    out_specs = (P("groups", None, "curve"), P("groups", None, "curve"))
    return jax.shard_map(
        functools.partial(on_device, mesh.shape["curve"]),
        mesh=mesh, in_specs=in_specs, out_specs=out_specs, check_vma=False,
    )
```

```python
import functools

import jax
import jax.numpy as jnp
from jax import lax
from jax.experimental import pallas as pl
from jax.experimental.pallas import tpu as pltpu
from jax.sharding import PartitionSpec as P

LANES = 128
ACC_LIMIT = 16 * 1024 * 1024


def round_up(value, unit):
    return -(-value // unit) * unit


def block_products(cotangent, weights, source):
    width = weights.shape[1]
    lead = cotangent.shape[0] * cotangent.shape[1]
    tiled = cotangent.reshape(lead, cotangent.shape[2] // width, width)
    picked = jnp.take(tiled, source, axis=1)
    products = jnp.einsum("kbi,bij->bkj", picked, weights, preferred_element_type=jnp.float32)
    return products.astype(jnp.bfloat16)


def pack_slots(products, target, count_row):
    blocks = products.shape[0]
    devices = count_row.shape[0]
    per_device = 2 * blocks // devices
    inclusive = jnp.cumsum(count_row)
    exclusive = inclusive - count_row
    positions = jnp.arange(blocks, dtype=jnp.int32)
    owner = jnp.sum((positions[:, None] >= inclusive[None, :]).astype(jnp.int32), axis=1)
    chosen = owner[:, None] == jnp.arange(devices, dtype=jnp.int32)[None, :]
    first = jnp.sum(jnp.where(chosen, exclusive[None, :], 0), axis=1)
    slot_index = owner * per_device + positions - first
    buffer = (
        jnp.zeros((devices * per_device,) + products.shape[1:], jnp.bfloat16)
        .at[slot_index]
        .set(products)
    )
    labels = jnp.full((devices * per_device,), -1, jnp.int32).at[slot_index].set(target)
    return (buffer, labels)


def sum_slots(received, labels, tiles_out, like_shape):
    selector = (labels[None, :] == jnp.arange(tiles_out, dtype=jnp.int32)[:, None]).astype(
        jnp.bfloat16
    )
    summed = jnp.einsum("ts,skc->ktc", selector, received, preferred_element_type=jnp.float32)
    return summed.reshape(like_shape[0], like_shape[1], -1).astype(jnp.bfloat16)


def slot_remap(cotangent, weights, source, target, counts, like_shape):
    products = block_products(cotangent, weights, source)
    buffer, labels = pack_slots(products, target, counts[0])
    arrived = lax.all_to_all(buffer, "curve", split_axis=0, concat_axis=0, tiled=True)
    arrived_labels = lax.all_to_all(labels, "curve", split_axis=0, concat_axis=0, tiled=True)
    return sum_slots(arrived, arrived_labels, like_shape[2] // weights.shape[1], like_shape)


STRAIGHT = ((0, 1, 2, 3), (0, 1, 2, 3))
MIXED = ((0, 1, 2, 3), (0, 2, 1, 3))
BITS = 4


def product_kernel(
    channels, pitch, chunks, step_blocks,
    source_hbm, target_hbm, counts_hbm, x_hbm, w_hbm, *rest,
):
    number = len(chunks)
    acc, send, send_on, xs, x_in, w, source, target, counts, places, sems = rest
    devices = counts.shape[1]
    steps = w.shape[0] // step_blocks
    me = lax.axis_index("curve")

    scalars = [
        pltpu.make_async_copy(source_hbm, source, sems.at[0]),
        pltpu.make_async_copy(target_hbm, target, sems.at[1]),
        pltpu.make_async_copy(counts_hbm, counts, sems.at[2]),
    ]
    x_copy = pltpu.make_async_copy(x_hbm, x_in, sems.at[3])

    def w_copy(step):
        at = pl.ds(step * step_blocks, step_blocks)
        return pltpu.make_async_copy(w_hbm.at[at], w.at[at], sems.at[4 + step])

    for copy in scalars + [x_copy]:
        copy.start()
    for step in range(steps):
        w_copy(step).start()

    @pl.loop(0, acc.shape[0] // pitch)
    def clear(index):
        acc[pl.ds(pl.multiple_of(index * pitch, pitch), pitch), :] = jnp.zeros((pitch, LANES), jnp.float32)

    for tile in range(xs.shape[0]):
        xs[tile] = jnp.zeros(xs.shape[1:], xs.dtype)

    for owner in range(devices):
        differ = jnp.bitwise_xor(me, owner)
        found = {}
        for chunk, (low, high, way) in enumerate(chunks):
            first, second, *others = way[owner % 2]
            key = (second, first, *others)
            if key not in found:
                place = jnp.int32(0)
                for bit in key:
                    place = place * 2 + jnp.bitwise_and(jnp.right_shift(differ, bit), 1)
                found[key] = place
            places[chunk, owner] = devices * low + found[key] * (high - low) - low

    x_copy.wait()
    for tile in range(xs.shape[0]):
        xs[tile, :channels, :] = x_in[0, :, tile * LANES:(tile + 1) * LANES]
    for copy in scalars:
        copy.wait()

    def some(step, carry):
        owner, end = carry
        w_copy(step).wait()
        rows = []
        for index in range(step_blocks):
            block = step * step_blocks + index
            passed = (block >= end).astype(jnp.int32)
            owner = jnp.minimum(owner + passed, devices - 1)
            end = end + passed * counts[0, owner]
            tile = target[block]
            place = places[0, owner]
            for chunk in range(1, number):
                place = jnp.where(tile >= chunks[chunk][0], places[chunk, owner], place)
            rows.append(pl.multiple_of((place + tile) * pitch, 8))
        for index, row in enumerate(rows):
            block = step * step_blocks + index
            product = jnp.dot(xs[source[block], :pitch, :], w[block], preferred_element_type=jnp.float32)
            acc[pl.ds(row, pitch), :] += product
        return owner, end

    lax.fori_loop(0, steps, some, (jnp.int32(0), counts[0, 0]))

    quarter = devices // 4
    for low, high, way in chunks:
        unit = (high - low) * pitch

        @pl.loop(0, quarter)
        def finish(index):
            at = pl.multiple_of(quarter * low * pitch + index * unit, 8)
            row = pl.multiple_of((devices * low + quarter * (high - low)) * pitch + index * unit, 8)
            send[pl.ds(at, unit), :] = acc[pl.ds(row, unit), :].astype(send.dtype)
            row = pl.multiple_of(row + 2 * quarter * unit, 8)
            send_on[pl.ds(at, unit), :] = acc[pl.ds(row, unit), :].astype(send.dtype)


def products(remap, chunks, devices):
    cotangent, weights, source, target, counts = remap[:5]
    channels = cotangent.shape[1]
    pitch = round_up(channels, 8)
    tiles_in = cotangent.shape[2] // LANES
    blocks = weights.shape[0]
    step_blocks = max(size for size in range(1, 17) if blocks % size == 0)
    rows = devices // 4 * chunks[-1][1] * pitch
    return pl.pallas_call(
        functools.partial(product_kernel, channels, pitch, chunks, step_blocks),
        out_shape=[
            jax.ShapeDtypeStruct((4 * rows, LANES), jnp.float32),
            jax.ShapeDtypeStruct((rows, LANES), jnp.bfloat16),
            jax.ShapeDtypeStruct((rows, LANES), jnp.bfloat16),
        ],
        in_specs=[pl.BlockSpec(memory_space=pltpu.HBM)] * 5,
        out_specs=[pl.BlockSpec(memory_space=pltpu.VMEM)] * 3,
        scratch_shapes=[
            pltpu.VMEM((tiles_in, round_up(pitch, 16), LANES), jnp.bfloat16),
            pltpu.VMEM(cotangent.shape, jnp.bfloat16),
            pltpu.VMEM(weights.shape, jnp.bfloat16),
            pltpu.SMEM(source.shape, jnp.int32),
            pltpu.SMEM(target.shape, jnp.int32),
            pltpu.SMEM(counts.shape, jnp.int32),
            pltpu.SMEM((len(chunks), devices), jnp.int32),
            pltpu.SemaphoreType.DMA((4 + blocks // step_blocks,)),
        ],
        compiler_params=pltpu.CompilerParams(vmem_limit_bytes=24 * 1024 * 1024),
        cost_estimate=pl.CostEstimate(
            flops=2 * blocks * channels * LANES * LANES,
            bytes_accessed=2 * weights.size + 20 * rows * LANES,
            transcendentals=0,
        ),
    )(*[pltpu.with_memory_space_constraint(value, pltpu.HBM) for value in (source, target, counts, cotangent, weights)])


def exchange(value, way, stage, devices):
    pairs = [(at, at ^ (1 << way[at % 2][stage])) for at in range(devices)]
    return lax.ppermute(value, "curve", pairs)


class Chain:
    def __init__(self, chunk, devices, pitch):
        self.chunk, self.devices = chunk, devices
        self.way = chunk[2]
        self.base = devices // 4 * chunk[0] * pitch
        self.length = devices // 4 * (chunk[1] - chunk[0]) * pitch

    def first(self, sums, got):
        self.terms = [(sums, 4 * self.base + 2 * self.length), (got, self.base)]
        self.total = self.part(0, self.length).astype(jnp.bfloat16)

    def part(self, low, high):
        return sum(term[base + low:base + high].astype(jnp.float32) for term, base in self.terms)

    def second(self):
        self.stage = 1
        self.got = exchange(self.total, self.way, self.stage, self.devices)

    def rest(self, sums, got):
        self.terms = [(sums, 4 * self.base), (got, self.base)]

    def send_next(self):
        self.terms = self.terms + [(self.got, 0)]
        self.stage += 1
        self.total = self.got
        if self.stage < BITS:
            half = self.length // 2
            self.total = self.part(half, self.length).astype(jnp.bfloat16)
            self.length = half
            self.got = exchange(self.total, self.way, self.stage, self.devices)
            if self.stage == BITS - 1:
                self.terms = [(self.part(0, half), 0)]


def final_kernel(channels, pitch, parts, *refs):
    out = refs[-1]
    at = 0
    for low, high, count in parts:
        terms = refs[at:at + count]
        at += count
        for tile in range(high - low):
            total = sum(
                term[tile * pitch:(tile + 1) * pitch, :].astype(jnp.float32) for term in terms
            )
            lane = (low + tile) * LANES
            out[0, :, lane:lane + LANES] = total[:channels].astype(jnp.bfloat16)


def final_sum(chains, like_shape, pitch):
    parts = [(chain.chunk[0], chain.chunk[1], len(chain.terms)) for chain in chains]
    flat, specs = [], []
    for chain in chains:
        rows = (chain.chunk[1] - chain.chunk[0]) * pitch
        for term, base in chain.terms:
            flat.append(term if base % rows == 0 else term[base:base + rows])
            at = base // rows if base % rows == 0 else 0
            specs.append(pl.BlockSpec((rows, LANES), lambda step, at=at: (at, 0)))
    return pl.pallas_call(
        functools.partial(final_kernel, like_shape[1], pitch, parts),
        out_shape=jax.ShapeDtypeStruct(like_shape, jnp.bfloat16),
        grid=(1,),
        in_specs=specs,
        out_specs=pl.BlockSpec(like_shape, lambda step: (0, 0, 0)),
        compiler_params=pltpu.CompilerParams(vmem_limit_bytes=24 * 1024 * 1024),
    )(*flat)


class Order:
    def __init__(self):
        self.last = ()

    def after(self, values):
        values, unused = lax.optimization_barrier((values, self.last))
        return values

    def before(self, values):
        self.last = values


def bit_remaps(remaps, devices):
    one, two = remaps
    pitch = round_up(one[-1][1], 8)
    tiles = one[-1][2] // LANES
    most = tiles * 7 // 12
    plans = (
        [(0, tiles, MIXED)],
        [(0, most, MIXED), (most, tiles, MIXED)],
    )
    ones, twos = [[Chain(chunk, devices, pitch) for chunk in chunks] for chunks in plans]
    order = Order()

    def step(*chains):
        gots = order.after([chain.got for chain in chains])
        for chain, got in zip(chains, gots):
            chain.got = got
            chain.send_next()
        order.before([chain.total for chain in chains])

    def summed(line, sums, got):
        got = order.after(got)
        for chain in line:
            chain.first(sums, got)
        order.before([chain.total for chain in line])

    def rested(line, sums, got):
        got = order.after(got)
        order.before(got)
        for chain in line:
            chain.rest(sums, got)

    def begun(chain):
        chain.total = order.after(chain.total)
        chain.second()

    def cores(send):
        return exchange(send, STRAIGHT, 0, devices)

    (a,) = ones
    b, c = twos

    sums, send, send_on = products(one, plans[0], devices)
    on, rest = cores(send_on), cores(send)
    summed(ones, sums, on)
    a.second()
    rested(ones, sums, rest)
    made = products((order.after(two[0]),) + two[1:], plans[1], devices)
    order.before(made)
    sums, send, send_on = made
    on, rest = cores(send_on), cores(send)

    step(a)
    summed(twos, sums, on)
    b.second()
    begun(c)
    step(a)
    rested(twos, sums, rest)
    step(b)
    step(c)
    step(a)
    step(b)
    step(c)
    step(b)
    step(c)
    return [final_sum(line, remap[-1], pitch) for line, remap in zip((ones, twos), remaps)]


def on_device(devices, *args):
    latlon, healpix = args[:2]
    remaps = [
        (latlon, args[2], args[3], args[4], args[5], healpix.shape),
        (healpix, args[6], args[7], args[8], args[9], latlon.shape),
    ]
    tiles = max(latlon.shape[2], healpix.shape[2]) // LANES
    size = devices * tiles * round_up(latlon.shape[1], 8) * LANES * 4
    if devices == 1 << BITS and size <= ACC_LIMIT:
        return tuple(bit_remaps(remaps, devices))
    return tuple(slot_remap(*remap) for remap in remaps)


def solution(mesh):
    in_specs = (
        P("groups", None, "curve"),
        P("groups", None, "curve"),
        P("curve", None, None),
        P("curve"),
        P("curve"),
        P("curve", None),
        P("curve", None, None),
        P("curve"),
        P("curve"),
        P("curve", None),
    )
    out_specs = (P("groups", None, "curve"), P("groups", None, "curve"))
    return jax.shard_map(
        functools.partial(on_device, mesh.shape["curve"]),
        mesh=mesh, in_specs=in_specs, out_specs=out_specs, check_vma=False,
    )
```

```python
import functools

import jax
import jax.numpy as jnp
from jax import lax
from jax.experimental import pallas as pl
from jax.experimental.pallas import tpu as pltpu
from jax.sharding import PartitionSpec as P

LANES = 128
ACC_LIMIT = 16 * 1024 * 1024


def round_up(value, unit):
    return -(-value // unit) * unit


def block_products(cotangent, weights, source):
    width = weights.shape[1]
    lead = cotangent.shape[0] * cotangent.shape[1]
    tiled = cotangent.reshape(lead, cotangent.shape[2] // width, width)
    picked = jnp.take(tiled, source, axis=1)
    products = jnp.einsum("kbi,bij->bkj", picked, weights, preferred_element_type=jnp.float32)
    return products.astype(jnp.bfloat16)


def pack_slots(products, target, count_row):
    blocks = products.shape[0]
    devices = count_row.shape[0]
    per_device = 2 * blocks // devices
    inclusive = jnp.cumsum(count_row)
    exclusive = inclusive - count_row
    positions = jnp.arange(blocks, dtype=jnp.int32)
    owner = jnp.sum((positions[:, None] >= inclusive[None, :]).astype(jnp.int32), axis=1)
    chosen = owner[:, None] == jnp.arange(devices, dtype=jnp.int32)[None, :]
    first = jnp.sum(jnp.where(chosen, exclusive[None, :], 0), axis=1)
    slot_index = owner * per_device + positions - first
    buffer = (
        jnp.zeros((devices * per_device,) + products.shape[1:], jnp.bfloat16)
        .at[slot_index]
        .set(products)
    )
    labels = jnp.full((devices * per_device,), -1, jnp.int32).at[slot_index].set(target)
    return (buffer, labels)


def sum_slots(received, labels, tiles_out, like_shape):
    selector = (labels[None, :] == jnp.arange(tiles_out, dtype=jnp.int32)[:, None]).astype(
        jnp.bfloat16
    )
    summed = jnp.einsum("ts,skc->ktc", selector, received, preferred_element_type=jnp.float32)
    return summed.reshape(like_shape[0], like_shape[1], -1).astype(jnp.bfloat16)


def slot_remap(cotangent, weights, source, target, counts, like_shape):
    products = block_products(cotangent, weights, source)
    buffer, labels = pack_slots(products, target, counts[0])
    arrived = lax.all_to_all(buffer, "curve", split_axis=0, concat_axis=0, tiled=True)
    arrived_labels = lax.all_to_all(labels, "curve", split_axis=0, concat_axis=0, tiled=True)
    return sum_slots(arrived, arrived_labels, like_shape[2] // weights.shape[1], like_shape)


STRAIGHT = ((0, 1, 2, 3), (0, 1, 2, 3))
MIXED = ((0, 1, 2, 3), (0, 2, 1, 3))
BITS = 4


def product_kernel(
    channels, pitch, chunks, step_blocks,
    source_hbm, target_hbm, counts_hbm, x_hbm, w_hbm, *rest,
):
    number = len(chunks)
    acc, send, send_on, xs, x_in, w, source, target, counts, places, sems = rest
    devices = counts.shape[1]
    steps = w.shape[0] // step_blocks
    me = lax.axis_index("curve")

    scalars = [
        pltpu.make_async_copy(source_hbm, source, sems.at[0]),
        pltpu.make_async_copy(target_hbm, target, sems.at[1]),
        pltpu.make_async_copy(counts_hbm, counts, sems.at[2]),
    ]
    x_copy = pltpu.make_async_copy(x_hbm, x_in, sems.at[3])

    def w_copy(step):
        at = pl.ds(step * step_blocks, step_blocks)
        return pltpu.make_async_copy(w_hbm.at[at], w.at[at], sems.at[4 + step])

    for copy in scalars + [x_copy]:
        copy.start()
    for step in range(steps):
        w_copy(step).start()

    @pl.loop(0, acc.shape[0] // pitch)
    def clear(index):
        acc[pl.ds(pl.multiple_of(index * pitch, pitch), pitch), :] = jnp.zeros((pitch, LANES), jnp.float32)

    for tile in range(xs.shape[0]):
        xs[tile] = jnp.zeros(xs.shape[1:], xs.dtype)

    for owner in range(devices):
        differ = jnp.bitwise_xor(me, owner)
        found = {}
        for chunk, (low, high, way) in enumerate(chunks):
            first, second, *others = way[owner % 2]
            key = (second, first, *others)
            if key not in found:
                place = jnp.int32(0)
                for bit in key:
                    place = place * 2 + jnp.bitwise_and(jnp.right_shift(differ, bit), 1)
                found[key] = place
            places[chunk, owner] = devices * low + found[key] * (high - low) - low

    x_copy.wait()
    for tile in range(xs.shape[0]):
        xs[tile, :channels, :] = x_in[0, :, tile * LANES:(tile + 1) * LANES]
    for copy in scalars:
        copy.wait()

    def some(step, carry):
        owner, end = carry
        w_copy(step).wait()
        rows = []
        for index in range(step_blocks):
            block = step * step_blocks + index
            passed = (block >= end).astype(jnp.int32)
            owner = jnp.minimum(owner + passed, devices - 1)
            end = end + passed * counts[0, owner]
            tile = target[block]
            place = places[0, owner]
            for chunk in range(1, number):
                place = jnp.where(tile >= chunks[chunk][0], places[chunk, owner], place)
            rows.append(pl.multiple_of((place + tile) * pitch, 8))
        for index, row in enumerate(rows):
            block = step * step_blocks + index
            product = jnp.dot(xs[source[block], :pitch, :], w[block], preferred_element_type=jnp.float32)
            acc[pl.ds(row, pitch), :] += product
        return owner, end

    lax.fori_loop(0, steps, some, (jnp.int32(0), counts[0, 0]))

    quarter = devices // 4
    for low, high, way in chunks:
        unit = (high - low) * pitch

        @pl.loop(0, quarter)
        def finish(index):
            at = pl.multiple_of(quarter * low * pitch + index * unit, 8)
            row = pl.multiple_of((devices * low + quarter * (high - low)) * pitch + index * unit, 8)
            send[pl.ds(at, unit), :] = acc[pl.ds(row, unit), :].astype(send.dtype)
            row = pl.multiple_of(row + 2 * quarter * unit, 8)
            send_on[pl.ds(at, unit), :] = acc[pl.ds(row, unit), :].astype(send.dtype)


def products(remap, chunks, devices):
    cotangent, weights, source, target, counts = remap[:5]
    channels = cotangent.shape[1]
    pitch = round_up(channels, 8)
    tiles_in = cotangent.shape[2] // LANES
    blocks = weights.shape[0]
    step_blocks = max(size for size in range(1, 17) if blocks % size == 0)
    rows = devices // 4 * chunks[-1][1] * pitch
    return pl.pallas_call(
        functools.partial(product_kernel, channels, pitch, chunks, step_blocks),
        out_shape=[
            jax.ShapeDtypeStruct((4 * rows, LANES), jnp.float32),
            jax.ShapeDtypeStruct((rows, LANES), jnp.bfloat16),
            jax.ShapeDtypeStruct((rows, LANES), jnp.bfloat16),
        ],
        in_specs=[pl.BlockSpec(memory_space=pltpu.HBM)] * 5,
        out_specs=[pl.BlockSpec(memory_space=pltpu.VMEM)] * 3,
        scratch_shapes=[
            pltpu.VMEM((tiles_in, round_up(pitch, 16), LANES), jnp.bfloat16),
            pltpu.VMEM(cotangent.shape, jnp.bfloat16),
            pltpu.VMEM(weights.shape, jnp.bfloat16),
            pltpu.SMEM(source.shape, jnp.int32),
            pltpu.SMEM(target.shape, jnp.int32),
            pltpu.SMEM(counts.shape, jnp.int32),
            pltpu.SMEM((len(chunks), devices), jnp.int32),
            pltpu.SemaphoreType.DMA((4 + blocks // step_blocks,)),
        ],
        compiler_params=pltpu.CompilerParams(vmem_limit_bytes=24 * 1024 * 1024),
        cost_estimate=pl.CostEstimate(
            flops=2 * blocks * channels * LANES * LANES,
            bytes_accessed=2 * weights.size + 20 * rows * LANES,
            transcendentals=0,
        ),
    )(*[pltpu.with_memory_space_constraint(value, pltpu.HBM) for value in (source, target, counts, cotangent, weights)])


def exchange(value, way, stage, devices):
    pairs = [(at, at ^ (1 << way[at % 2][stage])) for at in range(devices)]
    return lax.ppermute(value, "curve", pairs)


class Chain:
    def __init__(self, chunk, devices, pitch):
        self.chunk, self.devices = chunk, devices
        self.way = chunk[2]
        self.base = devices // 4 * chunk[0] * pitch
        self.length = devices // 4 * (chunk[1] - chunk[0]) * pitch

    def first(self, sums, got):
        self.terms = [(sums, 4 * self.base + 2 * self.length), (got, self.base)]
        self.total = self.part(0, self.length).astype(jnp.bfloat16)

    def part(self, low, high):
        return sum(term[base + low:base + high].astype(jnp.float32) for term, base in self.terms)

    def second(self):
        self.stage = 1
        self.got = exchange(self.total, self.way, self.stage, self.devices)

    def rest(self, sums, got):
        self.terms = [(sums, 4 * self.base), (got, self.base)]

    def send_next(self):
        self.terms = self.terms + [(self.got, 0)]
        self.stage += 1
        self.total = self.got
        if self.stage < BITS:
            half = self.length // 2
            self.total = self.part(half, self.length).astype(jnp.bfloat16)
            self.length = half
            self.got = exchange(self.total, self.way, self.stage, self.devices)
            if self.stage == BITS - 1:
                self.terms = [(self.part(0, half), 0)]


def final_kernel(channels, pitch, parts, *refs):
    out = refs[-1]
    at = 0
    for low, high, count in parts:
        terms = refs[at:at + count]
        at += count
        for tile in range(high - low):
            total = sum(
                term[tile * pitch:(tile + 1) * pitch, :].astype(jnp.float32) for term in terms
            )
            lane = (low + tile) * LANES
            out[0, :, lane:lane + LANES] = total[:channels].astype(jnp.bfloat16)


def final_sum(chains, like_shape, pitch):
    parts = [(chain.chunk[0], chain.chunk[1], len(chain.terms)) for chain in chains]
    flat, specs = [], []
    for chain in chains:
        rows = (chain.chunk[1] - chain.chunk[0]) * pitch
        for term, base in chain.terms:
            flat.append(term if base % rows == 0 else term[base:base + rows])
            at = base // rows if base % rows == 0 else 0
            specs.append(pl.BlockSpec((rows, LANES), lambda step, at=at: (at, 0)))
    return pl.pallas_call(
        functools.partial(final_kernel, like_shape[1], pitch, parts),
        out_shape=jax.ShapeDtypeStruct(like_shape, jnp.bfloat16),
        grid=(1,),
        in_specs=specs,
        out_specs=pl.BlockSpec(like_shape, lambda step: (0, 0, 0)),
        compiler_params=pltpu.CompilerParams(vmem_limit_bytes=24 * 1024 * 1024),
    )(*flat)


class Order:
    def __init__(self):
        self.last = ()

    def after(self, values):
        values, unused = lax.optimization_barrier((values, self.last))
        return values

    def before(self, values):
        self.last = values


def bit_remaps(remaps, devices):
    one, two = remaps
    pitch = round_up(one[-1][1], 8)
    tiles = one[-1][2] // LANES
    half, most, more = tiles // 2, tiles * 3 // 4, tiles * 5 // 6
    plans = (
        [(0, most, MIXED), (most, tiles, MIXED)],
        [(0, half, STRAIGHT), (half, more, STRAIGHT), (more, tiles, STRAIGHT)],
    )
    ones, twos = [[Chain(chunk, devices, pitch) for chunk in chunks] for chunks in plans]
    order = Order()

    def step(*chains):
        gots = order.after([chain.got for chain in chains])
        for chain, got in zip(chains, gots):
            chain.got = got
            chain.send_next()
        order.before([chain.total for chain in chains])

    def summed(line, sums, got):
        got = order.after(got)
        for chain in line:
            chain.first(sums, got)
        order.before([chain.total for chain in line])

    def rested(line, sums, got):
        got = order.after(got)
        order.before(got)
        for chain in line:
            chain.rest(sums, got)

    def begun(chain):
        chain.total = order.after(chain.total)
        chain.second()

    def cores(send):
        return exchange(send, STRAIGHT, 0, devices)

    a, b = ones
    c, d, e = twos

    sums, send, send_on = products(one, plans[0], devices)
    on, rest = cores(send_on), cores(send)
    summed(ones, sums, on)
    a.second()
    b.second()
    rested(ones, sums, rest)
    made = products((order.after(two[0]),) + two[1:], plans[1], devices)
    order.before(made)
    sums, send, send_on = made
    on, rest = cores(send_on), cores(send)

    step(a)
    step(b)
    summed(twos, sums, on)
    c.second()
    begun(d)
    step(a)
    step(b)
    rested(twos, sums, rest)
    step(c)
    begun(e)
    step(d)
    step(a)
    step(b)
    step(c)
    step(e)
    step(c)
    step(d)
    step(e)
    step(d)
    step(e)
    return [final_sum(line, remap[-1], pitch) for line, remap in zip((ones, twos), remaps)]


def on_device(devices, *args):
    latlon, healpix = args[:2]
    remaps = [
        (latlon, args[2], args[3], args[4], args[5], healpix.shape),
        (healpix, args[6], args[7], args[8], args[9], latlon.shape),
    ]
    tiles = max(latlon.shape[2], healpix.shape[2]) // LANES
    size = devices * tiles * round_up(latlon.shape[1], 8) * LANES * 4
    if devices == 1 << BITS and size <= ACC_LIMIT:
        return tuple(bit_remaps(remaps, devices))
    return tuple(slot_remap(*remap) for remap in remaps)


def solution(mesh):
    in_specs = (
        P("groups", None, "curve"),
        P("groups", None, "curve"),
        P("curve", None, None),
        P("curve"),
        P("curve"),
        P("curve", None),
        P("curve", None, None),
        P("curve"),
        P("curve"),
        P("curve", None),
    )
    out_specs = (P("groups", None, "curve"), P("groups", None, "curve"))
    return jax.shard_map(
        functools.partial(on_device, mesh.shape["curve"]),
        mesh=mesh, in_specs=in_specs, out_specs=out_specs, check_vma=False,
    )
```

```python
import functools

import jax
import jax.numpy as jnp
from jax import lax
from jax.experimental import pallas as pl
from jax.experimental.pallas import tpu as pltpu
from jax.sharding import PartitionSpec as P

LANES = 128
ACC_LIMIT = 16 * 1024 * 1024


def round_up(value, unit):
    return -(-value // unit) * unit


def block_products(cotangent, weights, source):
    width = weights.shape[1]
    lead = cotangent.shape[0] * cotangent.shape[1]
    tiled = cotangent.reshape(lead, cotangent.shape[2] // width, width)
    picked = jnp.take(tiled, source, axis=1)
    products = jnp.einsum("kbi,bij->bkj", picked, weights, preferred_element_type=jnp.float32)
    return products.astype(jnp.bfloat16)


def pack_slots(products, target, count_row):
    blocks = products.shape[0]
    devices = count_row.shape[0]
    per_device = 2 * blocks // devices
    inclusive = jnp.cumsum(count_row)
    exclusive = inclusive - count_row
    positions = jnp.arange(blocks, dtype=jnp.int32)
    owner = jnp.sum((positions[:, None] >= inclusive[None, :]).astype(jnp.int32), axis=1)
    chosen = owner[:, None] == jnp.arange(devices, dtype=jnp.int32)[None, :]
    first = jnp.sum(jnp.where(chosen, exclusive[None, :], 0), axis=1)
    slot_index = owner * per_device + positions - first
    buffer = (
        jnp.zeros((devices * per_device,) + products.shape[1:], jnp.bfloat16)
        .at[slot_index]
        .set(products)
    )
    labels = jnp.full((devices * per_device,), -1, jnp.int32).at[slot_index].set(target)
    return (buffer, labels)


def sum_slots(received, labels, tiles_out, like_shape):
    selector = (labels[None, :] == jnp.arange(tiles_out, dtype=jnp.int32)[:, None]).astype(
        jnp.bfloat16
    )
    summed = jnp.einsum("ts,skc->ktc", selector, received, preferred_element_type=jnp.float32)
    return summed.reshape(like_shape[0], like_shape[1], -1).astype(jnp.bfloat16)


def slot_remap(cotangent, weights, source, target, counts, like_shape):
    products = block_products(cotangent, weights, source)
    buffer, labels = pack_slots(products, target, counts[0])
    arrived = lax.all_to_all(buffer, "curve", split_axis=0, concat_axis=0, tiled=True)
    arrived_labels = lax.all_to_all(labels, "curve", split_axis=0, concat_axis=0, tiled=True)
    return sum_slots(arrived, arrived_labels, like_shape[2] // weights.shape[1], like_shape)


STRAIGHT = ((0, 1, 2, 3), (0, 1, 2, 3))
MIXED = ((0, 1, 2, 3), (0, 2, 1, 3))
BITS = 4


def product_kernel(
    channels, pitch, chunks, step_blocks,
    source_hbm, target_hbm, counts_hbm, x_hbm, w_hbm, *rest,
):
    number = len(chunks)
    acc, send, send_on, xs, x_in, w, source, target, counts, places, sems = rest
    devices = counts.shape[1]
    steps = w.shape[0] // step_blocks
    me = lax.axis_index("curve")

    scalars = [
        pltpu.make_async_copy(source_hbm, source, sems.at[0]),
        pltpu.make_async_copy(target_hbm, target, sems.at[1]),
        pltpu.make_async_copy(counts_hbm, counts, sems.at[2]),
    ]
    x_copy = pltpu.make_async_copy(x_hbm, x_in, sems.at[3])

    def w_copy(step):
        at = pl.ds(step * step_blocks, step_blocks)
        return pltpu.make_async_copy(w_hbm.at[at], w.at[at], sems.at[4 + step])

    for copy in scalars + [x_copy]:
        copy.start()
    for step in range(steps):
        w_copy(step).start()

    @pl.loop(0, acc.shape[0] // pitch)
    def clear(index):
        acc[pl.ds(pl.multiple_of(index * pitch, pitch), pitch), :] = jnp.zeros((pitch, LANES), jnp.float32)

    for tile in range(xs.shape[0]):
        xs[tile] = jnp.zeros(xs.shape[1:], xs.dtype)

    for owner in range(devices):
        differ = jnp.bitwise_xor(me, owner)
        found = {}
        for chunk, (low, high, way) in enumerate(chunks):
            first, second, *others = way[owner % 2]
            key = (second, first, *others)
            if key not in found:
                place = jnp.int32(0)
                for bit in key:
                    place = place * 2 + jnp.bitwise_and(jnp.right_shift(differ, bit), 1)
                found[key] = place
            places[chunk, owner] = devices * low + found[key] * (high - low) - low

    x_copy.wait()
    for tile in range(xs.shape[0]):
        xs[tile, :channels, :] = x_in[0, :, tile * LANES:(tile + 1) * LANES]
    for copy in scalars:
        copy.wait()

    def some(step, carry):
        owner, end = carry
        w_copy(step).wait()
        rows = []
        for index in range(step_blocks):
            block = step * step_blocks + index
            passed = (block >= end).astype(jnp.int32)
            owner = jnp.minimum(owner + passed, devices - 1)
            end = end + passed * counts[0, owner]
            tile = target[block]
            place = places[0, owner]
            for chunk in range(1, number):
                place = jnp.where(tile >= chunks[chunk][0], places[chunk, owner], place)
            rows.append(pl.multiple_of((place + tile) * pitch, 8))
        for index, row in enumerate(rows):
            block = step * step_blocks + index
            product = jnp.dot(xs[source[block], :pitch, :], w[block], preferred_element_type=jnp.float32)
            acc[pl.ds(row, pitch), :] += product
        return owner, end

    lax.fori_loop(0, steps, some, (jnp.int32(0), counts[0, 0]))

    quarter = devices // 4
    for low, high, way in chunks:
        unit = (high - low) * pitch

        @pl.loop(0, quarter)
        def finish(index):
            at = pl.multiple_of(quarter * low * pitch + index * unit, 8)
            row = pl.multiple_of((devices * low + quarter * (high - low)) * pitch + index * unit, 8)
            send[pl.ds(at, unit), :] = acc[pl.ds(row, unit), :].astype(send.dtype)
            row = pl.multiple_of(row + 2 * quarter * unit, 8)
            send_on[pl.ds(at, unit), :] = acc[pl.ds(row, unit), :].astype(send.dtype)


def products(remap, chunks, devices):
    cotangent, weights, source, target, counts = remap[:5]
    channels = cotangent.shape[1]
    pitch = round_up(channels, 8)
    tiles_in = cotangent.shape[2] // LANES
    blocks = weights.shape[0]
    step_blocks = max(size for size in range(1, 17) if blocks % size == 0)
    rows = devices // 4 * chunks[-1][1] * pitch
    return pl.pallas_call(
        functools.partial(product_kernel, channels, pitch, chunks, step_blocks),
        out_shape=[
            jax.ShapeDtypeStruct((4 * rows, LANES), jnp.float32),
            jax.ShapeDtypeStruct((rows, LANES), jnp.bfloat16),
            jax.ShapeDtypeStruct((rows, LANES), jnp.bfloat16),
        ],
        in_specs=[pl.BlockSpec(memory_space=pltpu.HBM)] * 5,
        out_specs=[pl.BlockSpec(memory_space=pltpu.VMEM)] * 3,
        scratch_shapes=[
            pltpu.VMEM((tiles_in, round_up(pitch, 16), LANES), jnp.bfloat16),
            pltpu.VMEM(cotangent.shape, jnp.bfloat16),
            pltpu.VMEM(weights.shape, jnp.bfloat16),
            pltpu.SMEM(source.shape, jnp.int32),
            pltpu.SMEM(target.shape, jnp.int32),
            pltpu.SMEM(counts.shape, jnp.int32),
            pltpu.SMEM((len(chunks), devices), jnp.int32),
            pltpu.SemaphoreType.DMA((4 + blocks // step_blocks,)),
        ],
        compiler_params=pltpu.CompilerParams(vmem_limit_bytes=24 * 1024 * 1024),
        cost_estimate=pl.CostEstimate(
            flops=2 * blocks * channels * LANES * LANES,
            bytes_accessed=2 * weights.size + 20 * rows * LANES,
            transcendentals=0,
        ),
    )(*[pltpu.with_memory_space_constraint(value, pltpu.HBM) for value in (source, target, counts, cotangent, weights)])


def exchange(value, way, stage, devices):
    pairs = [(at, at ^ (1 << way[at % 2][stage])) for at in range(devices)]
    return lax.ppermute(value, "curve", pairs)


class Chain:
    def __init__(self, chunk, devices, pitch):
        self.chunk, self.devices = chunk, devices
        self.way = chunk[2]
        self.base = devices // 4 * chunk[0] * pitch
        self.length = devices // 4 * (chunk[1] - chunk[0]) * pitch

    def first(self, sums, got):
        self.terms = [(sums, 4 * self.base + 2 * self.length), (got, self.base)]
        self.total = self.part(0, self.length).astype(jnp.bfloat16)

    def part(self, low, high):
        return sum(term[base + low:base + high].astype(jnp.float32) for term, base in self.terms)

    def second(self):
        self.stage = 1
        self.got = exchange(self.total, self.way, self.stage, self.devices)

    def rest(self, sums, got):
        self.terms = [(sums, 4 * self.base), (got, self.base)]

    def send_next(self):
        self.terms = self.terms + [(self.got, 0)]
        self.stage += 1
        self.total = self.got
        if self.stage < BITS:
            half = self.length // 2
            self.total = self.part(half, self.length).astype(jnp.bfloat16)
            self.length = half
            self.got = exchange(self.total, self.way, self.stage, self.devices)
            if self.stage == BITS - 1:
                self.terms = [(self.part(0, half), 0)]


def final_kernel(channels, pitch, parts, *refs):
    out = refs[-1]
    at = 0
    for low, high, count in parts:
        terms = refs[at:at + count]
        at += count
        for tile in range(high - low):
            total = sum(
                term[tile * pitch:(tile + 1) * pitch, :].astype(jnp.float32) for term in terms
            )
            lane = (low + tile) * LANES
            out[0, :, lane:lane + LANES] = total[:channels].astype(jnp.bfloat16)


def final_sum(chains, like_shape, pitch):
    parts = [(chain.chunk[0], chain.chunk[1], len(chain.terms)) for chain in chains]
    flat, specs = [], []
    for chain in chains:
        rows = (chain.chunk[1] - chain.chunk[0]) * pitch
        for term, base in chain.terms:
            flat.append(term if base % rows == 0 else term[base:base + rows])
            at = base // rows if base % rows == 0 else 0
            specs.append(pl.BlockSpec((rows, LANES), lambda step, at=at: (at, 0)))
    return pl.pallas_call(
        functools.partial(final_kernel, like_shape[1], pitch, parts),
        out_shape=jax.ShapeDtypeStruct(like_shape, jnp.bfloat16),
        grid=(1,),
        in_specs=specs,
        out_specs=pl.BlockSpec(like_shape, lambda step: (0, 0, 0)),
        compiler_params=pltpu.CompilerParams(vmem_limit_bytes=24 * 1024 * 1024),
    )(*flat)


class Order:
    def __init__(self):
        self.last = ()

    def after(self, values):
        values, unused = lax.optimization_barrier((values, self.last))
        return values

    def before(self, values):
        self.last = values


def bit_remaps(remaps, devices):
    one, two = remaps
    pitch = round_up(one[-1][1], 8)
    tiles = one[-1][2] // LANES
    half, most, more = tiles // 2, tiles * 3 // 4, tiles * 5 // 6
    plans = (
        [(0, most, MIXED), (most, tiles, MIXED)],
        [(0, half, STRAIGHT), (half, more, STRAIGHT), (more, tiles, STRAIGHT)],
    )
    ones, twos = [[Chain(chunk, devices, pitch) for chunk in chunks] for chunks in plans]
    order = Order()

    def step(*chains):
        gots = order.after([chain.got for chain in chains])
        for chain, got in zip(chains, gots):
            chain.got = got
            chain.send_next()
        order.before([chain.total for chain in chains])

    def summed(line, sums, got):
        got = order.after(got)
        for chain in line:
            chain.first(sums, got)
        order.before([chain.total for chain in line])

    def rested(line, sums, got):
        got = order.after(got)
        order.before(got)
        for chain in line:
            chain.rest(sums, got)

    def begun(chain):
        chain.total = order.after(chain.total)
        chain.second()

    def cores(send):
        return exchange(send, STRAIGHT, 0, devices)

    a, b = ones
    c, d, e = twos

    sums, send, send_on = products(one, plans[0], devices)
    on, rest = cores(send_on), cores(send)
    summed(ones, sums, on)
    a.second()
    b.second()
    rested(ones, sums, rest)
    made = products((order.after(two[0]),) + two[1:], plans[1], devices)
    order.before(made)
    sums, send, send_on = made
    on, rest = cores(send_on), cores(send)

    step(a)
    step(b)
    summed(twos, sums, on)
    c.second()
    begun(d)
    step(a)
    step(b)
    rested(twos, sums, rest)
    step(c)
    begun(e)
    step(d)
    step(a)
    step(b)
    step(c)
    step(e)
    step(d)
    step(e)
    step(c)
    step(d)
    step(e)
    return [final_sum(line, remap[-1], pitch) for line, remap in zip((ones, twos), remaps)]


def on_device(devices, *args):
    latlon, healpix = args[:2]
    remaps = [
        (latlon, args[2], args[3], args[4], args[5], healpix.shape),
        (healpix, args[6], args[7], args[8], args[9], latlon.shape),
    ]
    tiles = max(latlon.shape[2], healpix.shape[2]) // LANES
    size = devices * tiles * round_up(latlon.shape[1], 8) * LANES * 4
    if devices == 1 << BITS and size <= ACC_LIMIT:
        return tuple(bit_remaps(remaps, devices))
    return tuple(slot_remap(*remap) for remap in remaps)


def solution(mesh):
    in_specs = (
        P("groups", None, "curve"),
        P("groups", None, "curve"),
        P("curve", None, None),
        P("curve"),
        P("curve"),
        P("curve", None),
        P("curve", None, None),
        P("curve"),
        P("curve"),
        P("curve", None),
    )
    out_specs = (P("groups", None, "curve"), P("groups", None, "curve"))
    return jax.shard_map(
        functools.partial(on_device, mesh.shape["curve"]),
        mesh=mesh, in_specs=in_specs, out_specs=out_specs, check_vma=False,
    )
```

```python
import functools

import jax
import jax.numpy as jnp
from jax import lax
from jax.experimental import pallas as pl
from jax.experimental.pallas import tpu as pltpu
from jax.sharding import PartitionSpec as P

LANES = 128
ACC_LIMIT = 16 * 1024 * 1024


def round_up(value, unit):
    return -(-value // unit) * unit


def block_products(cotangent, weights, source):
    width = weights.shape[1]
    lead = cotangent.shape[0] * cotangent.shape[1]
    tiled = cotangent.reshape(lead, cotangent.shape[2] // width, width)
    picked = jnp.take(tiled, source, axis=1)
    products = jnp.einsum("kbi,bij->bkj", picked, weights, preferred_element_type=jnp.float32)
    return products.astype(jnp.bfloat16)


def pack_slots(products, target, count_row):
    blocks = products.shape[0]
    devices = count_row.shape[0]
    per_device = 2 * blocks // devices
    inclusive = jnp.cumsum(count_row)
    exclusive = inclusive - count_row
    positions = jnp.arange(blocks, dtype=jnp.int32)
    owner = jnp.sum((positions[:, None] >= inclusive[None, :]).astype(jnp.int32), axis=1)
    chosen = owner[:, None] == jnp.arange(devices, dtype=jnp.int32)[None, :]
    first = jnp.sum(jnp.where(chosen, exclusive[None, :], 0), axis=1)
    slot_index = owner * per_device + positions - first
    buffer = (
        jnp.zeros((devices * per_device,) + products.shape[1:], jnp.bfloat16)
        .at[slot_index]
        .set(products)
    )
    labels = jnp.full((devices * per_device,), -1, jnp.int32).at[slot_index].set(target)
    return (buffer, labels)


def sum_slots(received, labels, tiles_out, like_shape):
    selector = (labels[None, :] == jnp.arange(tiles_out, dtype=jnp.int32)[:, None]).astype(
        jnp.bfloat16
    )
    summed = jnp.einsum("ts,skc->ktc", selector, received, preferred_element_type=jnp.float32)
    return summed.reshape(like_shape[0], like_shape[1], -1).astype(jnp.bfloat16)


def slot_remap(cotangent, weights, source, target, counts, like_shape):
    products = block_products(cotangent, weights, source)
    buffer, labels = pack_slots(products, target, counts[0])
    arrived = lax.all_to_all(buffer, "curve", split_axis=0, concat_axis=0, tiled=True)
    arrived_labels = lax.all_to_all(labels, "curve", split_axis=0, concat_axis=0, tiled=True)
    return sum_slots(arrived, arrived_labels, like_shape[2] // weights.shape[1], like_shape)


STRAIGHT = ((0, 1, 2, 3), (0, 1, 2, 3))
MIXED = ((0, 1, 2, 3), (0, 2, 1, 3))
BITS = 4


def product_kernel(
    channels, pitch, chunks, step_blocks,
    source_hbm, target_hbm, counts_hbm, x_hbm, w_hbm, *rest,
):
    number = len(chunks)
    acc, send, send_on, xs, x_in, w, source, target, counts, places, sems = rest
    devices = counts.shape[1]
    steps = w.shape[0] // step_blocks
    me = lax.axis_index("curve")

    scalars = [
        pltpu.make_async_copy(source_hbm, source, sems.at[0]),
        pltpu.make_async_copy(target_hbm, target, sems.at[1]),
        pltpu.make_async_copy(counts_hbm, counts, sems.at[2]),
    ]
    x_copy = pltpu.make_async_copy(x_hbm, x_in, sems.at[3])

    def w_copy(step):
        at = pl.ds(step * step_blocks, step_blocks)
        return pltpu.make_async_copy(w_hbm.at[at], w.at[at], sems.at[4 + step])

    for copy in scalars + [x_copy]:
        copy.start()
    for step in range(steps):
        w_copy(step).start()

    @pl.loop(0, acc.shape[0] // pitch)
    def clear(index):
        acc[pl.ds(pl.multiple_of(index * pitch, pitch), pitch), :] = jnp.zeros((pitch, LANES), jnp.float32)

    for tile in range(xs.shape[0]):
        xs[tile] = jnp.zeros(xs.shape[1:], xs.dtype)

    for owner in range(devices):
        differ = jnp.bitwise_xor(me, owner)
        found = {}
        for chunk, (low, high, way) in enumerate(chunks):
            first, second, *others = way[owner % 2]
            key = (second, first, *others)
            if key not in found:
                place = jnp.int32(0)
                for bit in key:
                    place = place * 2 + jnp.bitwise_and(jnp.right_shift(differ, bit), 1)
                found[key] = place
            places[chunk, owner] = devices * low + found[key] * (high - low) - low

    x_copy.wait()
    for tile in range(xs.shape[0]):
        xs[tile, :channels, :] = x_in[0, :, tile * LANES:(tile + 1) * LANES]
    for copy in scalars:
        copy.wait()

    def some(step, carry):
        owner, end = carry
        w_copy(step).wait()
        rows = []
        for index in range(step_blocks):
            block = step * step_blocks + index
            passed = (block >= end).astype(jnp.int32)
            owner = jnp.minimum(owner + passed, devices - 1)
            end = end + passed * counts[0, owner]
            tile = target[block]
            place = places[0, owner]
            for chunk in range(1, number):
                place = jnp.where(tile >= chunks[chunk][0], places[chunk, owner], place)
            rows.append(pl.multiple_of((place + tile) * pitch, 8))
        for index, row in enumerate(rows):
            block = step * step_blocks + index
            product = jnp.dot(xs[source[block], :pitch, :], w[block], preferred_element_type=jnp.float32)
            acc[pl.ds(row, pitch), :] += product
        return owner, end

    lax.fori_loop(0, steps, some, (jnp.int32(0), counts[0, 0]))

    quarter = devices // 4
    for low, high, way in chunks:
        unit = (high - low) * pitch

        @pl.loop(0, quarter)
        def finish(index):
            at = pl.multiple_of(quarter * low * pitch + index * unit, 8)
            row = pl.multiple_of((devices * low + quarter * (high - low)) * pitch + index * unit, 8)
            send[pl.ds(at, unit), :] = acc[pl.ds(row, unit), :].astype(send.dtype)
            row = pl.multiple_of(row + 2 * quarter * unit, 8)
            send_on[pl.ds(at, unit), :] = acc[pl.ds(row, unit), :].astype(send.dtype)


def products(remap, chunks, devices):
    cotangent, weights, source, target, counts = remap[:5]
    channels = cotangent.shape[1]
    pitch = round_up(channels, 8)
    tiles_in = cotangent.shape[2] // LANES
    blocks = weights.shape[0]
    step_blocks = max(size for size in range(1, 17) if blocks % size == 0)
    rows = devices // 4 * chunks[-1][1] * pitch
    return pl.pallas_call(
        functools.partial(product_kernel, channels, pitch, chunks, step_blocks),
        out_shape=[
            jax.ShapeDtypeStruct((4 * rows, LANES), jnp.float32),
            jax.ShapeDtypeStruct((rows, LANES), jnp.bfloat16),
            jax.ShapeDtypeStruct((rows, LANES), jnp.bfloat16),
        ],
        in_specs=[pl.BlockSpec(memory_space=pltpu.HBM)] * 5,
        out_specs=[pl.BlockSpec(memory_space=pltpu.VMEM)] * 3,
        scratch_shapes=[
            pltpu.VMEM((tiles_in, round_up(pitch, 16), LANES), jnp.bfloat16),
            pltpu.VMEM(cotangent.shape, jnp.bfloat16),
            pltpu.VMEM(weights.shape, jnp.bfloat16),
            pltpu.SMEM(source.shape, jnp.int32),
            pltpu.SMEM(target.shape, jnp.int32),
            pltpu.SMEM(counts.shape, jnp.int32),
            pltpu.SMEM((len(chunks), devices), jnp.int32),
            pltpu.SemaphoreType.DMA((4 + blocks // step_blocks,)),
        ],
        compiler_params=pltpu.CompilerParams(vmem_limit_bytes=24 * 1024 * 1024),
        cost_estimate=pl.CostEstimate(
            flops=2 * blocks * channels * LANES * LANES,
            bytes_accessed=2 * weights.size + 20 * rows * LANES,
            transcendentals=0,
        ),
    )(*[pltpu.with_memory_space_constraint(value, pltpu.HBM) for value in (source, target, counts, cotangent, weights)])


def exchange(value, way, stage, devices):
    pairs = [(at, at ^ (1 << way[at % 2][stage])) for at in range(devices)]
    return lax.ppermute(value, "curve", pairs)


class Chain:
    def __init__(self, chunk, devices, pitch):
        self.chunk, self.devices = chunk, devices
        self.way = chunk[2]
        self.base = devices // 4 * chunk[0] * pitch
        self.length = devices // 4 * (chunk[1] - chunk[0]) * pitch

    def first(self, sums, got):
        self.terms = [(sums, 4 * self.base + 2 * self.length), (got, self.base)]
        self.total = self.part(0, self.length).astype(jnp.bfloat16)

    def part(self, low, high):
        return sum(term[base + low:base + high].astype(jnp.float32) for term, base in self.terms)

    def second(self):
        self.stage = 1
        self.got = exchange(self.total, self.way, self.stage, self.devices)

    def rest(self, sums, got):
        self.terms = [(sums, 4 * self.base), (got, self.base)]

    def send_next(self):
        self.terms = self.terms + [(self.got, 0)]
        self.stage += 1
        self.total = self.got
        if self.stage < BITS:
            half = self.length // 2
            self.total = self.part(half, self.length).astype(jnp.bfloat16)
            self.length = half
            self.got = exchange(self.total, self.way, self.stage, self.devices)
            if self.stage == BITS - 1:
                self.terms = [(self.part(0, half), 0)]


def final_kernel(channels, pitch, parts, *refs):
    out = refs[-1]
    at = 0
    for low, high, count in parts:
        terms = refs[at:at + count]
        at += count
        for tile in range(high - low):
            total = sum(
                term[tile * pitch:(tile + 1) * pitch, :].astype(jnp.float32) for term in terms
            )
            lane = (low + tile) * LANES
            out[0, :, lane:lane + LANES] = total[:channels].astype(jnp.bfloat16)


def final_sum(chains, like_shape, pitch):
    parts = [(chain.chunk[0], chain.chunk[1], len(chain.terms)) for chain in chains]
    flat, specs = [], []
    for chain in chains:
        rows = (chain.chunk[1] - chain.chunk[0]) * pitch
        for term, base in chain.terms:
            flat.append(term if base % rows == 0 else term[base:base + rows])
            at = base // rows if base % rows == 0 else 0
            specs.append(pl.BlockSpec((rows, LANES), lambda step, at=at: (at, 0)))
    return pl.pallas_call(
        functools.partial(final_kernel, like_shape[1], pitch, parts),
        out_shape=jax.ShapeDtypeStruct(like_shape, jnp.bfloat16),
        grid=(1,),
        in_specs=specs,
        out_specs=pl.BlockSpec(like_shape, lambda step: (0, 0, 0)),
        compiler_params=pltpu.CompilerParams(vmem_limit_bytes=24 * 1024 * 1024),
    )(*flat)


class Order:
    def __init__(self):
        self.last = ()

    def after(self, values):
        values, unused = lax.optimization_barrier((values, self.last))
        return values

    def before(self, values):
        self.last = values


def bit_remaps(remaps, devices):
    one, two = remaps
    pitch = round_up(one[-1][1], 8)
    tiles = one[-1][2] // LANES
    some, most = tiles * 5 // 12, tiles * 3 // 4
    plans = (
        [(0, most, MIXED), (most, tiles, MIXED)],
        [(0, some, MIXED), (some, most, STRAIGHT), (most, tiles, STRAIGHT)],
    )
    ones, twos = [[Chain(chunk, devices, pitch) for chunk in chunks] for chunks in plans]
    order = Order()

    def step(*chains):
        gots = order.after([chain.got for chain in chains])
        for chain, got in zip(chains, gots):
            chain.got = got
            chain.send_next()
        order.before([chain.total for chain in chains])

    def summed(line, sums, got):
        got = order.after(got)
        for chain in line:
            chain.first(sums, got)
        order.before([chain.total for chain in line])

    def rested(line, sums, got):
        got = order.after(got)
        order.before(got)
        for chain in line:
            chain.rest(sums, got)

    def begun(chain):
        chain.total = order.after(chain.total)
        chain.second()

    def cores(send):
        return exchange(send, STRAIGHT, 0, devices)

    a, b = ones
    c, d, e = twos

    sums, send, send_on = products(one, plans[0], devices)
    on, rest = cores(send_on), cores(send)
    summed(ones, sums, on)
    a.second()
    b.second()
    rested(ones, sums, rest)
    made = products((order.after(two[0]),) + two[1:], plans[1], devices)
    order.before(made)
    sums, send, send_on = made
    on, rest = cores(send_on), cores(send)

    step(a)
    step(b)
    summed(twos, sums, on)
    c.second()
    begun(d)
    step(a)
    step(b)
    rested(twos, sums, rest)
    step(c)
    begun(e)
    step(d)
    step(b)
    step(c)
    step(a)
    step(e)
    step(d)
    step(e)
    step(c)
    step(d)
    step(e)
    return [final_sum(line, remap[-1], pitch) for line, remap in zip((ones, twos), remaps)]


def on_device(devices, *args):
    latlon, healpix = args[:2]
    remaps = [
        (latlon, args[2], args[3], args[4], args[5], healpix.shape),
        (healpix, args[6], args[7], args[8], args[9], latlon.shape),
    ]
    tiles = max(latlon.shape[2], healpix.shape[2]) // LANES
    size = devices * tiles * round_up(latlon.shape[1], 8) * LANES * 4
    if devices == 1 << BITS and size <= ACC_LIMIT:
        return tuple(bit_remaps(remaps, devices))
    return tuple(slot_remap(*remap) for remap in remaps)


def solution(mesh):
    in_specs = (
        P("groups", None, "curve"),
        P("groups", None, "curve"),
        P("curve", None, None),
        P("curve"),
        P("curve"),
        P("curve", None),
        P("curve", None, None),
        P("curve"),
        P("curve"),
        P("curve", None),
    )
    out_specs = (P("groups", None, "curve"), P("groups", None, "curve"))
    return jax.shard_map(
        functools.partial(on_device, mesh.shape["curve"]),
        mesh=mesh, in_specs=in_specs, out_specs=out_specs, check_vma=False,
    )
```

```python
import functools

import jax
import jax.numpy as jnp
from jax import lax
from jax.experimental import pallas as pl
from jax.experimental.pallas import tpu as pltpu
from jax.sharding import PartitionSpec as P

LANES = 128
ACC_LIMIT = 16 * 1024 * 1024


def round_up(value, unit):
    return -(-value // unit) * unit


def block_products(cotangent, weights, source):
    width = weights.shape[1]
    lead = cotangent.shape[0] * cotangent.shape[1]
    tiled = cotangent.reshape(lead, cotangent.shape[2] // width, width)
    picked = jnp.take(tiled, source, axis=1)
    products = jnp.einsum("kbi,bij->bkj", picked, weights, preferred_element_type=jnp.float32)
    return products.astype(jnp.bfloat16)


def pack_slots(products, target, count_row):
    blocks = products.shape[0]
    devices = count_row.shape[0]
    per_device = 2 * blocks // devices
    inclusive = jnp.cumsum(count_row)
    exclusive = inclusive - count_row
    positions = jnp.arange(blocks, dtype=jnp.int32)
    owner = jnp.sum((positions[:, None] >= inclusive[None, :]).astype(jnp.int32), axis=1)
    chosen = owner[:, None] == jnp.arange(devices, dtype=jnp.int32)[None, :]
    first = jnp.sum(jnp.where(chosen, exclusive[None, :], 0), axis=1)
    slot_index = owner * per_device + positions - first
    buffer = (
        jnp.zeros((devices * per_device,) + products.shape[1:], jnp.bfloat16)
        .at[slot_index]
        .set(products)
    )
    labels = jnp.full((devices * per_device,), -1, jnp.int32).at[slot_index].set(target)
    return (buffer, labels)


def sum_slots(received, labels, tiles_out, like_shape):
    selector = (labels[None, :] == jnp.arange(tiles_out, dtype=jnp.int32)[:, None]).astype(
        jnp.bfloat16
    )
    summed = jnp.einsum("ts,skc->ktc", selector, received, preferred_element_type=jnp.float32)
    return summed.reshape(like_shape[0], like_shape[1], -1).astype(jnp.bfloat16)


def slot_remap(cotangent, weights, source, target, counts, like_shape):
    products = block_products(cotangent, weights, source)
    buffer, labels = pack_slots(products, target, counts[0])
    arrived = lax.all_to_all(buffer, "curve", split_axis=0, concat_axis=0, tiled=True)
    arrived_labels = lax.all_to_all(labels, "curve", split_axis=0, concat_axis=0, tiled=True)
    return sum_slots(arrived, arrived_labels, like_shape[2] // weights.shape[1], like_shape)


STRAIGHT = ((0, 1, 2, 3), (0, 1, 2, 3))
MIXED = ((0, 2, 1, 3), (0, 1, 2, 3))
BITS = 4


def product_kernel(
    channels, pitch, chunks, step_blocks,
    source_hbm, target_hbm, counts_hbm, x_hbm, w_hbm, *rest,
):
    number = len(chunks)
    acc, send, send_on, xs, x_in, w, source, target, counts, places, sems = rest
    devices = counts.shape[1]
    steps = w.shape[0] // step_blocks
    me = lax.axis_index("curve")

    scalars = [
        pltpu.make_async_copy(source_hbm, source, sems.at[0]),
        pltpu.make_async_copy(target_hbm, target, sems.at[1]),
        pltpu.make_async_copy(counts_hbm, counts, sems.at[2]),
    ]
    x_copy = pltpu.make_async_copy(x_hbm, x_in, sems.at[3])

    def w_copy(step):
        at = pl.ds(step * step_blocks, step_blocks)
        return pltpu.make_async_copy(w_hbm.at[at], w.at[at], sems.at[4 + step])

    for copy in scalars + [x_copy]:
        copy.start()
    for step in range(steps):
        w_copy(step).start()

    @pl.loop(0, acc.shape[0] // pitch)
    def clear(index):
        acc[pl.ds(pl.multiple_of(index * pitch, pitch), pitch), :] = jnp.zeros((pitch, LANES), jnp.float32)

    for tile in range(xs.shape[0]):
        xs[tile] = jnp.zeros(xs.shape[1:], xs.dtype)

    for owner in range(devices):
        differ = jnp.bitwise_xor(me, owner)
        found = {}
        for chunk, (low, high, way) in enumerate(chunks):
            first, second, *others = way[owner % 2]
            key = (second, first, *others)
            if key not in found:
                place = jnp.int32(0)
                for bit in key:
                    place = place * 2 + jnp.bitwise_and(jnp.right_shift(differ, bit), 1)
                found[key] = place
            places[chunk, owner] = devices * low + found[key] * (high - low) - low

    x_copy.wait()
    for tile in range(xs.shape[0]):
        xs[tile, :channels, :] = x_in[0, :, tile * LANES:(tile + 1) * LANES]
    for copy in scalars:
        copy.wait()

    def some(step, carry):
        owner, end = carry
        w_copy(step).wait()
        rows = []
        for index in range(step_blocks):
            block = step * step_blocks + index
            passed = (block >= end).astype(jnp.int32)
            owner = jnp.minimum(owner + passed, devices - 1)
            end = end + passed * counts[0, owner]
            tile = target[block]
            place = places[0, owner]
            for chunk in range(1, number):
                place = jnp.where(tile >= chunks[chunk][0], places[chunk, owner], place)
            rows.append(pl.multiple_of((place + tile) * pitch, 8))
        for index, row in enumerate(rows):
            block = step * step_blocks + index
            product = jnp.dot(xs[source[block], :pitch, :], w[block], preferred_element_type=jnp.float32)
            acc[pl.ds(row, pitch), :] += product
        return owner, end

    lax.fori_loop(0, steps, some, (jnp.int32(0), counts[0, 0]))

    quarter = devices // 4
    for low, high, way in chunks:
        unit = (high - low) * pitch

        @pl.loop(0, quarter)
        def finish(index):
            at = pl.multiple_of(quarter * low * pitch + index * unit, 8)
            row = pl.multiple_of((devices * low + quarter * (high - low)) * pitch + index * unit, 8)
            send[pl.ds(at, unit), :] = acc[pl.ds(row, unit), :].astype(send.dtype)
            row = pl.multiple_of(row + 2 * quarter * unit, 8)
            send_on[pl.ds(at, unit), :] = acc[pl.ds(row, unit), :].astype(send.dtype)


def products(remap, chunks, devices):
    cotangent, weights, source, target, counts = remap[:5]
    channels = cotangent.shape[1]
    pitch = round_up(channels, 8)
    tiles_in = cotangent.shape[2] // LANES
    blocks = weights.shape[0]
    step_blocks = max(size for size in range(1, 17) if blocks % size == 0)
    rows = devices // 4 * chunks[-1][1] * pitch
    return pl.pallas_call(
        functools.partial(product_kernel, channels, pitch, chunks, step_blocks),
        out_shape=[
            jax.ShapeDtypeStruct((4 * rows, LANES), jnp.float32),
            jax.ShapeDtypeStruct((rows, LANES), jnp.bfloat16),
            jax.ShapeDtypeStruct((rows, LANES), jnp.bfloat16),
        ],
        in_specs=[pl.BlockSpec(memory_space=pltpu.HBM)] * 5,
        out_specs=[pl.BlockSpec(memory_space=pltpu.VMEM)] * 3,
        scratch_shapes=[
            pltpu.VMEM((tiles_in, round_up(pitch, 16), LANES), jnp.bfloat16),
            pltpu.VMEM(cotangent.shape, jnp.bfloat16),
            pltpu.VMEM(weights.shape, jnp.bfloat16),
            pltpu.SMEM(source.shape, jnp.int32),
            pltpu.SMEM(target.shape, jnp.int32),
            pltpu.SMEM(counts.shape, jnp.int32),
            pltpu.SMEM((len(chunks), devices), jnp.int32),
            pltpu.SemaphoreType.DMA((4 + blocks // step_blocks,)),
        ],
        compiler_params=pltpu.CompilerParams(vmem_limit_bytes=24 * 1024 * 1024),
        cost_estimate=pl.CostEstimate(
            flops=2 * blocks * channels * LANES * LANES,
            bytes_accessed=2 * weights.size + 20 * rows * LANES,
            transcendentals=0,
        ),
    )(*[pltpu.with_memory_space_constraint(value, pltpu.HBM) for value in (source, target, counts, cotangent, weights)])


def exchange(value, way, stage, devices):
    pairs = [(at, at ^ (1 << way[at % 2][stage])) for at in range(devices)]
    return lax.ppermute(value, "curve", pairs)


class Chain:
    def __init__(self, chunk, devices, pitch):
        self.chunk, self.devices = chunk, devices
        self.way = chunk[2]
        self.base = devices // 4 * chunk[0] * pitch
        self.length = devices // 4 * (chunk[1] - chunk[0]) * pitch

    def first(self, sums, got):
        self.terms = [(sums, 4 * self.base + 2 * self.length), (got, self.base)]
        self.total = self.part(0, self.length).astype(jnp.bfloat16)

    def part(self, low, high):
        return sum(term[base + low:base + high].astype(jnp.float32) for term, base in self.terms)

    def second(self):
        self.stage = 1
        self.got = exchange(self.total, self.way, self.stage, self.devices)

    def rest(self, sums, got):
        self.terms = [(sums, 4 * self.base), (got, self.base)]

    def send_next(self):
        self.terms = self.terms + [(self.got, 0)]
        self.stage += 1
        self.total = self.got
        if self.stage < BITS:
            half = self.length // 2
            self.total = self.part(half, self.length).astype(jnp.bfloat16)
            self.length = half
            self.got = exchange(self.total, self.way, self.stage, self.devices)
            if self.stage == BITS - 1:
                self.terms = [(self.part(0, half), 0)]


def final_kernel(channels, pitch, parts, *refs):
    out = refs[-1]
    at = 0
    for low, high, count in parts:
        terms = refs[at:at + count]
        at += count
        for tile in range(high - low):
            total = sum(
                term[tile * pitch:(tile + 1) * pitch, :].astype(jnp.float32) for term in terms
            )
            lane = (low + tile) * LANES
            out[0, :, lane:lane + LANES] = total[:channels].astype(jnp.bfloat16)


def final_sum(chains, like_shape, pitch):
    parts = [(chain.chunk[0], chain.chunk[1], len(chain.terms)) for chain in chains]
    flat = [term for chain in chains for term, base in chain.terms]
    return pl.pallas_call(
        functools.partial(final_kernel, like_shape[1], pitch, parts),
        out_shape=jax.ShapeDtypeStruct(like_shape, jnp.bfloat16),
        in_specs=[pl.BlockSpec(memory_space=pltpu.VMEM)] * len(flat),
        out_specs=pl.BlockSpec(memory_space=pltpu.VMEM),
        compiler_params=pltpu.CompilerParams(vmem_limit_bytes=24 * 1024 * 1024),
    )(*flat)


class Order:
    def __init__(self):
        self.last = ()

    def after(self, values):
        values, unused = lax.optimization_barrier((values, self.last))
        return values

    def before(self, values):
        self.last = values


def bit_remaps(remaps, devices):
    one, two = remaps
    pitch = round_up(one[-1][1], 8)
    tiles = one[-1][2] // LANES
    some, most = tiles * 5 // 12, tiles * 3 // 4
    plans = (
        [(0, most, MIXED), (most, tiles, MIXED)],
        [(0, some, MIXED), (some, most, STRAIGHT), (most, tiles, STRAIGHT)],
    )
    ones, twos = [[Chain(chunk, devices, pitch) for chunk in chunks] for chunks in plans]
    order = Order()

    def step(*chains):
        gots = order.after([chain.got for chain in chains])
        for chain, got in zip(chains, gots):
            chain.got = got
            chain.send_next()
        order.before([chain.total for chain in chains])

    def summed(line, sums, got):
        got = order.after(got)
        for chain in line:
            chain.first(sums, got)
        order.before([chain.total for chain in line])

    def rested(line, sums, got):
        got = order.after(got)
        order.before(got)
        for chain in line:
            chain.rest(sums, got)

    def begun(chain):
        chain.total = order.after(chain.total)
        chain.second()

    def cores(send):
        return exchange(send, STRAIGHT, 0, devices)

    a, b = ones
    c, d, e = twos

    sums, send, send_on = products(one, plans[0], devices)
    on, rest = cores(send_on), cores(send)
    summed(ones, sums, on)
    a.second()
    b.second()
    rested(ones, sums, rest)
    made = products((order.after(two[0]),) + two[1:], plans[1], devices)
    order.before(made)
    sums, send, send_on = made
    on, rest = cores(send_on), cores(send)

    step(a)
    step(b)
    summed(twos, sums, on)
    c.second()
    begun(d)
    step(a)
    step(b)
    rested(twos, sums, rest)
    step(c)
    begun(e)
    step(d)
    step(c)
    step(e)
    step(b)
    step(d)
    step(a)
    step(e)
    step(*twos)
    return [final_sum(line, remap[-1], pitch) for line, remap in zip((ones, twos), remaps)]


def on_device(devices, *args):
    latlon, healpix = args[:2]
    remaps = [
        (latlon, args[2], args[3], args[4], args[5], healpix.shape),
        (healpix, args[6], args[7], args[8], args[9], latlon.shape),
    ]
    tiles = max(latlon.shape[2], healpix.shape[2]) // LANES
    size = devices * tiles * round_up(latlon.shape[1], 8) * LANES * 4
    if devices == 1 << BITS and size <= ACC_LIMIT:
        return tuple(bit_remaps(remaps, devices))
    return tuple(slot_remap(*remap) for remap in remaps)


def solution(mesh):
    in_specs = (
        P("groups", None, "curve"),
        P("groups", None, "curve"),
        P("curve", None, None),
        P("curve"),
        P("curve"),
        P("curve", None),
        P("curve", None, None),
        P("curve"),
        P("curve"),
        P("curve", None),
    )
    out_specs = (P("groups", None, "curve"), P("groups", None, "curve"))
    return jax.shard_map(
        functools.partial(on_device, mesh.shape["curve"]),
        mesh=mesh, in_specs=in_specs, out_specs=out_specs, check_vma=False,
    )
```

```python
import functools

import jax
import jax.numpy as jnp
from jax import lax
from jax.experimental import pallas as pl
from jax.experimental.pallas import tpu as pltpu
from jax.sharding import PartitionSpec as P

LANES = 128
ACC_LIMIT = 16 * 1024 * 1024


def round_up(value, unit):
    return -(-value // unit) * unit


def block_products(cotangent, weights, source):
    width = weights.shape[1]
    lead = cotangent.shape[0] * cotangent.shape[1]
    tiled = cotangent.reshape(lead, cotangent.shape[2] // width, width)
    picked = jnp.take(tiled, source, axis=1)
    products = jnp.einsum("kbi,bij->bkj", picked, weights, preferred_element_type=jnp.float32)
    return products.astype(jnp.bfloat16)


def pack_slots(products, target, count_row):
    blocks = products.shape[0]
    devices = count_row.shape[0]
    per_device = 2 * blocks // devices
    inclusive = jnp.cumsum(count_row)
    exclusive = inclusive - count_row
    positions = jnp.arange(blocks, dtype=jnp.int32)
    owner = jnp.sum((positions[:, None] >= inclusive[None, :]).astype(jnp.int32), axis=1)
    chosen = owner[:, None] == jnp.arange(devices, dtype=jnp.int32)[None, :]
    first = jnp.sum(jnp.where(chosen, exclusive[None, :], 0), axis=1)
    slot_index = owner * per_device + positions - first
    buffer = (
        jnp.zeros((devices * per_device,) + products.shape[1:], jnp.bfloat16)
        .at[slot_index]
        .set(products)
    )
    labels = jnp.full((devices * per_device,), -1, jnp.int32).at[slot_index].set(target)
    return (buffer, labels)


def sum_slots(received, labels, tiles_out, like_shape):
    selector = (labels[None, :] == jnp.arange(tiles_out, dtype=jnp.int32)[:, None]).astype(
        jnp.bfloat16
    )
    summed = jnp.einsum("ts,skc->ktc", selector, received, preferred_element_type=jnp.float32)
    return summed.reshape(like_shape[0], like_shape[1], -1).astype(jnp.bfloat16)


def slot_remap(cotangent, weights, source, target, counts, like_shape):
    products = block_products(cotangent, weights, source)
    buffer, labels = pack_slots(products, target, counts[0])
    arrived = lax.all_to_all(buffer, "curve", split_axis=0, concat_axis=0, tiled=True)
    arrived_labels = lax.all_to_all(labels, "curve", split_axis=0, concat_axis=0, tiled=True)
    return sum_slots(arrived, arrived_labels, like_shape[2] // weights.shape[1], like_shape)


STRAIGHT = ((0, 1, 2, 3), (0, 1, 2, 3))
MIXED = ((0, 2, 1, 3), (0, 1, 2, 3))
BITS = 4


def product_kernel(
    channels, pitch, chunks, step_blocks,
    source_hbm, target_hbm, counts_hbm, x_hbm, w_hbm, *rest,
):
    number = len(chunks)
    acc, send, send_on, xs, x_in, w, source, target, counts, places, sems = rest
    devices = counts.shape[1]
    steps = w.shape[0] // step_blocks
    me = lax.axis_index("curve")

    scalars = [
        pltpu.make_async_copy(source_hbm, source, sems.at[0]),
        pltpu.make_async_copy(target_hbm, target, sems.at[1]),
        pltpu.make_async_copy(counts_hbm, counts, sems.at[2]),
    ]
    x_copy = pltpu.make_async_copy(x_hbm, x_in, sems.at[3])

    def w_copy(step):
        at = pl.ds(step * step_blocks, step_blocks)
        return pltpu.make_async_copy(w_hbm.at[at], w.at[at], sems.at[4 + step])

    for copy in scalars + [x_copy]:
        copy.start()
    for step in range(steps):
        w_copy(step).start()

    @pl.loop(0, acc.shape[0] // pitch)
    def clear(index):
        acc[pl.ds(pl.multiple_of(index * pitch, pitch), pitch), :] = jnp.zeros((pitch, LANES), jnp.float32)

    for tile in range(xs.shape[0]):
        xs[tile] = jnp.zeros(xs.shape[1:], xs.dtype)

    for owner in range(devices):
        differ = jnp.bitwise_xor(me, owner)
        found = {}
        for chunk, (low, high, way) in enumerate(chunks):
            first, second, *others = way[owner % 2]
            key = (second, first, *others)
            if key not in found:
                place = jnp.int32(0)
                for bit in key:
                    place = place * 2 + jnp.bitwise_and(jnp.right_shift(differ, bit), 1)
                found[key] = place
            places[chunk, owner] = devices * low + found[key] * (high - low) - low

    x_copy.wait()
    for tile in range(xs.shape[0]):
        xs[tile, :channels, :] = x_in[0, :, tile * LANES:(tile + 1) * LANES]
    for copy in scalars:
        copy.wait()

    def some(step, carry):
        owner, end = carry
        w_copy(step).wait()
        rows = []
        for index in range(step_blocks):
            block = step * step_blocks + index
            passed = (block >= end).astype(jnp.int32)
            owner = jnp.minimum(owner + passed, devices - 1)
            end = end + passed * counts[0, owner]
            tile = target[block]
            place = places[0, owner]
            for chunk in range(1, number):
                place = jnp.where(tile >= chunks[chunk][0], places[chunk, owner], place)
            rows.append(pl.multiple_of((place + tile) * pitch, 8))
        for index, row in enumerate(rows):
            block = step * step_blocks + index
            product = jnp.dot(xs[source[block], :pitch, :], w[block], preferred_element_type=jnp.float32)
            acc[pl.ds(row, pitch), :] += product
        return owner, end

    lax.fori_loop(0, steps, some, (jnp.int32(0), counts[0, 0]))

    quarter = devices // 4
    for low, high, way in chunks:
        unit = (high - low) * pitch

        @pl.loop(0, quarter)
        def finish(index):
            at = pl.multiple_of(quarter * low * pitch + index * unit, 8)
            row = pl.multiple_of((devices * low + quarter * (high - low)) * pitch + index * unit, 8)
            send[pl.ds(at, unit), :] = acc[pl.ds(row, unit), :].astype(send.dtype)
            row = pl.multiple_of(row + 2 * quarter * unit, 8)
            send_on[pl.ds(at, unit), :] = acc[pl.ds(row, unit), :].astype(send.dtype)


def products(remap, chunks, devices):
    cotangent, weights, source, target, counts = remap[:5]
    channels = cotangent.shape[1]
    pitch = round_up(channels, 8)
    tiles_in = cotangent.shape[2] // LANES
    blocks = weights.shape[0]
    step_blocks = max(size for size in range(1, 17) if blocks % size == 0)
    rows = devices // 4 * chunks[-1][1] * pitch
    return pl.pallas_call(
        functools.partial(product_kernel, channels, pitch, chunks, step_blocks),
        out_shape=[
            jax.ShapeDtypeStruct((4 * rows, LANES), jnp.float32),
            jax.ShapeDtypeStruct((rows, LANES), jnp.bfloat16),
            jax.ShapeDtypeStruct((rows, LANES), jnp.bfloat16),
        ],
        in_specs=[pl.BlockSpec(memory_space=pltpu.HBM)] * 5,
        out_specs=[pl.BlockSpec(memory_space=pltpu.VMEM)] * 3,
        scratch_shapes=[
            pltpu.VMEM((tiles_in, round_up(pitch, 16), LANES), jnp.bfloat16),
            pltpu.VMEM(cotangent.shape, jnp.bfloat16),
            pltpu.VMEM(weights.shape, jnp.bfloat16),
            pltpu.SMEM(source.shape, jnp.int32),
            pltpu.SMEM(target.shape, jnp.int32),
            pltpu.SMEM(counts.shape, jnp.int32),
            pltpu.SMEM((len(chunks), devices), jnp.int32),
            pltpu.SemaphoreType.DMA((4 + blocks // step_blocks,)),
        ],
        compiler_params=pltpu.CompilerParams(vmem_limit_bytes=24 * 1024 * 1024),
        cost_estimate=pl.CostEstimate(
            flops=2 * blocks * channels * LANES * LANES,
            bytes_accessed=2 * weights.size + 20 * rows * LANES,
            transcendentals=0,
        ),
    )(*[pltpu.with_memory_space_constraint(value, pltpu.HBM) for value in (source, target, counts, cotangent, weights)])


def exchange(value, way, stage, devices):
    pairs = [(at, at ^ (1 << way[at % 2][stage])) for at in range(devices)]
    return lax.ppermute(value, "curve", pairs)


class Chain:
    def __init__(self, chunk, devices, pitch):
        self.chunk, self.devices = chunk, devices
        self.way = chunk[2]
        self.base = devices // 4 * chunk[0] * pitch
        self.length = devices // 4 * (chunk[1] - chunk[0]) * pitch

    def first(self, sums, got):
        self.terms = [(sums, 4 * self.base + 2 * self.length), (got, self.base)]
        self.total = self.part(0, self.length).astype(jnp.bfloat16)

    def part(self, low, high):
        return sum(term[base + low:base + high].astype(jnp.float32) for term, base in self.terms)

    def second(self):
        self.stage = 1
        self.got = exchange(self.total, self.way, self.stage, self.devices)

    def rest(self, sums, got):
        self.terms = [(sums, 4 * self.base), (got, self.base)]

    def send_next(self):
        self.terms = self.terms + [(self.got, 0)]
        self.stage += 1
        self.total = self.got
        if self.stage < BITS:
            half = self.length // 2
            self.total = self.part(half, self.length).astype(jnp.bfloat16)
            self.length = half
            self.got = exchange(self.total, self.way, self.stage, self.devices)
            if self.stage == BITS - 1:
                self.terms = [(self.part(0, half), 0)]


def final_kernel(channels, pitch, parts, *refs):
    out = refs[-1]
    at = 0
    for low, high, count in parts:
        terms = refs[at:at + count]
        at += count
        for tile in range(high - low):
            total = sum(
                term[tile * pitch:(tile + 1) * pitch, :].astype(jnp.float32) for term in terms
            )
            lane = (low + tile) * LANES
            out[0, :, lane:lane + LANES] = total[:channels].astype(jnp.bfloat16)


def final_sum(chains, like_shape, pitch):
    parts = [(chain.chunk[0], chain.chunk[1], len(chain.terms)) for chain in chains]
    flat = [term for chain in chains for term, base in chain.terms]
    return pl.pallas_call(
        functools.partial(final_kernel, like_shape[1], pitch, parts),
        out_shape=jax.ShapeDtypeStruct(like_shape, jnp.bfloat16),
        in_specs=[pl.BlockSpec(memory_space=pltpu.VMEM)] * len(flat),
        out_specs=pl.BlockSpec(memory_space=pltpu.VMEM),
        compiler_params=pltpu.CompilerParams(vmem_limit_bytes=24 * 1024 * 1024),
    )(*flat)


class Order:
    def __init__(self):
        self.last = ()

    def after(self, values):
        values, unused = lax.optimization_barrier((values, self.last))
        return values

    def before(self, values):
        self.last = values


def bit_remaps(remaps, devices):
    one, two = remaps
    pitch = round_up(one[-1][1], 8)
    tiles = one[-1][2] // LANES
    half, most, more = tiles // 2, tiles * 3 // 4, tiles * 5 // 6
    plans = (
        [(0, most, MIXED), (most, tiles, MIXED)],
        [(0, half, MIXED), (half, more, STRAIGHT), (more, tiles, STRAIGHT)],
    )
    ones, twos = [[Chain(chunk, devices, pitch) for chunk in chunks] for chunks in plans]
    order = Order()

    def step(*chains):
        gots = order.after([chain.got for chain in chains])
        for chain, got in zip(chains, gots):
            chain.got = got
            chain.send_next()
        order.before([chain.total for chain in chains])

    def summed(line, sums, got):
        got = order.after(got)
        for chain in line:
            chain.first(sums, got)
        order.before([chain.total for chain in line])

    def rested(line, sums, got):
        got = order.after(got)
        order.before(got)
        for chain in line:
            chain.rest(sums, got)

    def begun(chain):
        chain.total = order.after(chain.total)
        chain.second()

    def cores(send):
        return exchange(send, STRAIGHT, 0, devices)

    a, b = ones
    c, d, e = twos

    sums, send, send_on = products(one, plans[0], devices)
    on, rest = cores(send_on), cores(send)
    summed(ones, sums, on)
    a.second()
    b.second()
    rested(ones, sums, rest)
    made = products((order.after(two[0]),) + two[1:], plans[1], devices)
    order.before(made)
    sums, send, send_on = made
    on, rest = cores(send_on), cores(send)

    step(a)
    step(b)
    summed(twos, sums, on)
    c.second()
    begun(d)
    step(a)
    step(b)
    rested(twos, sums, rest)
    step(c)
    begun(e)
    step(d)
    step(c)
    step(e)
    step(d)
    step(e)
    step(b)
    step(a)
    step(c)
    step(d)
    step(e)
    return [final_sum(line, remap[-1], pitch) for line, remap in zip((ones, twos), remaps)]


def on_device(devices, *args):
    latlon, healpix = args[:2]
    remaps = [
        (latlon, args[2], args[3], args[4], args[5], healpix.shape),
        (healpix, args[6], args[7], args[8], args[9], latlon.shape),
    ]
    tiles = max(latlon.shape[2], healpix.shape[2]) // LANES
    size = devices * tiles * round_up(latlon.shape[1], 8) * LANES * 4
    if devices == 1 << BITS and size <= ACC_LIMIT:
        return tuple(bit_remaps(remaps, devices))
    return tuple(slot_remap(*remap) for remap in remaps)


def solution(mesh):
    in_specs = (
        P("groups", None, "curve"),
        P("groups", None, "curve"),
        P("curve", None, None),
        P("curve"),
        P("curve"),
        P("curve", None),
        P("curve", None, None),
        P("curve"),
        P("curve"),
        P("curve", None),
    )
    out_specs = (P("groups", None, "curve"), P("groups", None, "curve"))
    return jax.shard_map(
        functools.partial(on_device, mesh.shape["curve"]),
        mesh=mesh, in_specs=in_specs, out_specs=out_specs, check_vma=False,
    )
```

```python
import functools

import jax
import jax.numpy as jnp
from jax import lax
from jax.experimental import pallas as pl
from jax.experimental.pallas import tpu as pltpu
from jax.sharding import PartitionSpec as P

LANES = 128
ACC_LIMIT = 16 * 1024 * 1024


def round_up(value, unit):
    return -(-value // unit) * unit


def block_products(cotangent, weights, source):
    width = weights.shape[1]
    lead = cotangent.shape[0] * cotangent.shape[1]
    tiled = cotangent.reshape(lead, cotangent.shape[2] // width, width)
    picked = jnp.take(tiled, source, axis=1)
    products = jnp.einsum("kbi,bij->bkj", picked, weights, preferred_element_type=jnp.float32)
    return products.astype(jnp.bfloat16)


def pack_slots(products, target, count_row):
    blocks = products.shape[0]
    devices = count_row.shape[0]
    per_device = 2 * blocks // devices
    inclusive = jnp.cumsum(count_row)
    exclusive = inclusive - count_row
    positions = jnp.arange(blocks, dtype=jnp.int32)
    owner = jnp.sum((positions[:, None] >= inclusive[None, :]).astype(jnp.int32), axis=1)
    chosen = owner[:, None] == jnp.arange(devices, dtype=jnp.int32)[None, :]
    first = jnp.sum(jnp.where(chosen, exclusive[None, :], 0), axis=1)
    slot_index = owner * per_device + positions - first
    buffer = (
        jnp.zeros((devices * per_device,) + products.shape[1:], jnp.bfloat16)
        .at[slot_index]
        .set(products)
    )
    labels = jnp.full((devices * per_device,), -1, jnp.int32).at[slot_index].set(target)
    return (buffer, labels)


def sum_slots(received, labels, tiles_out, like_shape):
    selector = (labels[None, :] == jnp.arange(tiles_out, dtype=jnp.int32)[:, None]).astype(
        jnp.bfloat16
    )
    summed = jnp.einsum("ts,skc->ktc", selector, received, preferred_element_type=jnp.float32)
    return summed.reshape(like_shape[0], like_shape[1], -1).astype(jnp.bfloat16)


def slot_remap(cotangent, weights, source, target, counts, like_shape):
    products = block_products(cotangent, weights, source)
    buffer, labels = pack_slots(products, target, counts[0])
    arrived = lax.all_to_all(buffer, "curve", split_axis=0, concat_axis=0, tiled=True)
    arrived_labels = lax.all_to_all(labels, "curve", split_axis=0, concat_axis=0, tiled=True)
    return sum_slots(arrived, arrived_labels, like_shape[2] // weights.shape[1], like_shape)


STRAIGHT = ((0, 1, 2, 3), (0, 1, 2, 3))
MIXED = ((0, 2, 1, 3), (0, 1, 2, 3))
BITS = 4


def product_kernel(
    channels, pitch, chunks, step_blocks,
    source_hbm, target_hbm, counts_hbm, x_hbm, w_hbm, *rest,
):
    number = len(chunks)
    acc, send, send_on, xs, x_in, w, source, target, counts, places, sems = rest
    devices = counts.shape[1]
    steps = w.shape[0] // step_blocks
    me = lax.axis_index("curve")

    scalars = [
        pltpu.make_async_copy(source_hbm, source, sems.at[0]),
        pltpu.make_async_copy(target_hbm, target, sems.at[1]),
        pltpu.make_async_copy(counts_hbm, counts, sems.at[2]),
    ]
    x_copy = pltpu.make_async_copy(x_hbm, x_in, sems.at[3])

    def w_copy(step):
        at = pl.ds(step * step_blocks, step_blocks)
        return pltpu.make_async_copy(w_hbm.at[at], w.at[at], sems.at[4 + step])

    for copy in scalars + [x_copy]:
        copy.start()
    for step in range(steps):
        w_copy(step).start()

    @pl.loop(0, acc.shape[0] // pitch)
    def clear(index):
        acc[pl.ds(pl.multiple_of(index * pitch, pitch), pitch), :] = jnp.zeros((pitch, LANES), jnp.float32)

    for tile in range(xs.shape[0]):
        xs[tile] = jnp.zeros(xs.shape[1:], xs.dtype)

    for owner in range(devices):
        differ = jnp.bitwise_xor(me, owner)
        found = {}
        for chunk, (low, high, way) in enumerate(chunks):
            first, second, *others = way[owner % 2]
            key = (second, first, *others)
            if key not in found:
                place = jnp.int32(0)
                for bit in key:
                    place = place * 2 + jnp.bitwise_and(jnp.right_shift(differ, bit), 1)
                found[key] = place
            places[chunk, owner] = devices * low + found[key] * (high - low) - low

    x_copy.wait()
    for tile in range(xs.shape[0]):
        xs[tile, :channels, :] = x_in[0, :, tile * LANES:(tile + 1) * LANES]
    for copy in scalars:
        copy.wait()

    def some(step, carry):
        owner, end = carry
        w_copy(step).wait()
        rows = []
        for index in range(step_blocks):
            block = step * step_blocks + index
            passed = (block >= end).astype(jnp.int32)
            owner = jnp.minimum(owner + passed, devices - 1)
            end = end + passed * counts[0, owner]
            tile = target[block]
            place = places[0, owner]
            for chunk in range(1, number):
                place = jnp.where(tile >= chunks[chunk][0], places[chunk, owner], place)
            rows.append(pl.multiple_of((place + tile) * pitch, 8))
        for index, row in enumerate(rows):
            block = step * step_blocks + index
            product = jnp.dot(xs[source[block], :pitch, :], w[block], preferred_element_type=jnp.float32)
            acc[pl.ds(row, pitch), :] += product
        return owner, end

    lax.fori_loop(0, steps, some, (jnp.int32(0), counts[0, 0]))

    quarter = devices // 4
    for low, high, way in chunks:
        unit = (high - low) * pitch

        @pl.loop(0, quarter)
        def finish(index):
            at = pl.multiple_of(quarter * low * pitch + index * unit, 8)
            row = pl.multiple_of((devices * low + quarter * (high - low)) * pitch + index * unit, 8)
            send[pl.ds(at, unit), :] = acc[pl.ds(row, unit), :].astype(send.dtype)
            row = pl.multiple_of(row + 2 * quarter * unit, 8)
            send_on[pl.ds(at, unit), :] = acc[pl.ds(row, unit), :].astype(send.dtype)


def products(remap, chunks, devices):
    cotangent, weights, source, target, counts = remap[:5]
    channels = cotangent.shape[1]
    pitch = round_up(channels, 8)
    tiles_in = cotangent.shape[2] // LANES
    blocks = weights.shape[0]
    step_blocks = max(size for size in range(1, 17) if blocks % size == 0)
    rows = devices // 4 * chunks[-1][1] * pitch
    return pl.pallas_call(
        functools.partial(product_kernel, channels, pitch, chunks, step_blocks),
        out_shape=[
            jax.ShapeDtypeStruct((4 * rows, LANES), jnp.float32),
            jax.ShapeDtypeStruct((rows, LANES), jnp.bfloat16),
            jax.ShapeDtypeStruct((rows, LANES), jnp.bfloat16),
        ],
        in_specs=[pl.BlockSpec(memory_space=pltpu.HBM)] * 5,
        out_specs=[pl.BlockSpec(memory_space=pltpu.VMEM)] * 3,
        scratch_shapes=[
            pltpu.VMEM((tiles_in, round_up(pitch, 16), LANES), jnp.bfloat16),
            pltpu.VMEM(cotangent.shape, jnp.bfloat16),
            pltpu.VMEM(weights.shape, jnp.bfloat16),
            pltpu.SMEM(source.shape, jnp.int32),
            pltpu.SMEM(target.shape, jnp.int32),
            pltpu.SMEM(counts.shape, jnp.int32),
            pltpu.SMEM((len(chunks), devices), jnp.int32),
            pltpu.SemaphoreType.DMA((4 + blocks // step_blocks,)),
        ],
        compiler_params=pltpu.CompilerParams(vmem_limit_bytes=24 * 1024 * 1024),
        cost_estimate=pl.CostEstimate(
            flops=2 * blocks * channels * LANES * LANES,
            bytes_accessed=2 * weights.size + 20 * rows * LANES,
            transcendentals=0,
        ),
    )(*[pltpu.with_memory_space_constraint(value, pltpu.HBM) for value in (source, target, counts, cotangent, weights)])


def exchange(value, way, stage, devices):
    pairs = [(at, at ^ (1 << way[at % 2][stage])) for at in range(devices)]
    return lax.ppermute(value, "curve", pairs)


class Chain:
    def __init__(self, chunk, devices, pitch):
        self.chunk, self.devices = chunk, devices
        self.way = chunk[2]
        self.base = devices // 4 * chunk[0] * pitch
        self.length = devices // 4 * (chunk[1] - chunk[0]) * pitch

    def first(self, sums, got):
        self.terms = [(sums, 4 * self.base + 2 * self.length), (got, self.base)]
        self.total = self.part(0, self.length).astype(jnp.bfloat16)

    def part(self, low, high):
        return sum(term[base + low:base + high].astype(jnp.float32) for term, base in self.terms)

    def second(self):
        self.stage = 1
        self.got = exchange(self.total, self.way, self.stage, self.devices)

    def rest(self, sums, got):
        self.terms = [(sums, 4 * self.base), (got, self.base)]

    def send_next(self):
        self.terms = self.terms + [(self.got, 0)]
        self.stage += 1
        self.total = self.got
        if self.stage < BITS:
            half = self.length // 2
            self.total = self.part(half, self.length).astype(jnp.bfloat16)
            self.length = half
            self.got = exchange(self.total, self.way, self.stage, self.devices)
            if self.stage == BITS - 1:
                self.terms = [(self.part(0, half), 0)]


def final_kernel(channels, pitch, parts, *refs):
    out = refs[-1]
    at = 0
    for low, high, count in parts:
        terms = refs[at:at + count]
        at += count
        for tile in range(high - low):
            total = sum(
                term[tile * pitch:(tile + 1) * pitch, :].astype(jnp.float32) for term in terms
            )
            lane = (low + tile) * LANES
            out[0, :, lane:lane + LANES] = total[:channels].astype(jnp.bfloat16)


def final_sum(chains, like_shape, pitch):
    parts = [(chain.chunk[0], chain.chunk[1], len(chain.terms)) for chain in chains]
    flat = [term for chain in chains for term, base in chain.terms]
    return pl.pallas_call(
        functools.partial(final_kernel, like_shape[1], pitch, parts),
        out_shape=jax.ShapeDtypeStruct(like_shape, jnp.bfloat16),
        in_specs=[pl.BlockSpec(memory_space=pltpu.VMEM)] * len(flat),
        out_specs=pl.BlockSpec(memory_space=pltpu.VMEM),
        compiler_params=pltpu.CompilerParams(vmem_limit_bytes=24 * 1024 * 1024),
    )(*flat)


class Order:
    def __init__(self):
        self.last = ()

    def after(self, values):
        values, unused = lax.optimization_barrier((values, self.last))
        return values

    def before(self, values):
        self.last = values


def bit_remaps(remaps, devices):
    one, two = remaps
    pitch = round_up(one[-1][1], 8)
    tiles = one[-1][2] // LANES
    some, most, more = tiles * 5 // 12, tiles * 3 // 4, tiles * 5 // 6
    plans = (
        [(0, most, MIXED), (most, tiles, MIXED)],
        [(0, some, MIXED), (some, more, STRAIGHT), (more, tiles, STRAIGHT)],
    )
    ones, twos = [[Chain(chunk, devices, pitch) for chunk in chunks] for chunks in plans]
    order = Order()

    def step(*chains):
        gots = order.after([chain.got for chain in chains])
        for chain, got in zip(chains, gots):
            chain.got = got
            chain.send_next()
        order.before([chain.total for chain in chains])

    def summed(line, sums, got):
        got = order.after(got)
        for chain in line:
            chain.first(sums, got)
        order.before([chain.total for chain in line])

    def rested(line, sums, got):
        got = order.after(got)
        order.before(got)
        for chain in line:
            chain.rest(sums, got)

    def begun(chain):
        chain.total = order.after(chain.total)
        chain.second()

    def cores(send):
        return exchange(send, STRAIGHT, 0, devices)

    a, b = ones
    c, d, e = twos

    sums, send, send_on = products(one, plans[0], devices)
    on, rest = cores(send_on), cores(send)
    summed(ones, sums, on)
    a.second()
    b.second()
    rested(ones, sums, rest)
    made = products((order.after(two[0]),) + two[1:], plans[1], devices)
    order.before(made)
    sums, send, send_on = made
    on, rest = cores(send_on), cores(send)

    step(a)
    step(b)
    summed(twos, sums, on)
    c.second()
    begun(d)
    step(a)
    step(b)
    rested(twos, sums, rest)
    step(c)
    begun(e)
    step(d)
    step(c)
    step(e)
    step(d)
    step(e)
    step(b)
    step(a)
    step(c)
    step(d)
    step(e)
    return [final_sum(line, remap[-1], pitch) for line, remap in zip((ones, twos), remaps)]


def on_device(devices, *args):
    latlon, healpix = args[:2]
    remaps = [
        (latlon, args[2], args[3], args[4], args[5], healpix.shape),
        (healpix, args[6], args[7], args[8], args[9], latlon.shape),
    ]
    tiles = max(latlon.shape[2], healpix.shape[2]) // LANES
    size = devices * tiles * round_up(latlon.shape[1], 8) * LANES * 4
    if devices == 1 << BITS and size <= ACC_LIMIT:
        return tuple(bit_remaps(remaps, devices))
    return tuple(slot_remap(*remap) for remap in remaps)


def solution(mesh):
    in_specs = (
        P("groups", None, "curve"),
        P("groups", None, "curve"),
        P("curve", None, None),
        P("curve"),
        P("curve"),
        P("curve", None),
        P("curve", None, None),
        P("curve"),
        P("curve"),
        P("curve", None),
    )
    out_specs = (P("groups", None, "curve"), P("groups", None, "curve"))
    return jax.shard_map(
        functools.partial(on_device, mesh.shape["curve"]),
        mesh=mesh, in_specs=in_specs, out_specs=out_specs, check_vma=False,
    )
```

```python
import functools

import jax
import jax.numpy as jnp
from jax import lax
from jax.experimental import pallas as pl
from jax.experimental.pallas import tpu as pltpu
from jax.sharding import PartitionSpec as P

LANES = 128
ACC_LIMIT = 16 * 1024 * 1024


def round_up(value, unit):
    return -(-value // unit) * unit


def block_products(cotangent, weights, source):
    width = weights.shape[1]
    lead = cotangent.shape[0] * cotangent.shape[1]
    tiled = cotangent.reshape(lead, cotangent.shape[2] // width, width)
    picked = jnp.take(tiled, source, axis=1)
    products = jnp.einsum("kbi,bij->bkj", picked, weights, preferred_element_type=jnp.float32)
    return products.astype(jnp.bfloat16)


def pack_slots(products, target, count_row):
    blocks = products.shape[0]
    devices = count_row.shape[0]
    per_device = 2 * blocks // devices
    inclusive = jnp.cumsum(count_row)
    exclusive = inclusive - count_row
    positions = jnp.arange(blocks, dtype=jnp.int32)
    owner = jnp.sum((positions[:, None] >= inclusive[None, :]).astype(jnp.int32), axis=1)
    chosen = owner[:, None] == jnp.arange(devices, dtype=jnp.int32)[None, :]
    first = jnp.sum(jnp.where(chosen, exclusive[None, :], 0), axis=1)
    slot_index = owner * per_device + positions - first
    buffer = (
        jnp.zeros((devices * per_device,) + products.shape[1:], jnp.bfloat16)
        .at[slot_index]
        .set(products)
    )
    labels = jnp.full((devices * per_device,), -1, jnp.int32).at[slot_index].set(target)
    return (buffer, labels)


def sum_slots(received, labels, tiles_out, like_shape):
    selector = (labels[None, :] == jnp.arange(tiles_out, dtype=jnp.int32)[:, None]).astype(
        jnp.bfloat16
    )
    summed = jnp.einsum("ts,skc->ktc", selector, received, preferred_element_type=jnp.float32)
    return summed.reshape(like_shape[0], like_shape[1], -1).astype(jnp.bfloat16)


def slot_remap(cotangent, weights, source, target, counts, like_shape):
    products = block_products(cotangent, weights, source)
    buffer, labels = pack_slots(products, target, counts[0])
    arrived = lax.all_to_all(buffer, "curve", split_axis=0, concat_axis=0, tiled=True)
    arrived_labels = lax.all_to_all(labels, "curve", split_axis=0, concat_axis=0, tiled=True)
    return sum_slots(arrived, arrived_labels, like_shape[2] // weights.shape[1], like_shape)


STRAIGHT = ((0, 1, 2, 3), (0, 1, 2, 3))
MIXED = ((0, 2, 1, 3), (0, 1, 2, 3))
BITS = 4


def product_kernel(
    channels, pitch, chunks, step_blocks,
    source_hbm, target_hbm, counts_hbm, x_hbm, w_hbm, *rest,
):
    number = len(chunks)
    acc, send, send_on, xs, x_in, w, source, target, counts, places, sems = rest
    devices = counts.shape[1]
    steps = w.shape[0] // step_blocks
    me = lax.axis_index("curve")

    scalars = [
        pltpu.make_async_copy(source_hbm, source, sems.at[0]),
        pltpu.make_async_copy(target_hbm, target, sems.at[1]),
        pltpu.make_async_copy(counts_hbm, counts, sems.at[2]),
    ]
    x_copy = pltpu.make_async_copy(x_hbm, x_in, sems.at[3])

    def w_copy(step):
        at = pl.ds(step * step_blocks, step_blocks)
        return pltpu.make_async_copy(w_hbm.at[at], w.at[at], sems.at[4 + step])

    for copy in scalars + [x_copy]:
        copy.start()
    for step in range(steps):
        w_copy(step).start()

    @pl.loop(0, acc.shape[0] // pitch)
    def clear(index):
        acc[pl.ds(pl.multiple_of(index * pitch, pitch), pitch), :] = jnp.zeros((pitch, LANES), jnp.float32)

    for tile in range(xs.shape[0]):
        xs[tile] = jnp.zeros(xs.shape[1:], xs.dtype)

    for owner in range(devices):
        differ = jnp.bitwise_xor(me, owner)
        found = {}
        for chunk, (low, high, way) in enumerate(chunks):
            first, second, *others = way[owner % 2]
            key = (second, first, *others)
            if key not in found:
                place = jnp.int32(0)
                for bit in key:
                    place = place * 2 + jnp.bitwise_and(jnp.right_shift(differ, bit), 1)
                found[key] = place
            places[chunk, owner] = devices * low + found[key] * (high - low) - low

    x_copy.wait()
    for tile in range(xs.shape[0]):
        xs[tile, :channels, :] = x_in[0, :, tile * LANES:(tile + 1) * LANES]
    for copy in scalars:
        copy.wait()

    def some(step, carry):
        owner, end = carry
        w_copy(step).wait()
        rows = []
        for index in range(step_blocks):
            block = step * step_blocks + index
            passed = (block >= end).astype(jnp.int32)
            owner = jnp.minimum(owner + passed, devices - 1)
            end = end + passed * counts[0, owner]
            tile = target[block]
            place = places[0, owner]
            for chunk in range(1, number):
                place = jnp.where(tile >= chunks[chunk][0], places[chunk, owner], place)
            rows.append(pl.multiple_of((place + tile) * pitch, 8))
        for index, row in enumerate(rows):
            block = step * step_blocks + index
            product = jnp.dot(xs[source[block], :pitch, :], w[block], preferred_element_type=jnp.float32)
            acc[pl.ds(row, pitch), :] += product
        return owner, end

    lax.fori_loop(0, steps, some, (jnp.int32(0), counts[0, 0]))

    quarter = devices // 4
    for low, high, way in chunks:
        unit = (high - low) * pitch

        @pl.loop(0, quarter)
        def finish(index):
            at = pl.multiple_of(quarter * low * pitch + index * unit, 8)
            row = pl.multiple_of((devices * low + quarter * (high - low)) * pitch + index * unit, 8)
            send[pl.ds(at, unit), :] = acc[pl.ds(row, unit), :].astype(send.dtype)
            row = pl.multiple_of(row + 2 * quarter * unit, 8)
            send_on[pl.ds(at, unit), :] = acc[pl.ds(row, unit), :].astype(send.dtype)


def products(remap, chunks, devices):
    cotangent, weights, source, target, counts = remap[:5]
    channels = cotangent.shape[1]
    pitch = round_up(channels, 8)
    tiles_in = cotangent.shape[2] // LANES
    blocks = weights.shape[0]
    step_blocks = max(size for size in range(1, 17) if blocks % size == 0)
    rows = devices // 4 * chunks[-1][1] * pitch
    return pl.pallas_call(
        functools.partial(product_kernel, channels, pitch, chunks, step_blocks),
        out_shape=[
            jax.ShapeDtypeStruct((4 * rows, LANES), jnp.float32),
            jax.ShapeDtypeStruct((rows, LANES), jnp.bfloat16),
            jax.ShapeDtypeStruct((rows, LANES), jnp.bfloat16),
        ],
        in_specs=[pl.BlockSpec(memory_space=pltpu.HBM)] * 5,
        out_specs=[pl.BlockSpec(memory_space=pltpu.VMEM)] * 3,
        scratch_shapes=[
            pltpu.VMEM((tiles_in, round_up(pitch, 16), LANES), jnp.bfloat16),
            pltpu.VMEM(cotangent.shape, jnp.bfloat16),
            pltpu.VMEM(weights.shape, jnp.bfloat16),
            pltpu.SMEM(source.shape, jnp.int32),
            pltpu.SMEM(target.shape, jnp.int32),
            pltpu.SMEM(counts.shape, jnp.int32),
            pltpu.SMEM((len(chunks), devices), jnp.int32),
            pltpu.SemaphoreType.DMA((4 + blocks // step_blocks,)),
        ],
        compiler_params=pltpu.CompilerParams(vmem_limit_bytes=24 * 1024 * 1024),
        cost_estimate=pl.CostEstimate(
            flops=2 * blocks * channels * LANES * LANES,
            bytes_accessed=2 * weights.size + 20 * rows * LANES,
            transcendentals=0,
        ),
    )(*[pltpu.with_memory_space_constraint(value, pltpu.HBM) for value in (source, target, counts, cotangent, weights)])


def exchange(value, way, stage, devices):
    pairs = [(at, at ^ (1 << way[at % 2][stage])) for at in range(devices)]
    return lax.ppermute(value, "curve", pairs)


class Chain:
    def __init__(self, chunk, devices, pitch):
        self.chunk, self.devices = chunk, devices
        self.way = chunk[2]
        self.base = devices // 4 * chunk[0] * pitch
        self.length = devices // 4 * (chunk[1] - chunk[0]) * pitch

    def first(self, sums, got):
        self.terms = [(sums, 4 * self.base + 2 * self.length), (got, self.base)]
        self.total = self.part(0, self.length).astype(jnp.bfloat16)

    def part(self, low, high):
        return sum(term[base + low:base + high].astype(jnp.float32) for term, base in self.terms)

    def second(self):
        self.stage = 1
        self.got = exchange(self.total, self.way, self.stage, self.devices)

    def rest(self, sums, got):
        self.terms = [(sums, 4 * self.base), (got, self.base)]

    def send_next(self):
        self.terms = self.terms + [(self.got, 0)]
        self.stage += 1
        self.total = self.got
        if self.stage < BITS:
            half = self.length // 2
            self.total = self.part(half, self.length).astype(jnp.bfloat16)
            self.length = half
            self.got = exchange(self.total, self.way, self.stage, self.devices)
            if self.stage == BITS - 1:
                self.terms = [(self.part(0, half), 0)]


def final_kernel(channels, pitch, parts, *refs):
    out = refs[-1]
    at = 0
    for low, high, count in parts:
        terms = refs[at:at + count]
        at += count
        for tile in range(high - low):
            total = sum(
                term[tile * pitch:(tile + 1) * pitch, :].astype(jnp.float32) for term in terms
            )
            lane = (low + tile) * LANES
            out[0, :, lane:lane + LANES] = total[:channels].astype(jnp.bfloat16)


def final_sum(chains, like_shape, pitch):
    parts = [(chain.chunk[0], chain.chunk[1], len(chain.terms)) for chain in chains]
    flat = [term for chain in chains for term, base in chain.terms]
    return pl.pallas_call(
        functools.partial(final_kernel, like_shape[1], pitch, parts),
        out_shape=jax.ShapeDtypeStruct(like_shape, jnp.bfloat16),
        in_specs=[pl.BlockSpec(memory_space=pltpu.VMEM)] * len(flat),
        out_specs=pl.BlockSpec(memory_space=pltpu.VMEM),
        compiler_params=pltpu.CompilerParams(vmem_limit_bytes=24 * 1024 * 1024),
    )(*flat)


class Order:
    def __init__(self):
        self.last = ()

    def after(self, values):
        values, unused = lax.optimization_barrier((values, self.last))
        return values

    def before(self, values):
        self.last = values


def bit_remaps(remaps, devices):
    one, two = remaps
    pitch = round_up(one[-1][1], 8)
    tiles = one[-1][2] // LANES
    half, most, more = tiles // 2, tiles * 3 // 4, tiles * 5 // 6
    plans = (
        [(0, more, MIXED), (more, tiles, MIXED)],
        [(0, half, MIXED), (half, more, STRAIGHT), (more, tiles, STRAIGHT)],
    )
    ones, twos = [[Chain(chunk, devices, pitch) for chunk in chunks] for chunks in plans]
    order = Order()

    def step(*chains):
        gots = order.after([chain.got for chain in chains])
        for chain, got in zip(chains, gots):
            chain.got = got
            chain.send_next()
        order.before([chain.total for chain in chains])

    def summed(line, sums, got):
        got = order.after(got)
        for chain in line:
            chain.first(sums, got)
        order.before([chain.total for chain in line])

    def rested(line, sums, got):
        got = order.after(got)
        order.before(got)
        for chain in line:
            chain.rest(sums, got)

    def begun(chain):
        chain.total = order.after(chain.total)
        chain.second()

    def cores(send):
        return exchange(send, STRAIGHT, 0, devices)

    a, b = ones
    c, d, e = twos

    sums, send, send_on = products(one, plans[0], devices)
    on, rest = cores(send_on), cores(send)
    summed(ones, sums, on)
    a.second()
    b.second()
    rested(ones, sums, rest)
    made = products((order.after(two[0]),) + two[1:], plans[1], devices)
    order.before(made)
    sums, send, send_on = made
    on, rest = cores(send_on), cores(send)

    step(a)
    step(b)
    summed(twos, sums, on)
    c.second()
    begun(d)
    step(a)
    step(b)
    rested(twos, sums, rest)
    step(c)
    begun(e)
    step(d)
    step(c)
    step(e)
    step(d)
    step(e)
    step(b)
    step(a)
    step(c)
    step(d)
    step(e)
    return [final_sum(line, remap[-1], pitch) for line, remap in zip((ones, twos), remaps)]


def on_device(devices, *args):
    latlon, healpix = args[:2]
    remaps = [
        (latlon, args[2], args[3], args[4], args[5], healpix.shape),
        (healpix, args[6], args[7], args[8], args[9], latlon.shape),
    ]
    tiles = max(latlon.shape[2], healpix.shape[2]) // LANES
    size = devices * tiles * round_up(latlon.shape[1], 8) * LANES * 4
    if devices == 1 << BITS and size <= ACC_LIMIT:
        return tuple(bit_remaps(remaps, devices))
    return tuple(slot_remap(*remap) for remap in remaps)


def solution(mesh):
    in_specs = (
        P("groups", None, "curve"),
        P("groups", None, "curve"),
        P("curve", None, None),
        P("curve"),
        P("curve"),
        P("curve", None),
        P("curve", None, None),
        P("curve"),
        P("curve"),
        P("curve", None),
    )
    out_specs = (P("groups", None, "curve"), P("groups", None, "curve"))
    return jax.shard_map(
        functools.partial(on_device, mesh.shape["curve"]),
        mesh=mesh, in_specs=in_specs, out_specs=out_specs, check_vma=False,
    )
```

```python
import functools

import jax
import jax.numpy as jnp
from jax import lax
from jax.experimental import pallas as pl
from jax.experimental.pallas import tpu as pltpu
from jax.sharding import PartitionSpec as P

LANES = 128
ACC_LIMIT = 16 * 1024 * 1024


def round_up(value, unit):
    return -(-value // unit) * unit


def block_products(cotangent, weights, source):
    width = weights.shape[1]
    lead = cotangent.shape[0] * cotangent.shape[1]
    tiled = cotangent.reshape(lead, cotangent.shape[2] // width, width)
    picked = jnp.take(tiled, source, axis=1)
    products = jnp.einsum("kbi,bij->bkj", picked, weights, preferred_element_type=jnp.float32)
    return products.astype(jnp.bfloat16)


def pack_slots(products, target, count_row):
    blocks = products.shape[0]
    devices = count_row.shape[0]
    per_device = 2 * blocks // devices
    inclusive = jnp.cumsum(count_row)
    exclusive = inclusive - count_row
    positions = jnp.arange(blocks, dtype=jnp.int32)
    owner = jnp.sum((positions[:, None] >= inclusive[None, :]).astype(jnp.int32), axis=1)
    chosen = owner[:, None] == jnp.arange(devices, dtype=jnp.int32)[None, :]
    first = jnp.sum(jnp.where(chosen, exclusive[None, :], 0), axis=1)
    slot_index = owner * per_device + positions - first
    buffer = (
        jnp.zeros((devices * per_device,) + products.shape[1:], jnp.bfloat16)
        .at[slot_index]
        .set(products)
    )
    labels = jnp.full((devices * per_device,), -1, jnp.int32).at[slot_index].set(target)
    return (buffer, labels)


def sum_slots(received, labels, tiles_out, like_shape):
    selector = (labels[None, :] == jnp.arange(tiles_out, dtype=jnp.int32)[:, None]).astype(
        jnp.bfloat16
    )
    summed = jnp.einsum("ts,skc->ktc", selector, received, preferred_element_type=jnp.float32)
    return summed.reshape(like_shape[0], like_shape[1], -1).astype(jnp.bfloat16)


def slot_remap(cotangent, weights, source, target, counts, like_shape):
    products = block_products(cotangent, weights, source)
    buffer, labels = pack_slots(products, target, counts[0])
    arrived = lax.all_to_all(buffer, "curve", split_axis=0, concat_axis=0, tiled=True)
    arrived_labels = lax.all_to_all(labels, "curve", split_axis=0, concat_axis=0, tiled=True)
    return sum_slots(arrived, arrived_labels, like_shape[2] // weights.shape[1], like_shape)


STRAIGHT = ((0, 1, 2, 3), (0, 1, 2, 3))
MIXED = ((0, 1, 2, 3), (0, 2, 1, 3))
BITS = 4


def product_kernel(
    channels, pitch, chunks, step_blocks,
    source_hbm, target_hbm, counts_hbm, x_hbm, w_hbm, *rest,
):
    number = len(chunks)
    acc, send, send_on, xs, x_in, w, source, target, counts, places, sems = rest
    devices = counts.shape[1]
    steps = w.shape[0] // step_blocks
    me = lax.axis_index("curve")

    scalars = [
        pltpu.make_async_copy(source_hbm, source, sems.at[0]),
        pltpu.make_async_copy(target_hbm, target, sems.at[1]),
        pltpu.make_async_copy(counts_hbm, counts, sems.at[2]),
    ]
    x_copy = pltpu.make_async_copy(x_hbm, x_in, sems.at[3])

    def w_copy(step):
        at = pl.ds(step * step_blocks, step_blocks)
        return pltpu.make_async_copy(w_hbm.at[at], w.at[at], sems.at[4 + step])

    for copy in scalars + [x_copy]:
        copy.start()
    for step in range(steps):
        w_copy(step).start()

    @pl.loop(0, acc.shape[0] // pitch)
    def clear(index):
        acc[pl.ds(pl.multiple_of(index * pitch, pitch), pitch), :] = jnp.zeros((pitch, LANES), jnp.float32)

    for tile in range(xs.shape[0]):
        xs[tile] = jnp.zeros(xs.shape[1:], xs.dtype)

    for owner in range(devices):
        differ = jnp.bitwise_xor(me, owner)
        found = {}
        for chunk, (low, high, way) in enumerate(chunks):
            first, second, *others = way[owner % 2]
            key = (second, first, *others)
            if key not in found:
                place = jnp.int32(0)
                for bit in key:
                    place = place * 2 + jnp.bitwise_and(jnp.right_shift(differ, bit), 1)
                found[key] = place
            places[chunk, owner] = devices * low + found[key] * (high - low) - low

    x_copy.wait()
    for tile in range(xs.shape[0]):
        xs[tile, :channels, :] = x_in[0, :, tile * LANES:(tile + 1) * LANES]
    for copy in scalars:
        copy.wait()

    def some(step, carry):
        owner, end = carry
        w_copy(step).wait()
        rows = []
        for index in range(step_blocks):
            block = step * step_blocks + index
            passed = (block >= end).astype(jnp.int32)
            owner = jnp.minimum(owner + passed, devices - 1)
            end = end + passed * counts[0, owner]
            tile = target[block]
            place = places[0, owner]
            for chunk in range(1, number):
                place = jnp.where(tile >= chunks[chunk][0], places[chunk, owner], place)
            rows.append(pl.multiple_of((place + tile) * pitch, 8))
        for index, row in enumerate(rows):
            block = step * step_blocks + index
            product = jnp.dot(xs[source[block], :pitch, :], w[block], preferred_element_type=jnp.float32)
            acc[pl.ds(row, pitch), :] += product
        return owner, end

    lax.fori_loop(0, steps, some, (jnp.int32(0), counts[0, 0]))

    quarter = devices // 4
    for low, high, way in chunks:
        unit = (high - low) * pitch

        @pl.loop(0, quarter)
        def finish(index):
            at = pl.multiple_of(quarter * low * pitch + index * unit, 8)
            row = pl.multiple_of((devices * low + quarter * (high - low)) * pitch + index * unit, 8)
            send[pl.ds(at, unit), :] = acc[pl.ds(row, unit), :].astype(send.dtype)
            row = pl.multiple_of(row + 2 * quarter * unit, 8)
            send_on[pl.ds(at, unit), :] = acc[pl.ds(row, unit), :].astype(send.dtype)


def products(remap, chunks, devices):
    cotangent, weights, source, target, counts = remap[:5]
    channels = cotangent.shape[1]
    pitch = round_up(channels, 8)
    tiles_in = cotangent.shape[2] // LANES
    blocks = weights.shape[0]
    step_blocks = max(size for size in range(1, 17) if blocks % size == 0)
    rows = devices // 4 * chunks[-1][1] * pitch
    return pl.pallas_call(
        functools.partial(product_kernel, channels, pitch, chunks, step_blocks),
        out_shape=[
            jax.ShapeDtypeStruct((4 * rows, LANES), jnp.float32),
            jax.ShapeDtypeStruct((rows, LANES), jnp.bfloat16),
            jax.ShapeDtypeStruct((rows, LANES), jnp.bfloat16),
        ],
        in_specs=[pl.BlockSpec(memory_space=pltpu.HBM)] * 5,
        out_specs=[pl.BlockSpec(memory_space=pltpu.VMEM)] * 3,
        scratch_shapes=[
            pltpu.VMEM((tiles_in, round_up(pitch, 16), LANES), jnp.bfloat16),
            pltpu.VMEM(cotangent.shape, jnp.bfloat16),
            pltpu.VMEM(weights.shape, jnp.bfloat16),
            pltpu.SMEM(source.shape, jnp.int32),
            pltpu.SMEM(target.shape, jnp.int32),
            pltpu.SMEM(counts.shape, jnp.int32),
            pltpu.SMEM((len(chunks), devices), jnp.int32),
            pltpu.SemaphoreType.DMA((4 + blocks // step_blocks,)),
        ],
        compiler_params=pltpu.CompilerParams(vmem_limit_bytes=24 * 1024 * 1024),
        cost_estimate=pl.CostEstimate(
            flops=2 * blocks * channels * LANES * LANES,
            bytes_accessed=2 * weights.size + 20 * rows * LANES,
            transcendentals=0,
        ),
    )(*[pltpu.with_memory_space_constraint(value, pltpu.HBM) for value in (source, target, counts, cotangent, weights)])


def exchange(value, way, stage, devices):
    pairs = [(at, at ^ (1 << way[at % 2][stage])) for at in range(devices)]
    return lax.ppermute(value, "curve", pairs)


class Chain:
    def __init__(self, chunk, devices, pitch):
        self.chunk, self.devices = chunk, devices
        self.way = chunk[2]
        self.base = devices // 4 * chunk[0] * pitch
        self.length = devices // 4 * (chunk[1] - chunk[0]) * pitch

    def first(self, sums, got):
        self.terms = [(sums, 4 * self.base + 2 * self.length), (got, self.base)]
        self.total = self.part(0, self.length).astype(jnp.bfloat16)

    def part(self, low, high):
        return sum(term[base + low:base + high].astype(jnp.float32) for term, base in self.terms)

    def second(self):
        self.stage = 1
        self.got = exchange(self.total, self.way, self.stage, self.devices)

    def rest(self, sums, got):
        self.terms = [(sums, 4 * self.base), (got, self.base)]

    def send_next(self):
        self.terms = self.terms + [(self.got, 0)]
        self.stage += 1
        self.total = self.got
        if self.stage < BITS:
            half = self.length // 2
            self.total = self.part(half, self.length).astype(jnp.bfloat16)
            self.length = half
            self.got = exchange(self.total, self.way, self.stage, self.devices)
            if self.stage == BITS - 1:
                self.terms = [(self.part(0, half), 0)]


def final_kernel(channels, pitch, parts, *refs):
    out = refs[-1]
    at = 0
    for low, high, count in parts:
        terms = refs[at:at + count]
        at += count
        for tile in range(high - low):
            total = sum(
                term[tile * pitch:(tile + 1) * pitch, :].astype(jnp.float32) for term in terms
            )
            lane = (low + tile) * LANES
            out[0, :, lane:lane + LANES] = total[:channels].astype(jnp.bfloat16)


def final_sum(chains, like_shape, pitch):
    parts = [(chain.chunk[0], chain.chunk[1], len(chain.terms)) for chain in chains]
    flat = [term for chain in chains for term, base in chain.terms]
    return pl.pallas_call(
        functools.partial(final_kernel, like_shape[1], pitch, parts),
        out_shape=jax.ShapeDtypeStruct(like_shape, jnp.bfloat16),
        in_specs=[pl.BlockSpec(memory_space=pltpu.VMEM)] * len(flat),
        out_specs=pl.BlockSpec(memory_space=pltpu.VMEM),
        compiler_params=pltpu.CompilerParams(vmem_limit_bytes=24 * 1024 * 1024),
    )(*flat)


class Order:
    def __init__(self):
        self.last = ()

    def after(self, values):
        values, unused = lax.optimization_barrier((values, self.last))
        return values

    def before(self, values):
        self.last = values


def bit_remaps(remaps, devices):
    one, two = remaps
    pitch = round_up(one[-1][1], 8)
    tiles = one[-1][2] // LANES
    half, most, more = tiles // 2, tiles * 3 // 4, tiles * 5 // 6
    plans = (
        [(0, most, MIXED), (most, tiles, MIXED)],
        [(0, half, MIXED), (half, more, STRAIGHT), (more, tiles, STRAIGHT)],
    )
    ones, twos = [[Chain(chunk, devices, pitch) for chunk in chunks] for chunks in plans]
    order = Order()

    def step(*chains):
        gots = order.after([chain.got for chain in chains])
        for chain, got in zip(chains, gots):
            chain.got = got
            chain.send_next()
        order.before([chain.total for chain in chains])

    def summed(line, sums, got):
        got = order.after(got)
        for chain in line:
            chain.first(sums, got)
        order.before([chain.total for chain in line])

    def rested(line, sums, got):
        got = order.after(got)
        order.before(got)
        for chain in line:
            chain.rest(sums, got)

    def begun(chain):
        chain.total = order.after(chain.total)
        chain.second()

    def cores(send):
        return exchange(send, STRAIGHT, 0, devices)

    a, b = ones
    c, d, e = twos

    sums, send, send_on = products(one, plans[0], devices)
    on, rest = cores(send_on), cores(send)
    summed(ones, sums, on)
    a.second()
    b.second()
    rested(ones, sums, rest)
    made = products((order.after(two[0]),) + two[1:], plans[1], devices)
    order.before(made)
    sums, send, send_on = made
    on, rest = cores(send_on), cores(send)

    step(a)
    step(b)
    summed(twos, sums, on)
    c.second()
    begun(d)
    step(a)
    step(b)
    rested(twos, sums, rest)
    step(c)
    begun(e)
    step(d)
    step(c)
    step(e)
    step(d)
    step(e)
    step(b)
    step(a)
    step(c)
    step(d)
    step(e)
    return [final_sum(line, remap[-1], pitch) for line, remap in zip((ones, twos), remaps)]


def on_device(devices, *args):
    latlon, healpix = args[:2]
    remaps = [
        (latlon, args[2], args[3], args[4], args[5], healpix.shape),
        (healpix, args[6], args[7], args[8], args[9], latlon.shape),
    ]
    tiles = max(latlon.shape[2], healpix.shape[2]) // LANES
    size = devices * tiles * round_up(latlon.shape[1], 8) * LANES * 4
    if devices == 1 << BITS and size <= ACC_LIMIT:
        return tuple(bit_remaps(remaps, devices))
    return tuple(slot_remap(*remap) for remap in remaps)


def solution(mesh):
    in_specs = (
        P("groups", None, "curve"),
        P("groups", None, "curve"),
        P("curve", None, None),
        P("curve"),
        P("curve"),
        P("curve", None),
        P("curve", None, None),
        P("curve"),
        P("curve"),
        P("curve", None),
    )
    out_specs = (P("groups", None, "curve"), P("groups", None, "curve"))
    return jax.shard_map(
        functools.partial(on_device, mesh.shape["curve"]),
        mesh=mesh, in_specs=in_specs, out_specs=out_specs, check_vma=False,
    )
```
